32 devices in a mesh: gx: 4 (over y, x), gy: 2 (over core), gz: 4 (over z).
Axes of the slice: x: 2, y: 2, z: 4, core: 2. Of those that a mesh axis runs over, the one named last changes fastest.
Arguments:
- right_side: float32 [128, 32, 512], P('gx', 'gy', 'gz'), may hold values from -24 to 24
- conductivity: float32 [128, 32, 512], P('gx', 'gy', 'gz'), may hold values from 0.2 to 5
Outputs:
- solution: float32 [128, 32, 512], P('gx', 'gy', 'gz')
- final_residual: float32 [128, 32, 512], P('gx', 'gy', 'gz')
The draws below stay inside these ranges and needn't reach their ends.
All inputs are finite; a program needn't handle non-finite values.
Results may differ from the reference program's by a relative error of at most 0.0003.
Values sent between devices are 32-bit elements; how exact they have to be, the bound alone decides.
No kernel may reach another device: no remote copies, remote signals or barrier semaphores. Data moves between devices by JAX's collectives and lax.ppermute only.
A program may use at most 64 MiB of HBM per device.

```python
import math
import jax
import jax.numpy as jnp
from jax import lax

LEVELS = 4
STEPS = 3
COARSE_STEPS = 8
NX = 128
NY = 32
NZ = 512


def draw_right_side(key, part):
    noise_part = 4.0 * jax.random.normal(key, (NX, NY, NZ), jnp.float32)
    noise_part = jnp.clip(noise_part, -24.0, 24.0)
    return noise_part


def shard_levels(rng, shape, cuts, smallest, high):
    gain, own = 1.0, jax.random.fold_in(rng, 6)
    for dim, blocks in cuts:
        heights = jnp.exp(jax.random.uniform(jax.random.fold_in(own, dim), (blocks,), jnp.float32, smallest / len(cuts), high / len(cuts)))
        gain = gain * jnp.repeat(heights, shape[dim] // blocks).reshape([-1 if axis == dim else 1 for axis in range(len(shape))])
    return gain


def setup_inputs(seed: int = 0) -> dict:
    streams_of = jax.random.split(jax.random.key(seed), 3)
    right_side = draw_right_side(jax.random.fold_in(streams_of[2], 71), 0)
    conductivity = jnp.clip(jnp.exp(math.log(5.0) - 3.218876 * jax.random.uniform(streams_of[1], (NX, NY, NZ), jnp.float32) ** shard_levels(streams_of[1], (NX, NY, NZ), ((0, 4), (1, 2), (2, 4)), -0.2, 0.2)), 0.2, 5.0)
    return dict(right_side=right_side, conductivity=conductivity)


LOWER_EDGE = 0.3
UPPER_EDGE = 2.0


def chebyshev_factors(sweeps):
    centre_value = 0.5 * (UPPER_EDGE + LOWER_EDGE)
    half_width = 0.5 * (UPPER_EDGE - LOWER_EDGE)
    ratio_value = centre_value / half_width
    damping = 1.0 / ratio_value
    factors = [(0.0, 1.0 / centre_value)]
    for sweep_index in range(1, sweeps):
        damping_next = 1.0 / (2.0 * ratio_value - damping)
        factors.append((damping_next * damping, 2.0 * damping_next / half_width))
        damping = damping_next
    return factors


def neighbours(padded):
    return (padded[2:, 1:-1, 1:-1], padded[:-2, 1:-1, 1:-1], padded[1:-1, 2:, 1:-1],
            padded[1:-1, :-2, 1:-1], padded[1:-1, 1:-1, 2:], padded[1:-1, 1:-1, :-2])


def apply_operator(field_padded, coeff_padded, factor):
    centre_field = field_padded[1:-1, 1:-1, 1:-1]
    centre_coeff = coeff_padded[1:-1, 1:-1, 1:-1]
    summed = jnp.zeros(centre_field.shape, jnp.float32)
    for field_near, coeff_near in zip(neighbours(field_padded), neighbours(coeff_padded)):
        summed = summed + 0.5 * (centre_coeff + coeff_near) * (centre_field - field_near)
    return factor * summed


def diagonal_of(coeff_padded, factor):
    centre_coeff = coeff_padded[1:-1, 1:-1, 1:-1]
    summed = jnp.zeros(centre_coeff.shape, jnp.float32)
    for coeff_near in neighbours(coeff_padded):
        summed = summed + 0.5 * (centre_coeff + coeff_near)
    return factor * summed


def restrict_field(field):
    summed = field[0::2] + field[1::2]
    summed = summed[:, 0::2] + summed[:, 1::2]
    summed = summed[:, :, 0::2] + summed[:, :, 1::2]
    return 0.125 * summed


def prolong_field(padded):
    result = padded
    for axis_index in range(3):
        length = result.shape[axis_index] - 2
        middle = lax.slice_in_dim(result, 1, length + 1, axis=axis_index)
        preceding = lax.slice_in_dim(result, 0, length, axis=axis_index)
        following = lax.slice_in_dim(result, 2, length + 2, axis=axis_index)
        even_cells = 0.75 * middle + 0.25 * preceding
        odd_cells = 0.75 * middle + 0.25 * following
        joined = jnp.stack((even_cells, odd_cells), axis=axis_index + 1)
        new_shape = list(middle.shape)
        new_shape[axis_index] = 2 * length
        result = joined.reshape(new_shape)
    return result


def pad_zero(field):
    return jnp.pad(field, 1)


def smooth_field(source, initial, coeff_padded, factor, sweeps, want_residual, padder):
    diagonal = diagonal_of(coeff_padded, factor)
    if initial is None:
        residual = source
    else:
        residual = source - apply_operator(padder(initial), coeff_padded, factor)
    factors = chebyshev_factors(sweeps)
    direction = None
    solution = None
    for sweep_index in range(sweeps):
        keep_factor, push_factor = factors[sweep_index]
        if sweep_index > 0:
            residual = residual - apply_operator(padder(direction), coeff_padded, factor)
            direction = keep_factor * direction + push_factor * (residual / diagonal)
        else:
            direction = push_factor * (residual / diagonal)
        if solution is None and initial is None:
            solution = direction
        elif solution is None:
            solution = initial + direction
        else:
            solution = solution + direction
    if want_residual:
        residual = residual - apply_operator(padder(direction), coeff_padded, factor)
    return solution, residual


def reference(right_side, conductivity):
    conducts = [conductivity]
    for level_index in range(LEVELS):
        conducts.append(restrict_field(conducts[level_index]))
    padded_coeffs = [pad_zero(entry) for entry in conducts]
    sources = [right_side]
    presmoothed = []
    for level_index in range(LEVELS):
        factor = 0.25 ** level_index
        solution, residual = smooth_field(sources[level_index], None, padded_coeffs[level_index], factor, STEPS, True, pad_zero)
        presmoothed.append(solution)
        sources.append(restrict_field(residual))
    correction, unused = smooth_field(sources[LEVELS], None, padded_coeffs[LEVELS], 0.25 ** LEVELS, COARSE_STEPS, False, pad_zero)
    residual = sources[0]
    for level_index in reversed(range(LEVELS)):
        initial = presmoothed[level_index] + prolong_field(pad_zero(correction))
        correction, residual = smooth_field(sources[level_index], initial, padded_coeffs[level_index], 0.25 ** level_index, STEPS, level_index == 0, pad_zero)
    return correction, residual
```

```python
import functools
import jax
import jax.numpy as jnp
from jax import lax
from jax.experimental import pallas as pl
from jax.experimental.pallas import tpu as pltpu
from jax.sharding import PartitionSpec as P

LEVELS = 4
STEPS = 3
COARSE_STEPS = 8
LOWER_EDGE = 0.3
UPPER_EDGE = 2.0

LANES = 128
HALF = 64
REACH_X = 12
REACH_XB = 9
REACH_Z = 20
WIN0 = 4
WIN1 = REACH_X // 2
SLOTS = LANES // REACH_Z
AXES = ("gx", "gy", "gz")


def chebyshev_factors(sweeps):
    centre_value = 0.5 * (UPPER_EDGE + LOWER_EDGE)
    half_width = 0.5 * (UPPER_EDGE - LOWER_EDGE)
    ratio_value = centre_value / half_width
    damping = 1.0 / ratio_value
    factors = [(0.0, 1.0 / centre_value)]
    for _ in range(1, sweeps):
        damping_next = 1.0 / (2.0 * ratio_value - damping)
        factors.append((damping_next * damping, 2.0 * damping_next / half_width))
        damping = damping_next
    return factors


FACTORS = chebyshev_factors(STEPS)
COARSE_FACTORS = chebyshev_factors(COARSE_STEPS)


def chunks(count, body, size, first=1):
    if count == size:
        body(first)
    else:
        def step(i, carry):
            body(first + i * size)
            return carry
        lax.fori_loop(0, count // size, step, 0)


def rows_of(shape):
    return lax.broadcasted_iota(jnp.int32, shape, len(shape) - 2)


def lanes_of(shape):
    return lax.broadcasted_iota(jnp.int32, shape, len(shape) - 1)


class Grid:
    def __init__(self, x, y, z, sy, sz, whole_z, size):
        self.x, self.y, self.z, self.sy, self.sz = x, y, z, sy, sz
        self.whole_z, self.size = whole_z, size

    def up_y(self, v):
        return pltpu.roll(v, self.y - self.sy, v.ndim - 2)

    def down_y(self, v):
        return pltpu.roll(v, self.sy, v.ndim - 2)

    def up_z(self, v):
        return pltpu.roll(v, self.z - self.sz, v.ndim - 1)

    def down_z(self, v):
        return pltpu.roll(v, self.sz, v.ndim - 1)

    def setup(self, k_ref, cx, cy, cz, iv, ds, scale, after=None):
        cx[0] = 0.5 * (k_ref[0] + k_ref[1])

        def body(at):
            here = pl.ds(at, self.size)
            k = k_ref[here]
            row, lane = rows_of(k.shape), lanes_of(k.shape)
            k_next = k_ref[pl.ds(at + 1, self.size)]
            k_prev = k_ref[pl.ds(at - 1, self.size)]
            not_last = row < self.y - self.sy
            k_up = jnp.where(not_last, self.up_y(k), 0.0)
            k_down = jnp.where(row >= self.sy, self.down_y(k), 0.0)
            z_up, z_down = self.up_z(k), self.down_z(k)
            if self.whole_z:
                inner = lane < self.z - self.sz
                z_up = jnp.where(inner, z_up, 0.0)
                z_down = jnp.where(lane >= self.sz, z_down, 0.0)
            total = 3.0 * k + 0.5 * ((k_next + k_prev) + (k_up + k_down) + (z_up + z_down))
            inverse = jnp.where(k > 0.0, 1.0 / total, 0.0)
            cx[here] = 0.5 * (k + k_next)
            cy[here] = jnp.where(not_last, 0.5 * (k + k_up), 0.0)
            across = 0.5 * (k + z_up)
            cz[here] = jnp.where(inner, across, 0.0) if self.whole_z else across
            iv[here] = inverse
            if ds is not None:
                ds[here] = scale * total
            if after is not None:
                after(at, here, inverse)

        chunks(self.x, body, self.size)

    def step(self, coeffs, src, g_in, keep, push, out, first=1, count=None):
        cx, cy, cz, iv = coeffs

        def body(at):
            here, before = pl.ds(at, self.size), pl.ds(at - 1, self.size)
            v = src[here]
            y_coeff, z_coeff = cy[here], cz[here]
            near = cx[here] * src[pl.ds(at + 1, self.size)] + cx[before] * src[before]
            near = near + (y_coeff * self.up_y(v) + self.down_y(y_coeff * v))
            near = near + (z_coeff * self.up_z(v) + self.down_z(z_coeff * v))
            g = g_in[here] - v + iv[here] * near
            out(here, v, g, None if push is None else (keep * v + push * g if keep else push * g))

        chunks(count or self.x, body, self.size, first)


def pair_z(v, shift, lanes):
    even = (lanes_of(v.shape) // shift) % 2 == 0
    return v + jnp.where(even, pltpu.roll(v, lanes - shift, v.ndim - 1), pltpu.roll(v, shift, v.ndim - 1))


def pair_y(v, shift, rows):
    even = (rows_of(v.shape) // shift) % 2 == 0
    return v + jnp.where(even, pltpu.roll(v, rows - shift, v.ndim - 2), pltpu.roll(v, shift, v.ndim - 2))


def spread_z(v, shift, lanes, whole):
    lane = lanes_of(v.shape)
    even = (lane // shift) % 2 == 0
    low, high = pltpu.roll(v, shift, v.ndim - 1), pltpu.roll(v, lanes - shift, v.ndim - 1)
    if whole:
        low = jnp.where(lane >= shift, low, 0.0)
        high = jnp.where(lane < lanes - shift, high, 0.0)
    return 0.75 * v + 0.25 * jnp.where(even, low, high)


def spread_y(v, shift, rows):
    row = rows_of(v.shape)
    even = (row // shift) % 2 == 0
    low = jnp.where(row >= shift, pltpu.roll(v, shift, v.ndim - 2), 0.0)
    high = jnp.where(row < rows - shift, pltpu.roll(v, rows - shift, v.ndim - 2), 0.0)
    return 0.75 * v + 0.25 * jnp.where(even, low, high)


def zero_pads(*refs):
    for ref in refs:
        ref[0] = jnp.zeros(ref.shape[1:], jnp.float32)
        ref[ref.shape[0] - 1] = jnp.zeros(ref.shape[1:], jnp.float32)


def core_of():
    return lax.rem(lax.axis_index("gy"), 2)


def pack_kernel(geo, own_b, own_k, sib_b, sib_k, z_out, dp_out, dm_out):
    core = core_of()
    bx, ye = geo["bx"], geo["ye"]
    base = jnp.where(core == 1, LANES - REACH_Z, 0)
    lane = lanes_of((ye, LANES))

    def pack(out, first_b, count_b, first_k, count_k):
        for refs, half in (((own_b, own_k), core), ((sib_b, sib_k), 1 - core)):
            rows = pl.ds(pl.multiple_of(half * ye, 8), ye)
            planes = [(refs[0], first_b + p) for p in range(count_b)] + [(refs[1], first_k + p) for p in range(count_k)]
            for m in range(out.shape[0]):
                packed = jnp.zeros((ye, LANES), jnp.float32)
                for q, (ref, p) in enumerate(planes[m * SLOTS:(m + 1) * SLOTS]):
                    moved = pltpu.roll(ref[p], lax.rem(REACH_Z * q - base + LANES, LANES), 1)
                    packed = jnp.where((lane >= REACH_Z * q) & (lane < REACH_Z * (q + 1)), moved, packed)
                out[m, rows] = packed

    pack(z_out, 0, bx, 0, bx)
    high_b, high_k = bx - REACH_XB, bx - REACH_X
    pack(dp_out, jnp.where(core == 0, high_b, 0), REACH_XB, jnp.where(core == 0, high_k, 0), REACH_X)
    pack(dm_out, jnp.where(core == 0, 0, high_b), REACH_XB, jnp.where(core == 0, 0, high_k), REACH_X)


def down_kernel(geo, *refs):
    (own_b, own_k, sib_b, sib_k, even_own, odd_own, any_even, any_odd, any_z, any_dp, any_dm,
     packed_out, even_out, odd_out, o_cx, o_cy, o_cz, o_iv, o_g0, o_w, p_cx, p_cy, p_cz, p_iv, p_g0, p_w,
     even_sib, odd_sib, z_in, dp_in, dm_in,
     k0, cx, cy, cz, iv, ds, g0, g, d1, d2,
     k1, ex, ey, ez, ei, es, h0, h, f1, f2, u1, half_y, half_y1, sems, in_sems) = refs
    core = core_of()
    ix, nx = lax.axis_index("gx"), lax.axis_size("gx")
    iz, nz = lax.axis_index("gz"), lax.axis_size("gz")
    bx, ye, yw, xw = geo["bx"], geo["ye"], geo["yw"], geo["xw"]
    z_there = jnp.where(core == 0, iz > 0, iz < nz - 1)
    lo_there, hi_there = ix > 0, ix < nx - 1
    even = lax.rem(ix, 2) == 0

    arrivals = []
    for i, (source, target) in enumerate(
            ((any_even, even_sib), (any_odd, odd_sib), (any_z, z_in), (any_dp, dp_in), (any_dm, dm_in))):
        copy = pltpu.make_async_copy(source, target, in_sems.at[i])
        copy.start()
        arrivals.append(copy)

    lane = lanes_of((yw, LANES))
    halo_lanes = jnp.where(core == 0, lane - (LANES - REACH_Z), REACH_Z - 1 - lane) >= 0
    base = jnp.where(core == 0, LANES - REACH_Z, 0)

    def strip(ref, p):
        return pltpu.roll(ref[p // SLOTS], lax.rem(base - REACH_Z * (p % SLOTS) + LANES, LANES), 1)

    own_rows = pl.ds(pl.multiple_of(core * ye, 8), ye)
    sib_rows = pl.ds(pl.multiple_of((1 - core) * ye, 8), ye)
    zero_pads(k0, d1, d2, k1, f1, f2)
    windows = ((g0, own_b, sib_b, REACH_XB, 0, 0), (k0, own_k, sib_k, REACH_X, REACH_XB, bx))
    for p in range(REACH_X - REACH_XB):
        g0[1 + p] = jnp.zeros((yw, LANES), jnp.float32)
        g0[xw - p] = jnp.zeros((yw, LANES), jnp.float32)

    def halos(from_even, from_odd, rows):
        for window, _, _, width, at, _ in windows:
            e, o = from_even[pl.ds(at, width)], from_odd[pl.ds(at, width)]
            window[pl.ds(1 + REACH_X - width, width), rows] = jnp.where(lo_there, jnp.where(even, o, e), 0.0)
            window[pl.ds(1 + REACH_X + bx, width), rows] = jnp.where(hi_there, jnp.where(even, e, o), 0.0)

    for window, own, sib, _, _, _ in windows:
        window[pl.ds(1 + REACH_X, bx), own_rows] = own[...]
        window[pl.ds(1 + REACH_X, bx), sib_rows] = sib[...]
    halos(even_own, odd_own, own_rows)
    for copy in arrivals:
        copy.wait()
    halos(even_sib, odd_sib, sib_rows)
    for window, _, _, width, at_d, at_z in windows:
        for p in range(bx):
            at = 1 + REACH_X + p
            window[at] = jnp.where(halo_lanes, jnp.where(z_there, strip(z_in, at_z + p), 0.0), window[at])
        for p in range(width):
            plus, minus = strip(dp_in, at_d + p), strip(dm_in, at_d + p)
            low = jnp.where(core == 0, minus, plus)
            high = jnp.where(core == 0, plus, minus)
            at = 1 + REACH_X - width + p
            window[at] = jnp.where(halo_lanes, jnp.where(z_there & lo_there, low, 0.0), window[at])
            at = 1 + REACH_X + bx + p
            window[at] = jnp.where(halo_lanes, jnp.where(z_there & hi_there, high, 0.0), window[at])

    grid = Grid(xw, yw, LANES, 1, 1, False, 8)

    def first(at, here, inverse):
        scaled = g0[here] * inverse
        g0[here] = scaled
        d1[here] = FACTORS[0][1] * scaled

    grid.setup(k0, cx, cy, cz, iv, ds, 1.0, first)
    own0 = 1 + REACH_X - WIN0
    wide0 = bx + 2 * WIN0
    copies = []

    def send(source, start, count, target):
        copy = pltpu.make_async_copy(source.at[pl.ds(start, count)], target, sems.at[len(copies)])
        copy.start()
        copies.append(copy)

    send(cx, own0 - 1, wide0 + 1, o_cx)
    send(cy, own0, wide0, o_cy)
    send(cz, own0, wide0, o_cz)
    send(iv, own0, wide0, o_iv)
    send(g0, own0, wide0, o_g0)

    def restrict(source, target, tmp, x_count, at, y_first, y_rows, shift):
        for i in range(x_count):
            j = i % tmp.shape[0]
            tmp[j] = source[at + 2 * i] + source[at + 2 * i + 1]
            v = tmp[j, pl.ds(y_first, y_rows // 2, stride=2)] + tmp[j, pl.ds(y_first + 1, y_rows // 2, stride=2)]
            target(i, 0.125 * pair_z(v, shift, LANES))

    x1, y1 = xw // 2, yw // 2

    def put_k1(i, v):
        k1[1 + i] = v

    def put_b1(i, v):
        h0[1 + i] = v

    restrict(k0, put_k1, half_y, x1, 1, 0, yw, 1)
    coeffs = (cx, cy, cz, iv)

    def second(here, v, value, direction):
        g[here] = value
        d2[here] = direction

    grid.step(coeffs, d1, g0, *FACTORS[1], second)

    def third(here, v, value, direction):
        g[here] = value
        k0[here] = d1[here] + v + direction
        d1[here] = direction

    grid.step(coeffs, d2, g, *FACTORS[2], third)
    send(k0, own0, wide0, o_w)

    def residual(here, v, value, direction):
        g[here] = value * ds[here]

    grid.step(coeffs, d1, g, 0.0, None, residual)

    restrict(g, put_b1, half_y, x1, 1, 0, yw, 1)
    grid1 = Grid(x1, y1, LANES, 1, 2, False, geo["chunk1"])

    def first1(at, here, inverse):
        scaled = 4.0 * (h0[here] * inverse)
        h0[here] = scaled
        f1[here] = FACTORS[0][1] * scaled

    grid1.setup(k1, ex, ey, ez, ei, es, 0.25, first1)
    own1 = 1 + REACH_X // 2 - WIN1
    wide1 = bx // 2 + 2 * WIN1
    send(ex, own1 - 1, wide1 + 1, p_cx)
    send(ey, own1, wide1, p_cy)
    send(ez, own1, wide1, p_cz)
    send(ei, own1, wide1, p_iv)
    send(h0, own1, wide1, p_g0)
    coeffs1 = (ex, ey, ez, ei)

    def second1(here, v, value, direction):
        h[here] = value
        f2[here] = direction

    grid1.step(coeffs1, f1, h0, *FACTORS[1], second1)

    def third1(here, v, value, direction):
        h[here] = value
        u1[here] = f1[here] + v + direction
        f1[here] = direction

    grid1.step(coeffs1, f2, h, *FACTORS[2], third1)
    send(u1, own1, wide1, p_w)
    mine = 1 + REACH_X // 2
    last = mine + bx // 2
    for source, low, high, at, count in ((u1, mine + 1, last - WIN1, 0, 5), (h0, mine + 3, last - 5, 5, 2)):
        low, high = source[pl.ds(low, count)], source[pl.ds(high, count)]
        even_out[pl.ds(at, count)] = jnp.where(even, high, low)
        odd_out[pl.ds(at, count)] = jnp.where(even, low, high)

    def residual1(here, v, value, direction):
        h[here] = value * es[here]

    grid1.step(coeffs1, f1, h, 0.0, None, residual1)

    place = lax.rem(2 * iz + core, 8)
    x2, y2 = bx // 4, geo["by"] // 2
    row, column = rows_of((LANES, LANES)), lanes_of((LANES, LANES))
    pick = (row == HALF * core + 4 * lax.rem(column, 16)).astype(jnp.float32)
    slot = lanes_of((y2, LANES)) // 16
    for f, source in enumerate((h, k1)):
        boxes = []
        restrict(source, lambda i, v, boxes=boxes: boxes.append(v), half_y1, x2, 1 + REACH_X // 2, geo["oy"] // 2, 2 * y2, 2)
        stacked = jnp.concatenate(boxes, axis=0)
        picked = jnp.dot(stacked, pick, precision=lax.Precision.HIGHEST, preferred_element_type=jnp.float32)
        packed = jnp.zeros((y2, LANES), jnp.float32)
        for p in range(x2):
            packed = jnp.where(slot == lax.rem(p + place, 8), picked[p * y2:(p + 1) * y2], packed)
        packed_out[f] = packed
    for copy in copies:
        copy.wait()


def up_kernel(geo, *refs):
    refs = list(refs)

    def take(count):
        taken = refs[:count]
        del refs[:count]
        return taken

    gathered = take(2 if geo["packed"] else 1)
    from_even, from_odd = take(2)
    in0, in1 = take(6), take(6)
    o_send, o_u, o_r = take(3)
    k2, cx2, cy2, cz2, iv2, ds2, g02, g2, da2, db2, w2, e2 = take(12)
    k3, cx3, cy3, cz3, iv3, ds3, g03, g3, da3, db3, w3, e3 = take(12)
    k4, cx4, cy4, cz4, iv4, g04, g4, da4, db4, e4 = take(10)
    cx1, cy1, cz1, iv1, g01, w1, u1, g1, da1, db1, e1 = take(11)
    cx0, cy0, cz0, iv0, g00, w0, u0, g0, da0, db0 = take(10)
    e2_wide, sems = take(2)
    core = core_of()
    ix, nx = lax.axis_index("gx"), lax.axis_size("gx")
    iz, nz = lax.axis_index("gz"), lax.axis_size("gz")
    yp = lax.axis_index("gy") // 2
    bx, by, yw = geo["bx"], geo["by"], geo["yw"]
    x2, y2, z2 = geo["x2"], geo["y2"], geo["z2"]
    wide0, wide1 = bx + 2 * WIN0, bx // 2 + 2 * WIN1

    copies = []
    for sources, targets, wide in ((in1, (cx1, cy1, cz1, iv1, g01, w1), wide1), (in0, (cx0, cy0, cz0, iv0, g00, w0), wide0)):
        for i, (source, target) in enumerate(zip(sources, targets)):
            there = target.at[pl.ds(0, wide + 1)] if i == 0 else target.at[pl.ds(1, wide)]
            copy = pltpu.make_async_copy(source, there, sems.at[len(copies)])
            copy.start()
            copies.append(copy)

    zero_pads(k2, da2, db2, e2, k3, da3, db3, e3, k4, da4, db4, e4, u1, da1, db1, u0, da0, db0)

    if geo["packed"]:
        slot = lanes_of((y2, LANES)) // 16
        for jx in range(nx):
            gx = lax.bitwise_xor(ix, jx)
            for f, target in ((0, g02), (1, k2)):
                for p in range(8):
                    merged = jnp.zeros((y2, LANES), jnp.float32)
                    for jz in range(nz):
                        gz = lax.bitwise_xor(iz, jz)
                        for source, cc in ((gathered[0], core), (gathered[1], 1 - core)):
                            place = 2 * gz + cc
                            merged = jnp.where(slot == lax.rem(p + place, 8), source[jx, jz, f], merged)
                    target[1 + 8 * gx + p] = pltpu.roll(merged, (LANES - 16 * p) % LANES, 1)
    else:
        g02[pl.ds(1, x2)] = gathered[0][0]
        k2[pl.ds(1, x2)] = gathered[0][1]

    def descend(grid, level, k, cx, cy, cz, iv, ds, g0, first_target):
        def first(at, here, inverse):
            scaled = 4.0**level * (g0[here] * inverse)
            g0[here] = scaled
            first_target[here] = FACTORS[0][1] * scaled

        grid.setup(k, cx, cy, cz, iv, ds, 0.25**level, first)

    def pre(grid, level, k, cx, cy, cz, iv, ds, g0, g, da, db, w):
        descend(grid, level, k, cx, cy, cz, iv, ds, g0, da)
        coeffs = (cx, cy, cz, iv)

        def second(here, v, value, direction):
            g[here] = value
            db[here] = direction

        grid.step(coeffs, da, g0, *FACTORS[1], second)

        def third(here, v, value, direction):
            g[here] = value
            w[here] = da[here] + v + direction
            da[here] = direction

        grid.step(coeffs, db, g, *FACTORS[2], third)

        def residual(here, v, value, direction):
            g[here] = value * ds[here]

        grid.step(coeffs, da, g, 0.0, None, residual)

    def post(grid, coeffs, g0, u, g, da, db, result):
        def one(here, v, value, direction):
            g[here] = value
            da[here] = direction

        grid.step(coeffs, u, g0, *FACTORS[0], one)

        def two(here, v, value, direction):
            g[here] = value
            db[here] = direction

        grid.step(coeffs, da, g, *FACTORS[1], two)

        def three(here, v, value, direction):
            g[here] = value
            result[here] = u[here] + da[here] + v + direction
            da[here] = direction

        grid.step(coeffs, db, g, *FACTORS[2], three)

    def restrict(fine, coarse, count, shift):
        for i in range(count):
            v = fine[1 + 2 * i] + fine[2 + 2 * i]
            coarse[1 + i] = 0.125 * pair_z(pair_y(v, shift, y2), shift, z2)

    def prolong(coarse, w, target, count, shift):
        for i in range(count):
            middle = 0.75 * coarse[1 + i]
            for j, side in ((0, coarse[i]), (1, coarse[2 + i])):
                v = spread_y(middle + 0.25 * side, shift, y2)
                target[1 + 2 * i + j] = w[1 + 2 * i + j] + spread_z(v, shift, z2, True)

    def size_of(x):
        planes = max(1, 32 // ((y2 // 8) * (z2 // LANES)))
        return min(x, planes)

    x3, x4 = x2 // 2, x2 // 4
    grid2 = Grid(x2, y2, z2, 1, 1, True, size_of(x2))
    grid3 = Grid(x3, y2, z2, 2, 2, True, size_of(x3))
    grid4 = Grid(x4, y2, z2, 4, 4, True, size_of(x4))
    pre(grid2, 2, k2, cx2, cy2, cz2, iv2, ds2, g02, g2, da2, db2, w2)
    restrict(k2, k3, x3, 1)
    restrict(g2, g03, x3, 1)
    pre(grid3, 3, k3, cx3, cy3, cz3, iv3, ds3, g03, g3, da3, db3, w3)
    restrict(k3, k4, x4, 2)
    restrict(g3, g04, x4, 2)
    descend(grid4, 4, k4, cx4, cy4, cz4, iv4, None, g04, da4)
    e4[pl.ds(1, x4)] = da4[pl.ds(1, x4)]
    for sweep in range(1, COARSE_STEPS):
        src, dst = (da4, db4) if sweep % 2 else (db4, da4)

        def coarse(here, v, value, direction):
            g4[here] = value
            dst[here] = direction
            e4[here] = e4[here] + direction

        grid4.step((cx4, cy4, cz4, iv4), src, g04 if sweep == 1 else g4, *COARSE_FACTORS[sweep], coarse)
    prolong(e4, w3, e3, x4, 2)
    post(grid3, (cx3, cy3, cz3, iv3), g03, e3, g3, da3, db3, w3)
    e3[pl.ds(1, x3)] = w3[pl.ds(1, x3)]
    prolong(e3, w2, e2, x3, 1)
    post(grid2, (cx2, cy2, cz2, iv2), g02, e2, g2, da2, db2, w2)

    pad_y = geo["pad_y"]
    if pad_y:
        e2_wide[...] = jnp.zeros(e2_wide.shape, jnp.float32)
    else:
        edge = jnp.zeros((4,) + e2_wide.shape[1:], jnp.float32)
        e2_wide[pl.ds(0, 4)] = edge
        e2_wide[pl.ds(x2 + 4, 4)] = edge
    e2_wide[pl.ds(4, x2), pl.ds(pad_y, y2)] = w2[pl.ds(1, x2)]
    x2w, y2w = bx // 4 + 8, yw // 4
    cells, lane = rows_of((z2, LANES)), lanes_of((z2, LANES))
    shifted = jnp.where(core == 0, jnp.where(lane >= 104, -32, 0), jnp.where(lane < 24, 32, 0))
    pick = (cells == 32 * iz + lane // 4 + shifted).astype(jnp.float32)
    start = (bx // 4) * ix
    rows = pl.ds(pl.multiple_of(8 * yp, 8), y2w) if pad_y else pl.ds(0, y2w)
    window = e2_wide[pl.ds(start, x2w), rows].reshape(x2w * y2w, z2)
    window = jnp.dot(window, pick, precision=lax.Precision.HIGHEST, preferred_element_type=jnp.float32)
    window = window.reshape(x2w, y2w, LANES)

    def place_rows(target, plane, v, count):
        row = rows_of(v.shape)
        low = jnp.where(row >= 1, pltpu.roll(v, 1, 0), 0.0)
        high = jnp.where(row < count - 1, pltpu.roll(v, count - 1, 0), 0.0)
        target[plane, pl.ds(0, count, stride=2)] = 0.75 * v + 0.25 * low
        target[plane, pl.ds(1, count, stride=2)] = 0.75 * v + 0.25 * high

    for copy in copies[:6]:
        copy.wait()
    even, last1 = lax.rem(ix, 2) == 0, 1 + WIN1 + bx // 2
    for target, low, high, at, count in ((w1, 1, last1 + 1, 0, 5), (g01, 2, last1 + 3, 5, 2)):
        e, o = from_even[pl.ds(at, count)], from_odd[pl.ds(at, count)]
        low, high = pl.ds(low, count), pl.ds(high, count)
        target[low] = jnp.where(ix > 0, jnp.where(even, o, e), target[low])
        target[high] = jnp.where(ix < nx - 1, jnp.where(even, e, o), target[high])
    for plane in range(wide1):
        j = plane // 2
        v = 0.75 * window[j + 1] + 0.25 * window[j + 2 if plane % 2 else j]
        place_rows(u1, 1 + plane, spread_z(v, 2, LANES, False), y2w)
    grid1 = Grid(wide1, yw // 2, LANES, 1, 2, False, geo["chunk1"])

    def start1(at):
        here = pl.ds(at, grid1.size)
        u1[here] = jnp.where(iv1[here] > 0.0, w1[here] + u1[here], 0.0)

    chunks(wide1, start1, grid1.size)
    post(grid1, (cx1, cy1, cz1, iv1), g01, u1, g1, da1, db1, e1)

    for copy in copies[6:]:
        copy.wait()
    grid0 = Grid(wide0, yw, LANES, 1, 1, False, 8)

    def fill(i, carry):
        at = WIN1 + 1 - WIN0 // 2 + i
        middle = 0.75 * e1[at]
        for j, side in ((0, e1[at - 1]), (1, e1[at + 1])):
            place_rows(u0, 1 + 2 * i + j, spread_z(middle + 0.25 * side, 1, LANES, False), yw // 2)
        return carry

    lax.fori_loop(0, wide0 // 2, fill, 0, unroll=4)

    def start0(at):
        here = pl.ds(at, grid0.size)
        u0[here] = jnp.where(iv0[here] > 0.0, w0[here] + u0[here], 0.0)

    chunks(wide0, start0, grid0.size)
    coeffs0 = (cx0, cy0, cz0, iv0)
    post(grid0, coeffs0, g00, u0, g0, da0, db0, w0)

    def residual(here, v, value, direction):
        g0[here] = value / iv0[here]

    grid0.step(coeffs0, da0, g0, 0.0, None, residual, 1 + WIN0, bx)
    own = pl.ds(1 + WIN0, bx)
    own_rows = pl.ds(pl.multiple_of(geo["oy"] + core * by, 8), by)
    sib_rows = pl.ds(pl.multiple_of(geo["oy"] + (1 - core) * by, 8), by)
    mine = lanes_of((bx, by, LANES)) // HALF == core
    o_send[...] = jnp.where(mine, w0[own, sib_rows], pltpu.roll(g0[own, sib_rows], HALF, 2))
    o_u[...] = w0[own, own_rows]
    o_r[...] = g0[own, own_rows]


def merge_kernel(u_ref, r_ref, other, u_out, r_out):
    v = other[...]
    mine = lanes_of(v.shape) // HALF == core_of()
    u_out[...] = jnp.where(mine, u_ref[...], v)
    r_out[...] = jnp.where(mine, r_ref[...], pltpu.roll(v, HALF, 2))


PARAMS = pltpu.CompilerParams(vmem_limit_bytes=60 * 1024 * 1024)


def array(*shape):
    return jax.ShapeDtypeStruct(shape, jnp.float32)


def on_device(right_side, conductivity):
    bx, by, bz = right_side.shape
    nx, ny, nz = (lax.axis_size(axis) for axis in AXES)
    pairs = ny // 2
    ix, iy, iz = (lax.axis_index(axis) for axis in AXES)
    core = iy % 2

    def index(x, p, c, z):
        return ((x % nx) * ny + (p % pairs) * 2 + c) * nz + z % nz

    every = [(x, p, z) for x in range(nx) for p in range(pairs) for z in range(nz)]

    def sibling(v):
        return lax.ppermute(v, "gy", [(i, i ^ 1) for i in range(ny)])

    def xor(v, axis, k):
        return lax.ppermute(v, axis, [(i, i ^ k) for i in range(lax.axis_size(axis))])

    def paired(v, first):
        perm = [(i, i) for i in range(nx)]
        for i in range(first, nx - 1, 2):
            perm[i], perm[i + 1] = (i, i + 1), (i + 1, i)
        return lax.ppermute(v, "gx", perm)

    def facing(v, dx):
        perm = {}
        for x, p, z in every:
            if z > 0 and 0 <= x + dx < nx:
                a, b = index(x, p, 0, z), index(x + dx, p, 1, z - 1)
                perm[a], perm[b] = b, a
        return lax.ppermute(v, AXES, [(i, perm.get(i, i)) for i in range(nx * ny * nz)])

    own_b, own_k, ye = right_side, conductivity, by
    if ny > 2:
        near = []
        far = []
        for p in range(pairs):
            near += [(2 * p, 2 * ((p - 1) % pairs) + 1), (2 * ((p - 1) % pairs) + 1, 2 * p)]
            far += [(2 * p, 2 * ((p + 1) % pairs)), (2 * p + 1, 2 * ((p - 1) % pairs) + 1)]
        there = jnp.where(core == 0, iy > 0, iy < ny - 1)

        def widened(v):
            one = jnp.where(there, lax.ppermute(v, "gy", near), 0.0)
            two = jnp.where(there, lax.ppermute(v, "gy", far), 0.0)
            return jnp.where(core == 0, jnp.concatenate([two, one, v], 1), jnp.concatenate([v, one, two], 1))

        own_b, own_k = widened(own_b), widened(own_k)
        ye = 3 * by
    yw = 2 * ye
    xw = bx + 2 * REACH_X
    geo = dict(
        bx=bx, by=by, ye=ye, yw=yw, xw=xw, oy=(yw - 2 * by) // 2, chunk1=14 if yw == 32 else 4,
        packed=pairs == 1 and 32 * nz == LANES, x2=bx // 4 * nx, y2=by // 4 * ny, z2=bz // 4 * nz,
        pad_y=(yw // 4 - by // 2) // 2,
    )

    sib_b, sib_k = sibling(own_b), sibling(own_k)
    even = ix % 2 == 0
    high = jnp.concatenate([own_b[bx - REACH_XB:], own_k[bx - REACH_X:]], 0)
    low = jnp.concatenate([own_b[:REACH_XB], own_k[:REACH_X]], 0)
    even_own = paired(jnp.where(even, high, low), 0)
    odd_own = paired(jnp.where(even, low, high), 1)
    m, md = -(-2 * bx // SLOTS), -(-(REACH_X + REACH_XB) // SLOTS)
    z_send, dp_send, dm_send = pl.pallas_call(
        functools.partial(pack_kernel, geo),
        out_shape=[array(m, yw, LANES), array(md, yw, LANES), array(md, yw, LANES)],
        compiler_params=PARAMS, name="pack_z",
        cost_estimate=pl.CostEstimate(flops=4_000_000, bytes_accessed=8_000_000, transcendentals=0),
    )(own_b, own_k, sib_b, sib_k)
    z_in, dp_in, dm_in = facing(z_send, 0), facing(dp_send, 1), facing(dm_send, -1)
    even_sib, odd_sib = sibling(even_own), sibling(odd_own)

    wide0, wide1 = bx + 2 * WIN0, bx // 2 + 2 * WIN1
    x1, y1 = xw // 2, yw // 2
    some0 = pltpu.VMEM((xw + 2, yw, LANES), jnp.float32)
    some1 = pltpu.VMEM((x1 + 2, y1, LANES), jnp.float32)
    passed0 = [array(wide0 + (i == 0), yw, LANES) for i in range(6)]
    passed1 = [array(wide1 + (i == 0), y1, LANES) for i in range(6)]
    vmem, anywhere = pl.BlockSpec(memory_space=pltpu.VMEM), pl.BlockSpec(memory_space=pl.ANY)
    edge = 7
    down = pl.pallas_call(
        functools.partial(down_kernel, geo),
        out_shape=[array(2, by // 2, LANES), array(edge, y1, LANES), array(edge, y1, LANES)] + passed0 + passed1,
        in_specs=[vmem] * 6 + [anywhere] * 5,
        out_specs=[vmem] * 3 + [anywhere] * 12,
        scratch_shapes=[pltpu.VMEM(v.shape, jnp.float32) for v in (even_sib, odd_sib, z_in, dp_in, dm_in)]
        + [some0] * 10 + [some1] * 11
        + [pltpu.VMEM((6, yw, LANES), jnp.float32), pltpu.VMEM((6, y1, LANES), jnp.float32)]
        + [pltpu.SemaphoreType.DMA((12,)), pltpu.SemaphoreType.DMA((5,))],
        compiler_params=PARAMS, name="down",
    )(own_b, own_k, sib_b, sib_k, even_own, odd_own, even_sib, odd_sib, z_in, dp_in, dm_in)
    packed, even_send, odd_send, passed = down[0], down[1], down[2], down[3:]
    from_even, from_odd = paired(even_send, 0), paired(odd_send, 1)

    if geo["packed"]:
        along_z = jnp.stack([packed] + [xor(packed, "gz", j) for j in range(1, nz)])
        along_x = jnp.stack([along_z] + [xor(along_z, "gx", j) for j in range(1, nx)])
        gathered = (along_x, sibling(along_x))
    else:
        pieces = lax.all_gather(packed, AXES).reshape(nx, pairs, 2, nz, 2, by // 2, 8, 16)
        order = (jnp.arange(8) + 2 * jnp.arange(nz)[:, None, None] + jnp.arange(2)[:, None]) % 8
        order = jnp.transpose(order, (1, 0, 2))[None, None, :, :, None, None, :, None]
        pieces = jnp.take_along_axis(pieces, order, axis=6)
        gathered = (jnp.transpose(pieces, (4, 0, 6, 1, 5, 3, 2, 7)).reshape(2, geo["x2"], geo["y2"], geo["z2"]),)

    def level(planes, rows, lanes):
        return pltpu.VMEM((planes + 2, rows, lanes), jnp.float32)

    x2, y2, z2 = geo["x2"], geo["y2"], geo["z2"]
    send, keep_u, keep_r = pl.pallas_call(
        functools.partial(up_kernel, geo),
        out_shape=[array(bx, by, LANES)] * 3,
        in_specs=[vmem] * (len(gathered) + 2) + [anywhere] * 12,
        scratch_shapes=[level(x2, y2, z2)] * 12 + [level(x2 // 2, y2, z2)] * 12 + [level(x2 // 4, y2, z2)] * 10
        + [level(wide1, y1, LANES)] * 11 + [level(wide0, yw, LANES)] * 10
        + [pltpu.VMEM((x2 + 8, y2 + 2 * geo["pad_y"], z2), jnp.float32), pltpu.SemaphoreType.DMA((12,))],
        compiler_params=PARAMS, name="up",
    )(*gathered, from_even, from_odd, *passed)
    return pl.pallas_call(
        merge_kernel, out_shape=[array(bx, by, LANES)] * 2, compiler_params=PARAMS, name="merge",
    )(keep_u, keep_r, sibling(send))


def solution(mesh):
    specs = (P(*AXES), P(*AXES))
    return jax.shard_map(on_device, mesh=mesh, in_specs=specs, out_specs=specs, check_vma=False)
```

```python
import functools
import math
import jax
import jax.numpy as jnp
from jax import lax
from jax.experimental import pallas as pl
from jax.experimental.pallas import tpu as pltpu
from jax.sharding import PartitionSpec as P

LEVELS = 4
STEPS = 3
COARSE_STEPS = 8
LOWER_EDGE = 0.3
UPPER_EDGE = 2.0

LANES = 128
HALF = 64
REACH_X = 12
REACH_XB = 9
REACH_Z = 20
WIN0 = 4
WIN1 = REACH_X // 2
SLOTS = LANES // REACH_Z
SLAB = -(-(REACH_X + REACH_XB) // SLOTS)
VMEM_LIMIT = 48 * 1024 * 1024
AXES = ("gx", "gy", "gz")


def chebyshev_factors(sweeps):
    centre_value = 0.5 * (UPPER_EDGE + LOWER_EDGE)
    half_width = 0.5 * (UPPER_EDGE - LOWER_EDGE)
    ratio_value = centre_value / half_width
    damping = 1.0 / ratio_value
    factors = [(0.0, 1.0 / centre_value)]
    for _ in range(1, sweeps):
        damping_next = 1.0 / (2.0 * ratio_value - damping)
        factors.append((damping_next * damping, 2.0 * damping_next / half_width))
        damping = damping_next
    return factors


FACTORS = chebyshev_factors(STEPS)
COARSE_FACTORS = chebyshev_factors(COARSE_STEPS)


def chunks(count, body, size, first=1):
    if count == size:
        body(first)
    else:
        def step(i, carry):
            body(first + i * size)
            return carry
        lax.fori_loop(0, count // size, step, 0)


def rows_of(shape):
    return lax.broadcasted_iota(jnp.int32, shape, len(shape) - 2)


def lanes_of(shape):
    return lax.broadcasted_iota(jnp.int32, shape, len(shape) - 1)


class Grid:
    def __init__(self, x, y, z, sy, sz, whole_z, size):
        self.x, self.y, self.z, self.sy, self.sz = x, y, z, sy, sz
        self.whole_z, self.size = whole_z, size

    def up_y(self, v):
        return pltpu.roll(v, self.y - self.sy, v.ndim - 2)

    def down_y(self, v):
        return pltpu.roll(v, self.sy, v.ndim - 2)

    def up_z(self, v):
        return pltpu.roll(v, self.z - self.sz, v.ndim - 1)

    def down_z(self, v):
        return pltpu.roll(v, self.sz, v.ndim - 1)

    def setup(self, k_ref, cx, cy, cz, iv, ds, scale, after=None):
        cx[0] = 0.5 * (k_ref[0] + k_ref[1])

        def body(at):
            here = pl.ds(at, self.size)
            k = k_ref[here]
            row, lane = rows_of(k.shape), lanes_of(k.shape)
            k_next = k_ref[pl.ds(at + 1, self.size)]
            k_prev = k_ref[pl.ds(at - 1, self.size)]
            not_last = row < self.y - self.sy
            k_up = jnp.where(not_last, self.up_y(k), 0.0)
            k_down = jnp.where(row >= self.sy, self.down_y(k), 0.0)
            z_up, z_down = self.up_z(k), self.down_z(k)
            if self.whole_z:
                inner = lane < self.z - self.sz
                z_up = jnp.where(inner, z_up, 0.0)
                z_down = jnp.where(lane >= self.sz, z_down, 0.0)
            total = 3.0 * k + 0.5 * ((k_next + k_prev) + (k_up + k_down) + (z_up + z_down))
            inverse = jnp.where(k > 0.0, 1.0 / total, 0.0)
            cx[here] = 0.5 * (k + k_next)
            cy[here] = jnp.where(not_last, 0.5 * (k + k_up), 0.0)
            across = 0.5 * (k + z_up)
            cz[here] = jnp.where(inner, across, 0.0) if self.whole_z else across
            iv[here] = inverse
            if ds is not None:
                ds[here] = scale * total
            if after is not None:
                after(at, here, inverse)

        chunks(self.x, body, self.size)

    def step(self, coeffs, src, g_in, keep, push, out, first=1, count=None):
        cx, cy, cz, iv = coeffs

        def body(at):
            here, before = pl.ds(at, self.size), pl.ds(at - 1, self.size)
            v = src[here]
            y_coeff, z_coeff = cy[here], cz[here]
            near = cx[here] * src[pl.ds(at + 1, self.size)] + cx[before] * src[before]
            near = near + (y_coeff * self.up_y(v) + self.down_y(y_coeff * v))
            near = near + (z_coeff * self.up_z(v) + self.down_z(z_coeff * v))
            g = g_in[here] - v + iv[here] * near
            out(here, v, g, None if push is None else (keep * v + push * g if keep else push * g))

        chunks(count or self.x, body, self.size, first)


def pair_z(v, shift, lanes):
    even = (lanes_of(v.shape) // shift) % 2 == 0
    return v + jnp.where(even, pltpu.roll(v, lanes - shift, v.ndim - 1), pltpu.roll(v, shift, v.ndim - 1))


def pair_y(v, shift, rows):
    even = (rows_of(v.shape) // shift) % 2 == 0
    return v + jnp.where(even, pltpu.roll(v, rows - shift, v.ndim - 2), pltpu.roll(v, shift, v.ndim - 2))


def spread_z(v, shift, lanes, whole):
    lane = lanes_of(v.shape)
    even = (lane // shift) % 2 == 0
    low, high = pltpu.roll(v, shift, v.ndim - 1), pltpu.roll(v, lanes - shift, v.ndim - 1)
    if whole:
        low = jnp.where(lane >= shift, low, 0.0)
        high = jnp.where(lane < lanes - shift, high, 0.0)
    return 0.75 * v + 0.25 * jnp.where(even, low, high)


def spread_y(v, shift, rows):
    row = rows_of(v.shape)
    even = (row // shift) % 2 == 0
    low = jnp.where(row >= shift, pltpu.roll(v, shift, v.ndim - 2), 0.0)
    high = jnp.where(row < rows - shift, pltpu.roll(v, rows - shift, v.ndim - 2), 0.0)
    return 0.75 * v + 0.25 * jnp.where(even, low, high)


def zero_pads(*refs):
    for ref in refs:
        ref[0] = jnp.zeros(ref.shape[1:], jnp.float32)
        ref[ref.shape[0] - 1] = jnp.zeros(ref.shape[1:], jnp.float32)


def core_of():
    return lax.rem(lax.axis_index("gy"), 2)


def fetch(pairs, sems, first=0):
    copies = [pltpu.make_async_copy(source, target, sems.at[first + i]) for i, (source, target) in enumerate(pairs)]
    for copy in copies:
        copy.start()
    return copies


def strip_planes(bx):
    b0, b1, k0, k1 = REACH_XB, bx - REACH_XB, REACH_X, bx - REACH_X
    parts = ((0, b0, 0, k0), (b0, b1, k0, k1), (b1, bx, k1, bx))
    slots = []
    for b_first, b_last, k_first, k_last in parts:
        slots += [(0, p) for p in range(b_first, b_last)] + [(1, p) for p in range(k_first, k_last)]
        slots += [None] * (-len(slots) % SLOTS)
    return slots


def pack_kernel(geo, lists, count, *refs):
    count //= 2
    arrays, sems, scratch = refs[:2 * count], refs[-1], refs[-1 - 2 * count:-1]
    z_out, own, sib = refs[-2 - 2 * count], scratch[:count], scratch[count:]
    core, ye = core_of(), geo["ye"]
    copies = fetch(list(zip(arrays, own + sib)), sems)
    base = jnp.where(core == 1, LANES - REACH_Z, 0)
    lane = lanes_of((ye, LANES))
    for i, (fields, half) in enumerate(((own, core), (sib, 1 - core))):
        for copy in copies[i * count:(i + 1) * count]:
            copy.wait()
        rows = pl.ds(pl.multiple_of(half * ye, 8), ye)
        for m in range(len(lists) // SLOTS):
            packed = jnp.zeros((ye, LANES), jnp.float32)
            for q, slot in enumerate(lists[m * SLOTS:(m + 1) * SLOTS]):
                if slot is not None:
                    moved = pltpu.roll(fields[slot[0]][slot[1]], lax.rem(REACH_Z * q - base + LANES, LANES), 1)
                    packed = jnp.where((lane >= REACH_Z * q) & (lane < REACH_Z * (q + 1)), moved, packed)
            z_out[m, rows] = packed


def passed_views(geo, ref):
    wide0, wide1, rows = geo["bx"] + 2 * WIN0, geo["bx"] // 2 + 2 * WIN1, geo["yw"] // 2
    views, at = [], 0
    for i in range(6):
        views.append(ref.at[pl.ds(at, wide0 + (i == 0))])
        at += wide0 + 1
    for i in range(6):
        views.append(ref.at[pl.ds(at + i // 2 * (wide1 + 1), wide1 + (i == 0)), pl.ds(i % 2 * rows, rows)])
    return views


def down_kernel(geo, *refs):
    ins, refs = refs[:8], refs[8:]
    (packed_any, even_any, odd_any, passed,
     own_in, sib_in, even_own, odd_own, even_sib, odd_sib, z_in, zx_in,
     packed_out, even_out, odd_out,
     k0, cx, cy, cz, iv, ds, g0, g, d1, d2,
     k1, ex, ey, ez, ei, es, h0, h, f1, f2, u1, half_y, half_y1, sems, in_sems) = refs
    core = core_of()
    ix, nx = lax.axis_index("gx"), lax.axis_size("gx")
    iz, nz = lax.axis_index("gz"), lax.axis_size("gz")
    bx, ye, yw, xw = geo["bx"], geo["ye"], geo["yw"], geo["xw"]
    z_there = jnp.where(core == 0, iz > 0, iz < nz - 1)
    lo_there, hi_there = ix > 0, ix < nx - 1
    even = lax.rem(ix, 2) == 0

    arrivals = fetch(list(zip(ins, (
        own_in, sib_in, even_own, odd_own, even_sib, odd_sib, z_in, zx_in))), in_sems)

    lane = lanes_of((yw, LANES))
    halo_lanes = jnp.where(core == 0, lane - (LANES - REACH_Z), REACH_Z - 1 - lane) >= 0
    base = jnp.where(core == 0, LANES - REACH_Z, 0)

    def strip(ref, p):
        return pltpu.roll(ref[p // SLOTS], lax.rem(base - REACH_Z * (p % SLOTS) + LANES, LANES), 1)

    own_rows = pl.ds(pl.multiple_of(core * ye, 8), ye)
    sib_rows = pl.ds(pl.multiple_of((1 - core) * ye, 8), ye)
    zero_pads(k0, d1, d2, k1, f1, f2)
    windows = ((g0, 0, REACH_XB, 0), (k0, bx, REACH_X, REACH_XB))
    for p in range(REACH_X - REACH_XB):
        g0[1 + p] = jnp.zeros((yw, LANES), jnp.float32)
        g0[xw - p] = jnp.zeros((yw, LANES), jnp.float32)

    def halos(from_even, from_odd, rows):
        for window, _, width, at in windows:
            e, o = from_even[pl.ds(at, width)], from_odd[pl.ds(at, width)]
            window[pl.ds(1 + REACH_X - width, width), rows] = jnp.where(lo_there, jnp.where(even, o, e), 0.0)
            window[pl.ds(1 + REACH_X + bx, width), rows] = jnp.where(hi_there, jnp.where(even, e, o), 0.0)

    for copy in arrivals:
        copy.wait()
    for window, at, _, _ in windows:
        window[pl.ds(1 + REACH_X, bx), own_rows] = own_in[pl.ds(at, bx)]
        window[pl.ds(1 + REACH_X, bx), sib_rows] = sib_in[pl.ds(at, bx)]
    halos(even_own, odd_own, own_rows)
    halos(even_sib, odd_sib, sib_rows)
    for slot, plane in enumerate(strip_planes(bx)):
        if plane is not None:
            window, at = windows[plane[0]][0], 1 + REACH_X + plane[1]
            window[at] = jnp.where(halo_lanes, jnp.where(z_there, strip(z_in, slot), 0.0), window[at])
    for window, _, width, slot in windows:
        for p in range(width):
            e, o = strip(zx_in, slot + p), strip(zx_in, SLAB * SLOTS + slot + p)
            at = 1 + REACH_X - width + p
            low = jnp.where(z_there & lo_there, jnp.where(even, o, e), 0.0)
            window[at] = jnp.where(halo_lanes, low, window[at])
            at = 1 + REACH_X + bx + p
            high = jnp.where(z_there & hi_there, jnp.where(even, e, o), 0.0)
            window[at] = jnp.where(halo_lanes, high, window[at])

    grid = Grid(xw, yw, LANES, 1, 1, False, 8)

    def first(at, here, inverse):
        scaled = g0[here] * inverse
        g0[here] = scaled
        d1[here] = FACTORS[0][1] * scaled

    grid.setup(k0, cx, cy, cz, iv, ds, 1.0, first)
    own0 = 1 + REACH_X - WIN0
    wide0 = bx + 2 * WIN0
    copies = []

    views = passed_views(geo, passed)

    def send(source, start, count):
        i = len(copies)
        copy = pltpu.make_async_copy(source.at[pl.ds(start, count)], views[i], sems.at[i])
        copy.start()
        copies.append(copy)

    send(cx, own0 - 1, wide0 + 1)
    send(cy, own0, wide0)
    send(cz, own0, wide0)
    send(iv, own0, wide0)
    send(g0, own0, wide0)

    def restrict(source, target, tmp, x_count, at, y_first, y_rows, shift):
        for i in range(x_count):
            j = i % tmp.shape[0]
            tmp[j] = source[at + 2 * i] + source[at + 2 * i + 1]
            v = tmp[j, pl.ds(y_first, y_rows // 2, stride=2)] + tmp[j, pl.ds(y_first + 1, y_rows // 2, stride=2)]
            target(i, 0.125 * pair_z(v, shift, LANES))

    x1, y1 = xw // 2, yw // 2

    def put_k1(i, v):
        k1[1 + i] = v

    def put_b1(i, v):
        h0[1 + i] = v

    restrict(k0, put_k1, half_y, x1, 1, 0, yw, 1)
    coeffs = (cx, cy, cz, iv)

    def second(here, v, value, direction):
        g[here] = value
        d2[here] = direction

    grid.step(coeffs, d1, g0, *FACTORS[1], second)

    def third(here, v, value, direction):
        g[here] = value
        k0[here] = d1[here] + v + direction
        d1[here] = direction

    grid.step(coeffs, d2, g, *FACTORS[2], third)
    send(k0, own0, wide0)

    def residual(here, v, value, direction):
        g[here] = value * ds[here]

    grid.step(coeffs, d1, g, 0.0, None, residual)

    restrict(g, put_b1, half_y, x1, 1, 0, yw, 1)
    grid1 = Grid(x1, y1, LANES, 1, 2, False, geo["chunk1"])

    def first1(at, here, inverse):
        scaled = 4.0 * (h0[here] * inverse)
        h0[here] = scaled
        f1[here] = FACTORS[0][1] * scaled

    grid1.setup(k1, ex, ey, ez, ei, es, 0.25, first1)
    own1 = 1 + REACH_X // 2 - WIN1
    wide1 = bx // 2 + 2 * WIN1
    send(ex, own1 - 1, wide1 + 1)
    send(ey, own1, wide1)
    send(ez, own1, wide1)
    send(ei, own1, wide1)
    send(h0, own1, wide1)
    coeffs1 = (ex, ey, ez, ei)

    def second1(here, v, value, direction):
        h[here] = value
        f2[here] = direction

    grid1.step(coeffs1, f1, h0, *FACTORS[1], second1)

    def third1(here, v, value, direction):
        h[here] = value
        u1[here] = f1[here] + v + direction
        f1[here] = direction

    grid1.step(coeffs1, f2, h, *FACTORS[2], third1)
    send(u1, own1, wide1)
    mine = 1 + REACH_X // 2
    last = mine + bx // 2
    for source, low, high, at, count in ((u1, mine + 1, last - WIN1, 0, 5), (h0, mine + 3, last - 5, 5, 2)):
        low, high = source[pl.ds(low, count)], source[pl.ds(high, count)]
        even_out[pl.ds(at, count)] = jnp.where(even, high, low)
        odd_out[pl.ds(at, count)] = jnp.where(even, low, high)
    copies += fetch(((even_out, even_any), (odd_out, odd_any)), sems, 12)

    def residual1(here, v, value, direction):
        h[here] = value * es[here]

    grid1.step(coeffs1, f1, h, 0.0, None, residual1)

    place = lax.rem(2 * iz + core, 8)
    x2, y2 = bx // 4, geo["by"] // 2
    row, column = rows_of((LANES, LANES)), lanes_of((LANES, LANES))
    pick = (row == HALF * core + 4 * lax.rem(column, 16)).astype(jnp.float32)
    slot = lanes_of((y2, LANES)) // 16
    for f, source in enumerate((h, k1)):
        boxes = []
        restrict(source, lambda i, v, boxes=boxes: boxes.append(v), half_y1, x2, 1 + REACH_X // 2, geo["oy"] // 2, 2 * y2, 2)
        stacked = jnp.concatenate(boxes, axis=0)
        picked = jnp.dot(stacked, pick, precision=lax.Precision.HIGHEST, preferred_element_type=jnp.float32)
        packed = jnp.zeros((y2, LANES), jnp.float32)
        for p in range(x2):
            packed = jnp.where(slot == lax.rem(p + place, 8), picked[p * y2:(p + 1) * y2], packed)
        for j in range(packed_out.shape[0]):
            packed_out[j, f] = packed
    copies += fetch(((packed_out, packed_any),), sems, 14)
    for copy in copies:
        copy.wait()


def up_kernel(geo, *refs):
    refs = list(refs)

    def take(count):
        taken = refs[:count]
        del refs[:count]
        return taken

    any_gathered, any_even, any_odd = take(3)
    views = passed_views(geo, take(1)[0])
    in0, in1 = views[:6], views[6:]
    send_u, send_r, keep_u, keep_r = take(4)
    k2, cx2, cy2, cz2, iv2, ds2, g02, g2, da2, db2, w2, e2 = take(12)
    k3, cx3, cy3, cz3, iv3, ds3, g03, g3, da3, db3, w3, e3 = take(12)
    k4, cx4, cy4, cz4, iv4, g04, g4, da4, db4, e4 = take(10)
    cx1, cy1, cz1, iv1, g01, w1, u1, g1, da1, db1, e1 = take(11)
    cx0, cy0, cz0, iv0, g00, w0, u0, g0, da0, db0 = take(10)
    e2_wide, gathered, from_even, from_odd, sems = take(5)
    core = core_of()
    ix, nx = lax.axis_index("gx"), lax.axis_size("gx")
    iz, nz = lax.axis_index("gz"), lax.axis_size("gz")
    yp = lax.axis_index("gy") // 2
    bx, by, yw = geo["bx"], geo["by"], geo["yw"]
    x2, y2, z2 = geo["x2"], geo["y2"], geo["z2"]
    wide0, wide1 = bx + 2 * WIN0, bx // 2 + 2 * WIN1

    arrivals = fetch(((any_gathered, gathered), (any_even, from_even), (any_odd, from_odd)), sems, 12)
    copies = []
    for sources, targets, wide in ((in1, (cx1, cy1, cz1, iv1, g01, w1), wide1), (in0, (cx0, cy0, cz0, iv0, g00, w0), wide0)):
        for i, (source, target) in enumerate(zip(sources, targets)):
            there = target.at[pl.ds(0, wide + 1)] if i == 0 else target.at[pl.ds(1, wide)]
            copy = pltpu.make_async_copy(source, there, sems.at[len(copies)])
            copy.start()
            copies.append(copy)

    zero_pads(k2, da2, db2, e2, k3, da3, db3, e3, k4, da4, db4, e4, u1, da1, db1, u0, da0, db0)

    for copy in arrivals:
        copy.wait()
    if geo["packed"]:
        slot = lanes_of((y2, LANES)) // 16
        for gx in range(nx):
            for f, target in ((0, g02), (1, k2)):
                for p in range(8):
                    merged = jnp.zeros((y2, LANES), jnp.float32)
                    for gz in range(nz):
                        for cc in range(2):
                            here = gathered[(2 * gx + cc) * nz + gz, f]
                            merged = jnp.where(slot == (p + 2 * gz + cc) % 8, here, merged)
                    target[1 + 8 * gx + p] = pltpu.roll(merged, (LANES - 16 * p) % LANES, 1)
    else:
        g02[pl.ds(1, x2)] = gathered[0]
        k2[pl.ds(1, x2)] = gathered[1]

    def descend(grid, level, k, cx, cy, cz, iv, ds, g0, first_target):
        def first(at, here, inverse):
            scaled = 4.0**level * (g0[here] * inverse)
            g0[here] = scaled
            first_target[here] = FACTORS[0][1] * scaled

        grid.setup(k, cx, cy, cz, iv, ds, 0.25**level, first)

    def pre(grid, level, k, cx, cy, cz, iv, ds, g0, g, da, db, w):
        descend(grid, level, k, cx, cy, cz, iv, ds, g0, da)
        coeffs = (cx, cy, cz, iv)

        def second(here, v, value, direction):
            g[here] = value
            db[here] = direction

        grid.step(coeffs, da, g0, *FACTORS[1], second)

        def third(here, v, value, direction):
            g[here] = value
            w[here] = da[here] + v + direction
            da[here] = direction

        grid.step(coeffs, db, g, *FACTORS[2], third)

        def residual(here, v, value, direction):
            g[here] = value * ds[here]

        grid.step(coeffs, da, g, 0.0, None, residual)

    def post(grid, coeffs, g0, u, g, da, db, result):
        def one(here, v, value, direction):
            g[here] = value
            da[here] = direction

        grid.step(coeffs, u, g0, *FACTORS[0], one)

        def two(here, v, value, direction):
            g[here] = value
            db[here] = direction

        grid.step(coeffs, da, g, *FACTORS[1], two)

        def three(here, v, value, direction):
            g[here] = value
            result[here] = u[here] + da[here] + v + direction
            da[here] = direction

        grid.step(coeffs, db, g, *FACTORS[2], three)

    def restrict(fine, coarse, count, shift):
        for i in range(count):
            v = fine[1 + 2 * i] + fine[2 + 2 * i]
            coarse[1 + i] = 0.125 * pair_z(pair_y(v, shift, y2), shift, z2)

    def prolong(coarse, w, target, count, shift):
        for i in range(count):
            middle = 0.75 * coarse[1 + i]
            for j, side in ((0, coarse[i]), (1, coarse[2 + i])):
                v = spread_y(middle + 0.25 * side, shift, y2)
                target[1 + 2 * i + j] = w[1 + 2 * i + j] + spread_z(v, shift, z2, True)

    def size_of(x):
        planes = max(1, 32 // ((y2 // 8) * (z2 // LANES)))
        return min(x, planes)

    x3, x4 = x2 // 2, x2 // 4
    grid2 = Grid(x2, y2, z2, 1, 1, True, size_of(x2))
    grid3 = Grid(x3, y2, z2, 2, 2, True, size_of(x3))
    grid4 = Grid(x4, y2, z2, 4, 4, True, size_of(x4))
    pre(grid2, 2, k2, cx2, cy2, cz2, iv2, ds2, g02, g2, da2, db2, w2)
    restrict(k2, k3, x3, 1)
    restrict(g2, g03, x3, 1)
    pre(grid3, 3, k3, cx3, cy3, cz3, iv3, ds3, g03, g3, da3, db3, w3)
    restrict(k3, k4, x4, 2)
    restrict(g3, g04, x4, 2)
    descend(grid4, 4, k4, cx4, cy4, cz4, iv4, None, g04, da4)
    e4[pl.ds(1, x4)] = da4[pl.ds(1, x4)]
    for sweep in range(1, COARSE_STEPS):
        src, dst = (da4, db4) if sweep % 2 else (db4, da4)

        def coarse(here, v, value, direction):
            g4[here] = value
            dst[here] = direction
            e4[here] = e4[here] + direction

        grid4.step((cx4, cy4, cz4, iv4), src, g04 if sweep == 1 else g4, *COARSE_FACTORS[sweep], coarse)
    prolong(e4, w3, e3, x4, 2)
    post(grid3, (cx3, cy3, cz3, iv3), g03, e3, g3, da3, db3, w3)
    e3[pl.ds(1, x3)] = w3[pl.ds(1, x3)]
    prolong(e3, w2, e2, x3, 1)
    post(grid2, (cx2, cy2, cz2, iv2), g02, e2, g2, da2, db2, w2)

    pad_y = geo["pad_y"]
    if pad_y:
        e2_wide[...] = jnp.zeros(e2_wide.shape, jnp.float32)
    else:
        edge = jnp.zeros((4,) + e2_wide.shape[1:], jnp.float32)
        e2_wide[pl.ds(0, 4)] = edge
        e2_wide[pl.ds(x2 + 4, 4)] = edge
    e2_wide[pl.ds(4, x2), pl.ds(pad_y, y2)] = w2[pl.ds(1, x2)]
    x2w, y2w = bx // 4 + 8, yw // 4
    cells, lane = rows_of((z2, LANES)), lanes_of((z2, LANES))
    shifted = jnp.where(core == 0, jnp.where(lane >= 104, -32, 0), jnp.where(lane < 24, 32, 0))
    pick = (cells == 32 * iz + lane // 4 + shifted).astype(jnp.float32)
    start = (bx // 4) * ix
    rows = pl.ds(pl.multiple_of(8 * yp, 8), y2w) if pad_y else pl.ds(0, y2w)
    window = e2_wide[pl.ds(start, x2w), rows].reshape(x2w * y2w, z2)
    window = jnp.dot(window, pick, precision=lax.Precision.HIGHEST, preferred_element_type=jnp.float32)
    window = window.reshape(x2w, y2w, LANES)

    def place_rows(target, plane, v, count):
        row = rows_of(v.shape)
        low = jnp.where(row >= 1, pltpu.roll(v, 1, 0), 0.0)
        high = jnp.where(row < count - 1, pltpu.roll(v, count - 1, 0), 0.0)
        target[plane, pl.ds(0, count, stride=2)] = 0.75 * v + 0.25 * low
        target[plane, pl.ds(1, count, stride=2)] = 0.75 * v + 0.25 * high

    for copy in copies[:6]:
        copy.wait()
    even, last1 = lax.rem(ix, 2) == 0, 1 + WIN1 + bx // 2
    for target, low, high, at, count in ((w1, 1, last1 + 1, 0, 5), (g01, 2, last1 + 3, 5, 2)):
        e, o = from_even[pl.ds(at, count)], from_odd[pl.ds(at, count)]
        low, high = pl.ds(low, count), pl.ds(high, count)
        target[low] = jnp.where(ix > 0, jnp.where(even, o, e), target[low])
        target[high] = jnp.where(ix < nx - 1, jnp.where(even, e, o), target[high])
    for plane in range(wide1):
        j = plane // 2
        v = 0.75 * window[j + 1] + 0.25 * window[j + 2 if plane % 2 else j]
        place_rows(u1, 1 + plane, spread_z(v, 2, LANES, False), y2w)
    grid1 = Grid(wide1, yw // 2, LANES, 1, 2, False, geo["chunk1"])

    def start1(at):
        here = pl.ds(at, grid1.size)
        u1[here] = jnp.where(iv1[here] > 0.0, w1[here] + u1[here], 0.0)

    chunks(wide1, start1, grid1.size)
    post(grid1, (cx1, cy1, cz1, iv1), g01, u1, g1, da1, db1, e1)

    for copy in copies[6:]:
        copy.wait()
    grid0 = Grid(wide0, yw, LANES, 1, 1, False, 8)

    def fill(i, carry):
        at = WIN1 + 1 - WIN0 // 2 + i
        middle = 0.75 * e1[at]
        for j, side in ((0, e1[at - 1]), (1, e1[at + 1])):
            place_rows(u0, 1 + 2 * i + j, spread_z(middle + 0.25 * side, 1, LANES, False), yw // 2)
        return carry

    lax.fori_loop(0, wide0 // 2, fill, 0, unroll=4)

    def start0(at):
        here = pl.ds(at, grid0.size)
        u0[here] = jnp.where(iv0[here] > 0.0, w0[here] + u0[here], 0.0)

    chunks(wide0, start0, grid0.size)
    coeffs0 = (cx0, cy0, cz0, iv0)
    post(grid0, coeffs0, g00, u0, g0, da0, db0, w0)

    def residual(here, v, value, direction):
        g0[here] = value / iv0[here]

    grid0.step(coeffs0, da0, g0, 0.0, None, residual, 1 + WIN0, bx)
    own = pl.ds(1 + WIN0, bx)
    own_rows = pl.ds(pl.multiple_of(geo["oy"] + core * by, 8), by)
    sib_rows = pl.ds(pl.multiple_of(geo["oy"] + (1 - core) * by, 8), by)
    leaving = fetch(((w0.at[own, sib_rows], send_u), (g0.at[own, sib_rows], send_r),
                     (w0.at[own, own_rows], keep_u), (g0.at[own, own_rows], keep_r)), sems, 15)
    for copy in leaving:
        copy.wait()


def array(*shape):
    return jax.ShapeDtypeStruct(shape, jnp.float32)


def on_device(right_side, conductivity):
    bx, by, bz = right_side.shape
    nx, ny, nz = (lax.axis_size(axis) for axis in AXES)
    pairs = ny // 2
    ix, iy, iz = (lax.axis_index(axis) for axis in AXES)
    core = iy % 2

    def index(x, p, c, z):
        return ((x % nx) * ny + (p % pairs) * 2 + c) * nz + z % nz

    every = [(x, p, z) for x in range(nx) for p in range(pairs) for z in range(nz)]

    def sibling(v):
        return lax.ppermute(v, "gy", [(i, i ^ 1) for i in range(ny)])

    def xor(v, axis, k):
        return lax.ppermute(v, axis, [(i, i ^ k) for i in range(lax.axis_size(axis))])

    def paired(v, first):
        perm = [(i, i) for i in range(nx)]
        for i in range(first, nx - 1, 2):
            perm[i], perm[i + 1] = (i, i + 1), (i + 1, i)
        return lax.ppermute(v, "gx", perm)

    def facing(v):
        perm = {}
        for x, p, z in every:
            if z > 0:
                a, b = index(x, p, 0, z), index(x, p, 1, z - 1)
                perm[a], perm[b] = b, a
        return lax.ppermute(v, AXES, [(i, perm.get(i, i)) for i in range(nx * ny * nz)])

    own_b, own_k, ye = right_side, conductivity, by
    if ny > 2:
        near = []
        far = []
        for p in range(pairs):
            near += [(2 * p, 2 * ((p - 1) % pairs) + 1), (2 * ((p - 1) % pairs) + 1, 2 * p)]
            far += [(2 * p, 2 * ((p + 1) % pairs)), (2 * p + 1, 2 * ((p - 1) % pairs) + 1)]
        there = jnp.where(core == 0, iy > 0, iy < ny - 1)

        def widened(v):
            one = jnp.where(there, lax.ppermute(v, "gy", near), 0.0)
            two = jnp.where(there, lax.ppermute(v, "gy", far), 0.0)
            return jnp.where(core == 0, jnp.concatenate([two, one, v], 1), jnp.concatenate([v, one, two], 1))

        own_b, own_k = widened(own_b), widened(own_k)
        ye = 3 * by
    yw = 2 * ye
    xw = bx + 2 * REACH_X
    geo = dict(
        bx=bx, by=by, ye=ye, yw=yw, xw=xw, oy=(yw - 2 * by) // 2, chunk1=14 if yw == 32 else 4,
        packed=pairs == 1 and 32 * nz == LANES, x2=bx // 4 * nx, y2=by // 4 * ny, z2=bz // 4 * nz,
        pad_y=(yw // 4 - by // 2) // 2,
    )

    own = lax.optimization_barrier(jnp.concatenate([own_b, own_k], 0))
    even = ix % 2 == 0
    high = jnp.concatenate([own[bx - REACH_XB:bx], own[2 * bx - REACH_X:]], 0)
    low = jnp.concatenate([own[:REACH_XB], own[bx:bx + REACH_X]], 0)
    even_own = paired(jnp.where(even, high, low), 0)
    odd_own = paired(jnp.where(even, low, high), 1)
    sib = sibling(own)
    anywhere, hbm = pl.BlockSpec(memory_space=pl.ANY), pl.BlockSpec(memory_space=pltpu.HBM)

    def call(name, kernel, ins, outs, scratch, hbm_ins=0, hbm_outs=0, limit=0):
        held = sum(4 * math.prod(v.shape) for v in scratch if v.dtype == jnp.float32)
        return pl.pallas_call(
            kernel, out_shape=outs, in_specs=[anywhere] * (len(ins) - hbm_ins) + [hbm] * hbm_ins,
            out_specs=[anywhere] * (len(outs) - hbm_outs) + [hbm] * hbm_outs,
            scratch_shapes=scratch, name=name,
            compiler_params=pltpu.CompilerParams(vmem_limit_bytes=max(limit, held + 6 * 1024 * 1024)),
        )(*ins)

    def vmem(shape):
        return pltpu.VMEM(shape, jnp.float32)

    def pack(name, lists, ins, later=()):
        shape = (len(lists) // SLOTS, yw, LANES)
        return pl.pallas_call(
            functools.partial(pack_kernel, geo, lists, len(ins)),
            out_shape=array(*shape), in_specs=[anywhere] * (len(ins) + len(later)),
            scratch_shapes=[vmem(v.shape) for v in ins] + [pltpu.SemaphoreType.DMA((len(ins),))],
            compiler_params=pltpu.CompilerParams(vmem_limit_bytes=8 * 1024 * 1024 * max(1, yw // 32)), name=name,
            cost_estimate=pl.CostEstimate(flops=4_000_000, bytes_accessed=8_000_000, transcendentals=0),
        )(*ins, *later)

    z_send = pack("pack_box", [p and (0, p[0] * bx + p[1]) for p in strip_planes(bx)], (own, sib))
    z_in = facing(z_send)
    even_own, odd_own, z_send = lax.optimization_barrier((even_own, odd_own, z_send))
    even_sib, odd_sib = sibling(even_own), sibling(odd_own)
    slab = [(0, p) for p in range(REACH_X + REACH_XB)]
    slab += [None] * (SLAB * SLOTS - len(slab))
    slabs = slab + [p and (1, p[1]) for p in slab]
    zx_in = facing(pack("pack_halo", slabs, (even_own, odd_own, even_sib, odd_sib), (z_in,)))

    wide0, wide1 = bx + 2 * WIN0, bx // 2 + 2 * WIN1
    x1, y1 = xw // 2, yw // 2
    some0 = vmem((xw + 2, yw, LANES))
    some1 = vmem((x1 + 2, y1, LANES))
    passed = array(6 * (wide0 + 1) + 3 * (wide1 + 1), yw, LANES)
    edge = 7
    ins = (own, sib, even_own, odd_own, even_sib, odd_sib, z_in, zx_in)
    sends = [array(nx * ny * nz if geo["packed"] else 1, 2, by // 2, LANES), array(edge, y1, LANES), array(edge, y1, LANES)]
    down = call(
        "down", functools.partial(down_kernel, geo), ins, sends + [passed],
        [vmem(v.shape) for v in ins] + [vmem(v.shape) for v in sends] + [some0] * 10 + [some1] * 11
        + [vmem((6, yw, LANES)), vmem((6, y1, LANES)), pltpu.SemaphoreType.DMA((15,)), pltpu.SemaphoreType.DMA((8,))],
        hbm_outs=1, limit=VMEM_LIMIT,
    )
    packed, even_send, odd_send, passed = down[0], down[1], down[2], down[3]
    from_even, from_odd = paired(even_send, 0), paired(odd_send, 1)

    if geo["packed"]:
        gathered = lax.all_to_all(packed, AXES, 0, 0, tiled=True)
    else:
        pieces = lax.all_gather(packed, AXES).reshape(nx, pairs, 2, nz, 2, by // 2, 8, 16)
        order = (jnp.arange(8) + 2 * jnp.arange(nz)[:, None, None] + jnp.arange(2)[:, None]) % 8
        order = jnp.transpose(order, (1, 0, 2))[None, None, :, :, None, None, :, None]
        pieces = jnp.take_along_axis(pieces, order, axis=6)
        gathered = jnp.transpose(pieces, (4, 0, 6, 1, 5, 3, 2, 7)).reshape(2, geo["x2"], geo["y2"], geo["z2"])

    def level(planes, rows, lanes):
        return vmem((planes + 2, rows, lanes))

    x2, y2, z2 = geo["x2"], geo["y2"], geo["z2"]
    send_u, send_r, keep_u, keep_r = call(
        "up", functools.partial(up_kernel, geo), (gathered, from_even, from_odd, passed), [array(bx, by, LANES)] * 4,
        [level(x2, y2, z2)] * 12 + [level(x2 // 2, y2, z2)] * 12 + [level(x2 // 4, y2, z2)] * 10
        + [level(wide1, y1, LANES)] * 11 + [level(wide0, yw, LANES)] * 10
        + [vmem((x2 + 8, y2 + 2 * geo["pad_y"], z2)), vmem(gathered.shape), vmem(from_even.shape), vmem(from_odd.shape)]
        + [pltpu.SemaphoreType.DMA((19,))],
        hbm_ins=1, limit=VMEM_LIMIT,
    )
    mine = lanes_of((1, 1, LANES)) // HALF == core
    return jnp.where(mine, keep_u, sibling(send_u)), jnp.where(mine, keep_r, sibling(send_r))


def solution(mesh):
    specs = (P(*AXES), P(*AXES))
    return jax.shard_map(on_device, mesh=mesh, in_specs=specs, out_specs=specs, check_vma=False)
```

```python
import functools
import math
import jax
import jax.numpy as jnp
from jax import lax
from jax.experimental import pallas as pl
from jax.experimental.pallas import tpu as pltpu
from jax.sharding import PartitionSpec as P

LEVELS = 4
STEPS = 3
COARSE_STEPS = 8
LOWER_EDGE = 0.3
UPPER_EDGE = 2.0

LANES = 128
HALF = 64
REACH_X = 12
REACH_XB = 9
REACH_Z = 20
WIN0 = 4
WIN1 = REACH_X // 2
VMEM_LIMIT = 48 * 1024 * 1024
AXES = ("gx", "gy", "gz")


def chebyshev_factors(sweeps):
    centre_value = 0.5 * (UPPER_EDGE + LOWER_EDGE)
    half_width = 0.5 * (UPPER_EDGE - LOWER_EDGE)
    ratio_value = centre_value / half_width
    damping = 1.0 / ratio_value
    factors = [(0.0, 1.0 / centre_value)]
    for _ in range(1, sweeps):
        damping_next = 1.0 / (2.0 * ratio_value - damping)
        factors.append((damping_next * damping, 2.0 * damping_next / half_width))
        damping = damping_next
    return factors


FACTORS = chebyshev_factors(STEPS)
COARSE_FACTORS = chebyshev_factors(COARSE_STEPS)


def chunks(count, body, size, first=1):
    if count == size:
        body(first)
    else:
        def step(i, carry):
            body(first + i * size)
            return carry
        lax.fori_loop(0, count // size, step, 0)


def rows_of(shape):
    return lax.broadcasted_iota(jnp.int32, shape, len(shape) - 2)


def lanes_of(shape):
    return lax.broadcasted_iota(jnp.int32, shape, len(shape) - 1)


class Grid:
    def __init__(self, x, y, z, sy, sz, whole_z, size):
        self.x, self.y, self.z, self.sy, self.sz = x, y, z, sy, sz
        self.whole_z, self.size = whole_z, size

    def up_y(self, v):
        return pltpu.roll(v, self.y - self.sy, v.ndim - 2)

    def down_y(self, v):
        return pltpu.roll(v, self.sy, v.ndim - 2)

    def up_z(self, v):
        return pltpu.roll(v, self.z - self.sz, v.ndim - 1)

    def down_z(self, v):
        return pltpu.roll(v, self.sz, v.ndim - 1)

    def setup(self, k_ref, cx, cy, cz, iv, ds, scale, after=None):
        cx[0] = 0.5 * (k_ref[0] + k_ref[1])

        def body(at):
            here = pl.ds(at, self.size)
            k = k_ref[here]
            row, lane = rows_of(k.shape), lanes_of(k.shape)
            k_next = k_ref[pl.ds(at + 1, self.size)]
            k_prev = k_ref[pl.ds(at - 1, self.size)]
            not_last = row < self.y - self.sy
            k_up = jnp.where(not_last, self.up_y(k), 0.0)
            k_down = jnp.where(row >= self.sy, self.down_y(k), 0.0)
            z_up, z_down = self.up_z(k), self.down_z(k)
            if self.whole_z:
                inner = lane < self.z - self.sz
                z_up = jnp.where(inner, z_up, 0.0)
                z_down = jnp.where(lane >= self.sz, z_down, 0.0)
            total = 3.0 * k + 0.5 * ((k_next + k_prev) + (k_up + k_down) + (z_up + z_down))
            inverse = jnp.where(k > 0.0, 1.0 / total, 0.0)
            cx[here] = 0.5 * (k + k_next)
            cy[here] = jnp.where(not_last, 0.5 * (k + k_up), 0.0)
            across = 0.5 * (k + z_up)
            cz[here] = jnp.where(inner, across, 0.0) if self.whole_z else across
            iv[here] = inverse
            if ds is not None:
                ds[here] = scale * total
            if after is not None:
                after(at, here, inverse)

        chunks(self.x, body, self.size)

    def step(self, coeffs, src, g_in, keep, push, out, first=1, count=None):
        cx, cy, cz, iv = coeffs

        def body(at):
            here = pl.ds(at, self.size)
            planes, x_coeff = src[pl.ds(at - 1, self.size + 2)], cx[pl.ds(at - 1, self.size + 1)]
            v = planes[1:-1]
            y_coeff, z_coeff = cy[here], cz[here]
            near = x_coeff[1:] * planes[2:] + x_coeff[:-1] * planes[:-2]
            near = near + (y_coeff * self.up_y(v) + self.down_y(y_coeff * v))
            near = near + (z_coeff * self.up_z(v) + self.down_z(z_coeff * v))
            g = g_in[here] - v + iv[here] * near
            out(here, v, g, None if push is None else (keep * v + push * g if keep else push * g))

        chunks(count or self.x, body, self.size, first)


def pair_z(v, shift, lanes):
    even = (lanes_of(v.shape) // shift) % 2 == 0
    return v + jnp.where(even, pltpu.roll(v, lanes - shift, v.ndim - 1), pltpu.roll(v, shift, v.ndim - 1))


def pair_y(v, shift, rows):
    even = (rows_of(v.shape) // shift) % 2 == 0
    return v + jnp.where(even, pltpu.roll(v, rows - shift, v.ndim - 2), pltpu.roll(v, shift, v.ndim - 2))


def spread_z(v, shift, lanes, whole):
    lane = lanes_of(v.shape)
    even = (lane // shift) % 2 == 0
    low, high = pltpu.roll(v, shift, v.ndim - 1), pltpu.roll(v, lanes - shift, v.ndim - 1)
    if whole:
        low = jnp.where(lane >= shift, low, 0.0)
        high = jnp.where(lane < lanes - shift, high, 0.0)
    return 0.75 * v + 0.25 * jnp.where(even, low, high)


def spread_y(v, shift, rows):
    row = rows_of(v.shape)
    even = (row // shift) % 2 == 0
    low = jnp.where(row >= shift, pltpu.roll(v, shift, v.ndim - 2), 0.0)
    high = jnp.where(row < rows - shift, pltpu.roll(v, rows - shift, v.ndim - 2), 0.0)
    return 0.75 * v + 0.25 * jnp.where(even, low, high)


def picked_lanes(v, pick):
    pick, total = pick.astype(jnp.bfloat16), None
    for _ in range(3):
        part = v.astype(jnp.bfloat16)
        v = v - part.astype(jnp.float32)
        product = jnp.dot(part, pick, preferred_element_type=jnp.float32)
        total = product if total is None else total + product
    return total


def zero_pads(*refs):
    for ref in refs:
        ref[0] = jnp.zeros(ref.shape[1:], jnp.float32)
        ref[ref.shape[0] - 1] = jnp.zeros(ref.shape[1:], jnp.float32)


def core_of():
    return lax.rem(lax.axis_index("gy"), 2)


def reaches():
    source1 = {0: WIN1 + 2, 1: WIN1 + 1, 2: WIN1, 3: 0}
    coeff1 = {a: max(source1.get(a, -1) + 1, source1.get(a - 1, -1), source1.get(a + 1, -1), min(WIN1, 7 - a)) for a in range(7)}
    residual0 = {0: 2 * source1[0]}
    coeff0 = {0: 2 * coeff1[0]}
    for a in range(1, 7):
        for x in (2 * a - 1, 2 * a):
            coeff0[x] = 2 * coeff1[a]
            if a in source1:
                residual0[x] = 2 * source1[a]

    def grown(steps, x):
        return max([z + steps - abs(x - at) for at, z in residual0.items() if abs(x - at) <= steps], default=0)

    source = [grown(3, x) for x in range(REACH_XB + 1)]
    coeff = [max(grown(4, x), coeff0[x]) for x in range(REACH_X + 1)]
    assert max(source + coeff) <= REACH_Z
    return source, coeff


def slots_of(items):
    rows, used = [], LANES
    for item, width in items:
        if width:
            if used + width > LANES:
                rows.append([])
                used = 0
            rows[-1].append((item, used, width))
            used += width
    return rows


def box_slots(bx):
    source, coeff = reaches()
    return slots_of([((0, p), source[0]) for p in range(bx)] + [((1, p), coeff[0]) for p in range(bx)])


def halo_slots():
    source, coeff = reaches()
    items = []
    for pair in range(2):
        items += [((pair, 0, x), source[x]) for x in range(1, REACH_XB + 1)]
        items += [((pair, 1, x), coeff[x]) for x in range(1, REACH_X + 1)]
    return slots_of(items)


def pack_kernel(geo, slots, plane_of, count, *refs):
    own, sib, z_out = refs[:count // 2], refs[count // 2:count], refs[-1]
    core, ye = core_of(), geo["ye"]
    lane = lanes_of((ye, LANES))
    for fields, half in ((own, core), (sib, 1 - core)):
        rows = pl.ds(pl.multiple_of(half * ye, 8), ye)
        for m, row in enumerate(slots):
            packed = jnp.zeros((ye, LANES), jnp.float32)
            for item, at, width in row:
                shift = jnp.where(core == 1, (at + width) % LANES, at)
                field, plane = plane_of(item)
                packed = jnp.where((lane >= at) & (lane < at + width), pltpu.roll(fields[field][plane], shift, 1), packed)
            z_out[m, rows] = packed


def passed_views(geo, ref):
    wide0, wide1, rows = geo["bx"] + 2 * WIN0, geo["bx"] // 2 + 2 * WIN1, geo["yw"] // 2
    views, at = [], 0
    for i in range(6):
        views.append(ref.at[pl.ds(at, wide0 + (i == 0))])
        at += wide0 + 1
    for i in range(6):
        views.append(ref.at[pl.ds(at + i // 2 * (wide1 + 1), wide1 + (i == 0)), pl.ds(i % 2 * rows, rows)])
    return views


def down_kernel(geo, *refs):
    (own_in, sib_in, even_own, odd_own, even_sib, odd_sib, z_in, zx_in, packed_any, even_any, odd_any, passed,
     packed_out, even_out, odd_out,
     k0, cx, cy, cz, iv, ds, g0, g, d1, d2,
     k1, ex, ey, ez, ei, es, h0, h, f1, f2, u1, half_y, half_y1, sems) = refs
    core = core_of()
    ix, nx = lax.axis_index("gx"), lax.axis_size("gx")
    iz, nz = lax.axis_index("gz"), lax.axis_size("gz")
    bx, ye, yw, xw = geo["bx"], geo["ye"], geo["yw"], geo["xw"]
    z_there = jnp.where(core == 0, iz > 0, iz < nz - 1)
    lo_there, hi_there = ix > 0, ix < nx - 1
    even = lax.rem(ix, 2) == 0

    lane = lanes_of((yw, LANES))

    def strip(ref, m, at, width):
        shift = jnp.where(core == 0, (2 * LANES - width - at) % LANES, (LANES - at) % LANES)
        return pltpu.roll(ref[m], shift, 1)

    def merge(window, at, width, there, moved):
        halo = jnp.where(core == 0, lane - (LANES - width), width - 1 - lane) >= 0
        window[at] = jnp.where(halo, jnp.where(there, moved, 0.0), window[at])

    own_rows = pl.ds(pl.multiple_of(core * ye, 8), ye)
    sib_rows = pl.ds(pl.multiple_of((1 - core) * ye, 8), ye)
    zero_pads(k0, d1, d2, k1, f1, f2)
    windows = ((g0, 0, REACH_XB, 0), (k0, bx, REACH_X, REACH_XB))
    for p in range(REACH_X - REACH_XB):
        g0[1 + p] = jnp.zeros((yw, LANES), jnp.float32)
        g0[xw - p] = jnp.zeros((yw, LANES), jnp.float32)

    def halos(from_even, from_odd, rows):
        for window, _, width, at in windows:
            e, o = from_even[pl.ds(at, width)], from_odd[pl.ds(at, width)]
            window[pl.ds(1 + REACH_X - width, width), rows] = jnp.where(lo_there, jnp.where(even, o, e), 0.0)
            window[pl.ds(1 + REACH_X + bx, width), rows] = jnp.where(hi_there, jnp.where(even, e, o), 0.0)

    for window, at, _, _ in windows:
        window[pl.ds(1 + REACH_X, bx), own_rows] = own_in[pl.ds(at, bx)]
        window[pl.ds(1 + REACH_X, bx), sib_rows] = sib_in[pl.ds(at, bx)]
    halos(even_own, odd_own, own_rows)
    halos(even_sib, odd_sib, sib_rows)
    for m, row in enumerate(box_slots(bx)):
        for (f, p), at, width in row:
            merge(windows[f][0], 1 + REACH_X + p, width, z_there, strip(z_in, m, at, width))
    places = {item: (m, at, width) for m, row in enumerate(halo_slots()) for item, at, width in row}
    for (pair, f, x), place in places.items():
        if pair == 0:
            window, width = windows[f][0], place[2]
            e, o = strip(zx_in, *place), strip(zx_in, *places[1, f, x])
            merge(window, 1 + REACH_X - x, width, z_there & lo_there, jnp.where(even, o, e))
            merge(window, REACH_X + bx + x, width, z_there & hi_there, jnp.where(even, e, o))

    grid = Grid(xw, yw, LANES, 1, 1, False, geo["chunk0"])
    inner = Grid(xw - 8, yw, LANES, 1, 1, False, geo["chunk0_inner"])
    nothing = jnp.zeros((4, yw, LANES), jnp.float32)
    for ref in (g, d2):
        ref[pl.ds(1, 4)] = nothing
        ref[pl.ds(xw - 3, 4)] = nothing

    def first(at, here, inverse):
        scaled = g0[here] * inverse
        g0[here] = scaled
        d1[here] = FACTORS[0][1] * scaled

    grid.setup(k0, cx, cy, cz, iv, ds, 1.0, first)
    own0 = 1 + REACH_X - WIN0
    wide0 = bx + 2 * WIN0
    copies = []

    views = passed_views(geo, passed)

    def send(source, start, count):
        i = len(copies)
        copy = pltpu.make_async_copy(source.at[pl.ds(start, count)], views[i], sems.at[i])
        copy.start()
        copies.append(copy)

    send(cx, own0 - 1, wide0 + 1)
    send(cy, own0, wide0)
    send(cz, own0, wide0)
    send(iv, own0, wide0)
    send(g0, own0, wide0)

    def restrict(source, target, tmp, x_count, at, y_first, y_rows, shift):
        for i in range(x_count):
            j = i % tmp.shape[0]
            tmp[j] = source[at + 2 * i] + source[at + 2 * i + 1]
            v = tmp[j, pl.ds(y_first, y_rows // 2, stride=2)] + tmp[j, pl.ds(y_first + 1, y_rows // 2, stride=2)]
            target(i, 0.125 * pair_z(v, shift, LANES))

    x1, y1 = xw // 2, yw // 2

    def put_k1(i, v):
        k1[1 + i] = v

    def put_b1(i, v):
        h0[1 + i] = v

    restrict(k0, put_k1, half_y, x1, 1, 0, yw, 1)
    coeffs = (cx, cy, cz, iv)

    def second(here, v, value, direction):
        g[here] = value
        d2[here] = direction

    inner.step(coeffs, d1, g0, *FACTORS[1], second, 5)

    def third(here, v, value, direction):
        g[here] = value
        k0[here] = d1[here] + v + direction
        d1[here] = direction

    inner.step(coeffs, d2, g, *FACTORS[2], third, 5)
    send(k0, own0, wide0)

    def residual(here, v, value, direction):
        g[here] = value * ds[here]

    inner.step(coeffs, d1, g, 0.0, None, residual, 5)

    restrict(g, put_b1, half_y, x1, 1, 0, yw, 1)
    grid1 = Grid(x1, y1, LANES, 1, 2, False, geo["chunk1"])

    def first1(at, here, inverse):
        scaled = 4.0 * (h0[here] * inverse)
        h0[here] = scaled
        f1[here] = FACTORS[0][1] * scaled

    grid1.setup(k1, ex, ey, ez, ei, es, 0.25, first1)
    own1 = 1 + REACH_X // 2 - WIN1
    wide1 = bx // 2 + 2 * WIN1
    send(ex, own1 - 1, wide1 + 1)
    send(ey, own1, wide1)
    send(ez, own1, wide1)
    send(ei, own1, wide1)
    send(h0, own1, wide1)
    coeffs1 = (ex, ey, ez, ei)

    def second1(here, v, value, direction):
        h[here] = value
        f2[here] = direction

    grid1.step(coeffs1, f1, h0, *FACTORS[1], second1)

    def third1(here, v, value, direction):
        h[here] = value
        u1[here] = f1[here] + v + direction
        f1[here] = direction

    grid1.step(coeffs1, f2, h, *FACTORS[2], third1)
    send(u1, own1, wide1)
    mine = 1 + REACH_X // 2
    last = mine + bx // 2
    for source, low, high, at, count in ((u1, mine, last - WIN1, 0, 6), (h0, mine + 2, last - 5, 6, 3)):
        low, high = source[pl.ds(low, count)], source[pl.ds(high, count)]
        even_out[pl.ds(at, count)] = jnp.where(even, high, low)
        odd_out[pl.ds(at, count)] = jnp.where(even, low, high)

    def leave(source, target):
        copy = pltpu.make_async_copy(source, target, sems.at[len(copies)])
        copy.start()
        copies.append(copy)

    leave(even_out, even_any)
    leave(odd_out, odd_any)

    def residual1(here, v, value, direction):
        h[here] = value * es[here]

    grid1.step(coeffs1, f1, h, 0.0, None, residual1)

    place = lax.rem(2 * iz + core, 8)
    x2, y2 = bx // 4, geo["by"] // 2
    row, column = rows_of((LANES, LANES)), lanes_of((LANES, LANES))
    pick = (row == HALF * core + 4 * lax.rem(column, 16)).astype(jnp.float32)
    slot = lanes_of((y2, LANES)) // 16
    for f, source in enumerate((h, k1)):
        boxes = []
        restrict(source, lambda i, v, boxes=boxes: boxes.append(v), half_y1, x2, 1 + REACH_X // 2, geo["oy"] // 2, 2 * y2, 2)
        stacked = jnp.concatenate(boxes, axis=0)
        picked = picked_lanes(stacked, pick)
        packed = jnp.zeros((y2, LANES), jnp.float32)
        for p in range(x2):
            packed = jnp.where(slot == lax.rem(p + place, 8), picked[p * y2:(p + 1) * y2], packed)
        for j in range(packed_out.shape[0]):
            packed_out[j, f] = packed
    leave(packed_out, packed_any)
    for copy in copies:
        copy.wait()


def up_kernel(geo, *refs):
    refs = list(refs)

    def take(count):
        taken = refs[:count]
        del refs[:count]
        return taken

    arriving = take(3)
    views = passed_views(geo, take(1)[0])
    in0, in1 = views[:6], views[6:]
    send_u, send_r, keep_u, keep_r = take(4)
    k2, cx2, cy2, cz2, iv2, ds2, g02, g2, da2, db2, w2, e2 = take(12)
    k3, cx3, cy3, cz3, iv3, ds3, g03, g3, da3, db3, w3, e3 = take(12)
    k4, cx4, cy4, cz4, iv4, g04, g4, da4, db4, e4 = take(10)
    cx1, cy1, cz1, iv1, g01, w1, u1, g1, da1, db1, e1 = take(11)
    cx0, cy0, cz0, iv0, g00, w0, u0, g0, da0, db0 = take(10)
    e2_wide, gathered, from_even, from_odd, sems = take(5)
    core = core_of()
    ix, nx = lax.axis_index("gx"), lax.axis_size("gx")
    iz, nz = lax.axis_index("gz"), lax.axis_size("gz")
    yp = lax.axis_index("gy") // 2
    bx, by, yw = geo["bx"], geo["by"], geo["yw"]
    x2, y2, z2 = geo["x2"], geo["y2"], geo["z2"]
    wide0, wide1 = bx + 2 * WIN0, bx // 2 + 2 * WIN1

    arrivals = []
    for source, target in zip(arriving, (gathered, from_even, from_odd)):
        arrivals.append(pltpu.make_async_copy(source, target, sems.at[16 + len(arrivals)]))
        arrivals[-1].start()
    copies = []
    for sources, targets, wide in ((in1, (cx1, cy1, cz1, iv1, g01, w1), wide1), (in0, (cx0, cy0, cz0, iv0, g00, w0), wide0)):
        for i, (source, target) in enumerate(zip(sources, targets)):
            there = target.at[pl.ds(0, wide + 1)] if i == 0 else target.at[pl.ds(1, wide)]
            copy = pltpu.make_async_copy(source, there, sems.at[len(copies)])
            copy.start()
            copies.append(copy)

    zero_pads(k2, da2, db2, e2, k3, da3, db3, e3, k4, da4, db4, e4, u1, da1, db1, u0, da0, db0)

    for copy in arrivals:
        copy.wait()
    if geo["packed"]:
        slot = lanes_of((y2, LANES)) // 16
        for gx in range(nx):
            for f, target in ((0, g02), (1, k2)):
                for p in range(8):
                    merged = jnp.zeros((y2, LANES), jnp.float32)
                    for gz in range(nz):
                        for cc in range(2):
                            here = gathered[(2 * gx + cc) * nz + gz, f]
                            merged = jnp.where(slot == (p + 2 * gz + cc) % 8, here, merged)
                    target[1 + 8 * gx + p] = pltpu.roll(merged, (LANES - 16 * p) % LANES, 1)
    else:
        g02[pl.ds(1, x2)] = gathered[0]
        k2[pl.ds(1, x2)] = gathered[1]

    def descend(grid, level, k, cx, cy, cz, iv, ds, g0, first_target):
        def first(at, here, inverse):
            scaled = 4.0**level * (g0[here] * inverse)
            g0[here] = scaled
            first_target[here] = FACTORS[0][1] * scaled

        grid.setup(k, cx, cy, cz, iv, ds, 0.25**level, first)

    def pre(grid, level, k, cx, cy, cz, iv, ds, g0, g, da, db, w):
        descend(grid, level, k, cx, cy, cz, iv, ds, g0, da)
        coeffs = (cx, cy, cz, iv)

        def second(here, v, value, direction):
            g[here] = value
            db[here] = direction

        grid.step(coeffs, da, g0, *FACTORS[1], second)

        def third(here, v, value, direction):
            g[here] = value
            w[here] = da[here] + v + direction
            da[here] = direction

        grid.step(coeffs, db, g, *FACTORS[2], third)

        def residual(here, v, value, direction):
            g[here] = value * ds[here]

        grid.step(coeffs, da, g, 0.0, None, residual)

    def post(grid, coeffs, g0, u, g, da, db, result, shrink=0):
        def step(i, *args):
            part = Grid(grid.x - 2 * i * shrink, grid.y, grid.z, grid.sy, grid.sz, grid.whole_z, grid.size)
            if shrink:
                part.size = part.x if grid.size == grid.x else 2
            part.step(coeffs, *args, 1 + i * shrink)

        def one(here, v, value, direction):
            g[here] = value
            da[here] = direction

        step(1, u, g0, *FACTORS[0], one)

        def two(here, v, value, direction):
            g[here] = value
            db[here] = direction

        step(2, da, g, *FACTORS[1], two)

        def three(here, v, value, direction):
            g[here] = value
            result[here] = u[here] + da[here] + v + direction
            da[here] = direction

        step(3, db, g, *FACTORS[2], three)

    def restrict(fine, coarse, count, shift):
        for i in range(count):
            v = fine[1 + 2 * i] + fine[2 + 2 * i]
            coarse[1 + i] = 0.125 * pair_z(pair_y(v, shift, y2), shift, z2)

    def prolong(coarse, w, target, count, shift):
        for i in range(count):
            middle = 0.75 * coarse[1 + i]
            for j, side in ((0, coarse[i]), (1, coarse[2 + i])):
                v = spread_y(middle + 0.25 * side, shift, y2)
                target[1 + 2 * i + j] = w[1 + 2 * i + j] + spread_z(v, shift, z2, True)

    def size_of(x):
        planes = max(1, 32 // ((y2 // 8) * (z2 // LANES)))
        return min(x, planes)

    x3, x4 = x2 // 2, x2 // 4
    grid2 = Grid(x2, y2, z2, 1, 1, True, size_of(x2))
    grid3 = Grid(x3, y2, z2, 2, 2, True, size_of(x3))
    grid4 = Grid(x4, y2, z2, 4, 4, True, size_of(x4))
    pre(grid2, 2, k2, cx2, cy2, cz2, iv2, ds2, g02, g2, da2, db2, w2)
    restrict(k2, k3, x3, 1)
    restrict(g2, g03, x3, 1)
    pre(grid3, 3, k3, cx3, cy3, cz3, iv3, ds3, g03, g3, da3, db3, w3)
    restrict(k3, k4, x4, 2)
    restrict(g3, g04, x4, 2)
    descend(grid4, 4, k4, cx4, cy4, cz4, iv4, None, g04, da4)
    e4[pl.ds(1, x4)] = da4[pl.ds(1, x4)]
    for sweep in range(1, COARSE_STEPS):
        src, dst = (da4, db4) if sweep % 2 else (db4, da4)

        def coarse(here, v, value, direction):
            g4[here] = value
            dst[here] = direction
            e4[here] = e4[here] + direction

        grid4.step((cx4, cy4, cz4, iv4), src, g04 if sweep == 1 else g4, *COARSE_FACTORS[sweep], coarse)
    prolong(e4, w3, e3, x4, 2)
    post(grid3, (cx3, cy3, cz3, iv3), g03, e3, g3, da3, db3, w3)
    e3[pl.ds(1, x3)] = w3[pl.ds(1, x3)]
    prolong(e3, w2, e2, x3, 1)
    post(grid2, (cx2, cy2, cz2, iv2), g02, e2, g2, da2, db2, w2)

    pad_y = geo["pad_y"]
    if pad_y:
        e2_wide[...] = jnp.zeros(e2_wide.shape, jnp.float32)
    else:
        edge = jnp.zeros((4,) + e2_wide.shape[1:], jnp.float32)
        e2_wide[pl.ds(0, 4)] = edge
        e2_wide[pl.ds(x2 + 4, 4)] = edge
    e2_wide[pl.ds(4, x2), pl.ds(pad_y, y2)] = w2[pl.ds(1, x2)]
    x2w, y2w = bx // 4 + 8, yw // 4
    cells, lane = rows_of((z2, LANES)), lanes_of((z2, LANES))
    shifted = jnp.where(core == 0, jnp.where(lane >= 104, -32, 0), jnp.where(lane < 24, 32, 0))
    pick = (cells == 32 * iz + lane // 4 + shifted).astype(jnp.float32)
    start = (bx // 4) * ix
    rows = pl.ds(pl.multiple_of(8 * yp, 8), y2w) if pad_y else pl.ds(0, y2w)
    window = e2_wide[pl.ds(start, x2w), rows].reshape(x2w * y2w, z2)
    window = picked_lanes(window, pick)
    window = window.reshape(x2w, y2w, LANES)

    def place_rows(target, plane, v, count):
        row = rows_of(v.shape)
        low = jnp.where(row >= 1, pltpu.roll(v, 1, 0), 0.0)
        high = jnp.where(row < count - 1, pltpu.roll(v, count - 1, 0), 0.0)
        target[plane, pl.ds(0, count, stride=2)] = 0.75 * v + 0.25 * low
        target[plane, pl.ds(1, count, stride=2)] = 0.75 * v + 0.25 * high

    for copy in copies[:6]:
        copy.wait()
    even, last1 = lax.rem(ix, 2) == 0, 1 + WIN1 + bx // 2
    for target, low, high, at, count in ((w1, 1, last1, 0, 6), (g01, 2, last1 + 2, 6, 3)):
        e, o = from_even[pl.ds(at, count)], from_odd[pl.ds(at, count)]
        low, high = pl.ds(low, count), pl.ds(high, count)
        target[low] = jnp.where(ix > 0, jnp.where(even, o, e), target[low])
        target[high] = jnp.where(ix < nx - 1, jnp.where(even, e, o), target[high])
    for plane in range(wide1):
        j = plane // 2
        v = 0.75 * window[j + 1] + 0.25 * window[j + 2 if plane % 2 else j]
        place_rows(u1, 1 + plane, spread_z(v, 2, LANES, False), y2w)
    grid1 = Grid(wide1, yw // 2, LANES, 1, 2, False, geo["chunk1"])

    def start1(at):
        here = pl.ds(at, grid1.size)
        u1[here] = jnp.where(iv1[here] > 0.0, w1[here] + u1[here], 0.0)

    chunks(wide1, start1, grid1.size)
    post(grid1, (cx1, cy1, cz1, iv1), g01, u1, g1, da1, db1, e1, 1)

    for copy in copies[6:]:
        copy.wait()
    grid0 = Grid(wide0, yw, LANES, 1, 1, False, geo["chunk_up"])

    def fill(i, carry):
        at = WIN1 + 1 - WIN0 // 2 + i
        middle = 0.75 * e1[at]
        for j, side in ((0, e1[at - 1]), (1, e1[at + 1])):
            place_rows(u0, 1 + 2 * i + j, spread_z(middle + 0.25 * side, 1, LANES, False), yw // 2)
        return carry

    lax.fori_loop(0, wide0 // 2, fill, 0, unroll=4)

    def start0(at):
        here = pl.ds(at, grid0.size)
        u0[here] = jnp.where(iv0[here] > 0.0, w0[here] + u0[here], 0.0)

    chunks(wide0, start0, grid0.size)
    coeffs0 = (cx0, cy0, cz0, iv0)
    post(grid0, coeffs0, g00, u0, g0, da0, db0, w0, 1)

    own = pl.ds(1 + WIN0, bx)
    own_rows = pl.ds(pl.multiple_of(geo["oy"] + core * by, 8), by)
    sib_rows = pl.ds(pl.multiple_of(geo["oy"] + (1 - core) * by, 8), by)
    leaving = []

    def leave(source, rows, target):
        copy = pltpu.make_async_copy(source.at[own, rows], target, sems.at[12 + len(leaving)])
        copy.start()
        leaving.append(copy)

    leave(w0, sib_rows, send_u)
    leave(w0, own_rows, keep_u)

    def residual(here, v, value, direction):
        g0[here] = value / iv0[here]

    Grid(bx, yw, LANES, 1, 1, False, geo["chunk_last"]).step(coeffs0, da0, g0, 0.0, None, residual, 1 + WIN0)
    leave(g0, sib_rows, send_r)
    leave(g0, own_rows, keep_r)
    for copy in leaving:
        copy.wait()


def array(*shape):
    return jax.ShapeDtypeStruct(shape, jnp.float32)


def on_device(right_side, conductivity):
    bx, by, bz = right_side.shape
    nx, ny, nz = (lax.axis_size(axis) for axis in AXES)
    pairs = ny // 2
    ix, iy, iz = (lax.axis_index(axis) for axis in AXES)
    core = iy % 2

    def index(x, p, c, z):
        return ((x % nx) * ny + (p % pairs) * 2 + c) * nz + z % nz

    every = [(x, p, z) for x in range(nx) for p in range(pairs) for z in range(nz)]

    def sibling(v):
        return lax.ppermute(v, "gy", [(i, i ^ 1) for i in range(ny)])

    def xor(v, axis, k):
        return lax.ppermute(v, axis, [(i, i ^ k) for i in range(lax.axis_size(axis))])

    def paired(v, first):
        perm = [(i, i) for i in range(nx)]
        for i in range(first, nx - 1, 2):
            perm[i], perm[i + 1] = (i, i + 1), (i + 1, i)
        return lax.ppermute(v, "gx", perm)

    def facing(v):
        perm = {}
        for x, p, z in every:
            if z > 0:
                a, b = index(x, p, 0, z), index(x, p, 1, z - 1)
                perm[a], perm[b] = b, a
        return lax.ppermute(v, AXES, [(i, perm.get(i, i)) for i in range(nx * ny * nz)])

    own_b, own_k, ye = right_side, conductivity, by
    if ny > 2:
        near = []
        far = []
        for p in range(pairs):
            near += [(2 * p, 2 * ((p - 1) % pairs) + 1), (2 * ((p - 1) % pairs) + 1, 2 * p)]
            far += [(2 * p, 2 * ((p + 1) % pairs)), (2 * p + 1, 2 * ((p - 1) % pairs) + 1)]
        there = jnp.where(core == 0, iy > 0, iy < ny - 1)

        def widened(v):
            one = jnp.where(there, lax.ppermute(v, "gy", near), 0.0)
            two = jnp.where(there, lax.ppermute(v, "gy", far), 0.0)
            return jnp.where(core == 0, jnp.concatenate([two, one, v], 1), jnp.concatenate([v, one, two], 1))

        own_b, own_k = widened(own_b), widened(own_k)
        ye = 3 * by
    yw = 2 * ye
    xw = bx + 2 * REACH_X
    geo = dict(
        bx=bx, by=by, ye=ye, yw=yw, xw=xw, oy=(yw - 2 * by) // 2, chunk0=56 if yw == 32 else 4, chunk0_inner=48 if yw == 32 else 4,
        chunk_up=40 if yw == 32 else 4, chunk_last=32 if yw == 32 else 4, chunk1=28 if yw == 32 else 4,
        packed=pairs == 1 and 32 * nz == LANES, x2=bx // 4 * nx, y2=by // 4 * ny, z2=bz // 4 * nz,
        pad_y=(yw // 4 - by // 2) // 2,
    )

    own = lax.optimization_barrier(jnp.concatenate([own_b, own_k], 0))
    even = ix % 2 == 0
    high = jnp.concatenate([own[bx - REACH_XB:bx], own[2 * bx - REACH_X:]], 0)
    low = jnp.concatenate([own[:REACH_XB], own[bx:bx + REACH_X]], 0)
    even_own = paired(jnp.where(even, high, low), 0)
    sib, odd_send = lax.optimization_barrier((sibling(own), jnp.where(even, low, high)))
    odd_own = paired(odd_send, 1)
    inside, hbm, anywhere = (pl.BlockSpec(memory_space=space) for space in (pltpu.VMEM, pltpu.HBM, pl.ANY))

    def call(name, kernel, ins, outs, scratch, hbm_ins=0, hbm_outs=0, limit=0, operand=inside, result=inside):
        held = sum(4 * math.prod(v.shape) for v in (*ins, *outs, *scratch) if v.dtype == jnp.float32)
        return pl.pallas_call(
            kernel, out_shape=outs, in_specs=[operand] * (len(ins) - hbm_ins) + [hbm] * hbm_ins,
            out_specs=[result] * (len(outs) - hbm_outs) + [hbm] * hbm_outs,
            scratch_shapes=scratch, name=name,
            compiler_params=pltpu.CompilerParams(vmem_limit_bytes=max(limit, held + 6 * 1024 * 1024)),
            cost_estimate=pl.CostEstimate(flops=4_000_000, bytes_accessed=8_000_000, transcendentals=0),
        )(*ins)

    def vmem(shape):
        return pltpu.VMEM(shape, jnp.float32)

    def pack(name, slots, plane_of, ins, later=()):
        kernel = functools.partial(pack_kernel, geo, slots, plane_of, len(ins))
        return call(name, kernel, (*ins, *later), [array(len(slots), yw, LANES)], [], len(later))[0]

    z_send = pack("pack_box", box_slots(bx), lambda item: (0, item[0] * bx + item[1]), (own, sib))
    z_in = facing(z_send)
    even_own, odd_own, z_send = lax.optimization_barrier((even_own, odd_own, z_send))
    even_sib, odd_sib = sibling(even_own), sibling(odd_own)

    def halo_plane(item):
        pair, field, x = item
        first, count = (0, REACH_XB) if field == 0 else (REACH_XB, REACH_X)
        from_above = (lax.rem(lax.axis_index("gx"), 2) == 0) == (pair == 0)
        return pair, first + jnp.where(from_above, x - 1, count - x)

    zx_in = facing(pack("pack_halo", halo_slots(), halo_plane, (even_own, odd_own, even_sib, odd_sib), (z_in,)))

    wide0, wide1 = bx + 2 * WIN0, bx // 2 + 2 * WIN1
    x1, y1 = xw // 2, yw // 2
    some0 = vmem((xw + 2, yw, LANES))
    some1 = vmem((x1 + 2, y1, LANES))
    passed = array(6 * (wide0 + 1) + 3 * (wide1 + 1), yw, LANES)
    edge = 9
    ins = (own, sib, even_own, odd_own, even_sib, odd_sib, z_in, zx_in)
    sends = [array(nx * ny * nz if geo["packed"] else 1, 2, by // 2, LANES), array(edge, y1, LANES), array(edge, y1, LANES)]
    down = call(
        "down", functools.partial(down_kernel, geo), ins, sends + [passed],
        [vmem(v.shape) for v in sends] + [some0] * 10 + [some1] * 11
        + [vmem((6, yw, LANES)), vmem((6, y1, LANES)), pltpu.SemaphoreType.DMA((15,))],
        hbm_outs=1, limit=VMEM_LIMIT, result=anywhere,
    )
    packed, even_send, odd_send, passed = down[0], down[1], down[2], down[3]
    from_even, from_odd = paired(even_send, 0), paired(odd_send, 1)

    if geo["packed"]:
        gathered = lax.all_to_all(packed, AXES, 0, 0, tiled=True)
    else:
        pieces = lax.all_gather(packed, AXES).reshape(nx, pairs, 2, nz, 2, by // 2, 8, 16)
        order = (jnp.arange(8) + 2 * jnp.arange(nz)[:, None, None] + jnp.arange(2)[:, None]) % 8
        order = jnp.transpose(order, (1, 0, 2))[None, None, :, :, None, None, :, None]
        pieces = jnp.take_along_axis(pieces, order, axis=6)
        gathered = jnp.transpose(pieces, (4, 0, 6, 1, 5, 3, 2, 7)).reshape(2, geo["x2"], geo["y2"], geo["z2"])

    def level(planes, rows, lanes):
        return vmem((planes + 2, rows, lanes))

    x2, y2, z2 = geo["x2"], geo["y2"], geo["z2"]
    send_u, send_r, keep_u, keep_r = call(
        "up", functools.partial(up_kernel, geo), (gathered, from_even, from_odd, passed), [array(bx, by, LANES)] * 4,
        [level(x2, y2, z2)] * 12 + [level(x2 // 2, y2, z2)] * 12 + [level(x2 // 4, y2, z2)] * 10
        + [level(wide1, y1, LANES)] * 11 + [level(wide0, yw, LANES)] * 10
        + [vmem((x2 + 8, y2 + 2 * geo["pad_y"], z2)), vmem(gathered.shape), vmem(from_even.shape), vmem(from_odd.shape)]
        + [pltpu.SemaphoreType.DMA((19,))],
        hbm_ins=1, limit=VMEM_LIMIT, operand=anywhere, result=anywhere,
    )
    mine = lanes_of((1, 1, LANES)) // HALF == core
    return jnp.where(mine, keep_u, sibling(send_u)), jnp.where(mine, keep_r, sibling(send_r))


def solution(mesh):
    specs = (P(*AXES), P(*AXES))
    return jax.shard_map(on_device, mesh=mesh, in_specs=specs, out_specs=specs, check_vma=False)
```

```python
import functools
import math
import jax
import jax.numpy as jnp
from jax import lax
from jax.experimental import pallas as pl
from jax.experimental.pallas import tpu as pltpu
from jax.sharding import PartitionSpec as P

LEVELS = 4
STEPS = 3
COARSE_STEPS = 8
LOWER_EDGE = 0.3
UPPER_EDGE = 2.0

LANES = 128
HALF = 64
REACH_X = 12
REACH_XB = 9
REACH_Z = 20
WIN0 = 4
WIN1 = REACH_X // 2
VMEM_LIMIT = 48 * 1024 * 1024
AXES = ("gx", "gy", "gz")


def chebyshev_factors(sweeps):
    centre_value = 0.5 * (UPPER_EDGE + LOWER_EDGE)
    half_width = 0.5 * (UPPER_EDGE - LOWER_EDGE)
    ratio_value = centre_value / half_width
    damping = 1.0 / ratio_value
    factors = [(0.0, 1.0 / centre_value)]
    for _ in range(1, sweeps):
        damping_next = 1.0 / (2.0 * ratio_value - damping)
        factors.append((damping_next * damping, 2.0 * damping_next / half_width))
        damping = damping_next
    return factors


FACTORS = chebyshev_factors(STEPS)
COARSE_FACTORS = chebyshev_factors(COARSE_STEPS)


def chunks(count, body, size, first=1):
    if count == size:
        body(first)
    else:
        def step(i, carry):
            body(first + i * size)
            return carry
        lax.fori_loop(0, count // size, step, 0)


def rows_of(shape):
    return lax.broadcasted_iota(jnp.int32, shape, len(shape) - 2)


def lanes_of(shape):
    return lax.broadcasted_iota(jnp.int32, shape, len(shape) - 1)


class Grid:
    def __init__(self, x, y, z, sy, sz, whole_z, size):
        self.x, self.y, self.z, self.sy, self.sz = x, y, z, sy, sz
        self.whole_z, self.size = whole_z, size

    def up_y(self, v):
        return pltpu.roll(v, self.y - self.sy, v.ndim - 2)

    def down_y(self, v):
        return pltpu.roll(v, self.sy, v.ndim - 2)

    def up_z(self, v):
        return pltpu.roll(v, self.z - self.sz, v.ndim - 1)

    def down_z(self, v):
        return pltpu.roll(v, self.sz, v.ndim - 1)

    def setup(self, k_ref, cx, cy, cz, iv, ds, scale, after=None):
        cx[0] = 0.5 * (k_ref[0] + k_ref[1])

        def body(at):
            here = pl.ds(at, self.size)
            k = k_ref[here]
            row, lane = rows_of(k.shape), lanes_of(k.shape)
            k_next = k_ref[pl.ds(at + 1, self.size)]
            k_prev = k_ref[pl.ds(at - 1, self.size)]
            not_last = row < self.y - self.sy
            k_up = jnp.where(not_last, self.up_y(k), 0.0)
            k_down = jnp.where(row >= self.sy, self.down_y(k), 0.0)
            z_up, z_down = self.up_z(k), self.down_z(k)
            if self.whole_z:
                inner = lane < self.z - self.sz
                z_up = jnp.where(inner, z_up, 0.0)
                z_down = jnp.where(lane >= self.sz, z_down, 0.0)
            total = 3.0 * k + 0.5 * ((k_next + k_prev) + (k_up + k_down) + (z_up + z_down))
            inverse = jnp.where(k > 0.0, 1.0 / total, 0.0)
            cx[here] = 0.5 * (k + k_next)
            cy[here] = jnp.where(not_last, 0.5 * (k + k_up), 0.0)
            across = 0.5 * (k + z_up)
            cz[here] = jnp.where(inner, across, 0.0) if self.whole_z else across
            iv[here] = inverse
            if ds is not None:
                ds[here] = scale * total
            if after is not None:
                after(at, here, inverse)

        chunks(self.x, body, self.size)

    def step(self, coeffs, src, g_in, keep, push, out, first=1, count=None):
        cx, cy, cz, iv = coeffs

        def body(at):
            here = pl.ds(at, self.size)
            planes, x_coeff = src[pl.ds(at - 1, self.size + 2)], cx[pl.ds(at - 1, self.size + 1)]
            v = planes[1:-1]
            y_coeff, z_coeff = cy[here], cz[here]
            near = x_coeff[1:] * planes[2:] + x_coeff[:-1] * planes[:-2]
            near = near + (y_coeff * self.up_y(v) + self.down_y(y_coeff * v))
            near = near + (z_coeff * self.up_z(v) + self.down_z(z_coeff * v))
            g = g_in[here] - v + iv[here] * near
            out(here, v, g, None if push is None else (keep * v + push * g if keep else push * g))

        chunks(count or self.x, body, self.size, first)


def pair_z(v, shift, lanes):
    even = (lanes_of(v.shape) // shift) % 2 == 0
    return v + jnp.where(even, pltpu.roll(v, lanes - shift, v.ndim - 1), pltpu.roll(v, shift, v.ndim - 1))


def pair_y(v, shift, rows):
    even = (rows_of(v.shape) // shift) % 2 == 0
    return v + jnp.where(even, pltpu.roll(v, rows - shift, v.ndim - 2), pltpu.roll(v, shift, v.ndim - 2))


def spread_z(v, shift, lanes, whole):
    lane = lanes_of(v.shape)
    even = (lane // shift) % 2 == 0
    low, high = pltpu.roll(v, shift, v.ndim - 1), pltpu.roll(v, lanes - shift, v.ndim - 1)
    if whole:
        low = jnp.where(lane >= shift, low, 0.0)
        high = jnp.where(lane < lanes - shift, high, 0.0)
    return 0.75 * v + 0.25 * jnp.where(even, low, high)


def spread_y(v, shift, rows):
    row = rows_of(v.shape)
    even = (row // shift) % 2 == 0
    low = jnp.where(row >= shift, pltpu.roll(v, shift, v.ndim - 2), 0.0)
    high = jnp.where(row < rows - shift, pltpu.roll(v, rows - shift, v.ndim - 2), 0.0)
    return 0.75 * v + 0.25 * jnp.where(even, low, high)


def picked_lanes(v, pick):
    pick, total = pick.astype(jnp.bfloat16), None
    for _ in range(3):
        part = v.astype(jnp.bfloat16)
        v = v - part.astype(jnp.float32)
        product = jnp.dot(part, pick, preferred_element_type=jnp.float32)
        total = product if total is None else total + product
    return total


def zero_pads(*refs):
    for ref in refs:
        ref[0] = jnp.zeros(ref.shape[1:], jnp.float32)
        ref[ref.shape[0] - 1] = jnp.zeros(ref.shape[1:], jnp.float32)


def core_of():
    return lax.rem(lax.axis_index("gy"), 2)


def reaches():
    source1 = {0: WIN1 + 2, 1: WIN1 + 1, 2: WIN1, 3: 0}
    coeff1 = {a: max(source1.get(a, -1) + 1, source1.get(a - 1, -1), source1.get(a + 1, -1), min(WIN1, 7 - a)) for a in range(7)}
    residual0 = {0: 2 * source1[0]}
    coeff0 = {0: 2 * coeff1[0]}
    for a in range(1, 7):
        for x in (2 * a - 1, 2 * a):
            coeff0[x] = 2 * coeff1[a]
            if a in source1:
                residual0[x] = 2 * source1[a]

    def grown(steps, x):
        return max([z + steps - abs(x - at) for at, z in residual0.items() if abs(x - at) <= steps], default=0)

    source = [grown(3, x) for x in range(REACH_XB + 1)]
    coeff = [max(grown(4, x), coeff0[x]) for x in range(REACH_X + 1)]
    assert max(source + coeff) <= REACH_Z
    return source, coeff


def slots_of(items):
    rows, used = [], LANES
    for item, width in items:
        if width:
            if used + width > LANES:
                rows.append([])
                used = 0
            rows[-1].append((item, used, width))
            used += width
    return rows


def box_slots(bx):
    source, coeff = reaches()
    return slots_of([((0, p), source[0]) for p in range(bx)] + [((1, p), coeff[0]) for p in range(bx)])


def halo_slots():
    source, coeff = reaches()
    items = []
    for pair in range(2):
        items += [((pair, 0, x), source[x]) for x in range(1, REACH_XB + 1)]
        items += [((pair, 1, x), coeff[x]) for x in range(1, REACH_X + 1)]
    return slots_of(items)


def pack_kernel(geo, slots, plane_of, count, *refs):
    own, sib, z_out = refs[:count // 2], refs[count // 2:count], refs[-1]
    core, ye = core_of(), geo["ye"]
    lane = lanes_of((ye, LANES))
    for fields, half in ((own, core), (sib, 1 - core)):
        rows = pl.ds(pl.multiple_of(half * ye, 8), ye)
        for m, row in enumerate(slots):
            packed = jnp.zeros((ye, LANES), jnp.float32)
            for item, at, width in row:
                shift = jnp.where(core == 1, (at + width) % LANES, at)
                field, plane = plane_of(item)
                packed = jnp.where((lane >= at) & (lane < at + width), pltpu.roll(fields[field][plane], shift, 1), packed)
            z_out[m, rows] = packed


def passed_views(geo, ref):
    wide0, wide1, rows = geo["bx"] + 2 * WIN0, geo["bx"] // 2 + 2 * WIN1, geo["yw"] // 2
    views, at = [], 0
    for i in range(6):
        views.append(ref.at[pl.ds(at, wide0 + (i == 0))])
        at += wide0 + 1
    for i in range(6):
        views.append(ref.at[pl.ds(at + i // 2 * (wide1 + 1), wide1 + (i == 0)), pl.ds(i % 2 * rows, rows)])
    return views


def down_kernel(geo, *refs):
    (own_in, sib_in, even_own, odd_own, even_sib, odd_sib, z_in, zx_in, packed_any, even_any, odd_any, passed,
     packed_out, even_out, odd_out,
     k0, cx, cy, cz, iv, ds, g0, g, d1, d2,
     k1, ex, ey, ez, ei, es, h0, h, f1, f2, u1, half_y, half_y1, sems) = refs
    core = core_of()
    ix, nx = lax.axis_index("gx"), lax.axis_size("gx")
    iz, nz = lax.axis_index("gz"), lax.axis_size("gz")
    bx, ye, yw, xw = geo["bx"], geo["ye"], geo["yw"], geo["xw"]
    z_there = jnp.where(core == 0, iz > 0, iz < nz - 1)
    lo_there, hi_there = ix > 0, ix < nx - 1
    even = lax.rem(ix, 2) == 0

    lane = lanes_of((yw, LANES))

    def strip(ref, m, at, width):
        shift = jnp.where(core == 0, (2 * LANES - width - at) % LANES, (LANES - at) % LANES)
        return pltpu.roll(ref[m], shift, 1)

    def merge(window, at, width, there, moved):
        halo = jnp.where(core == 0, lane - (LANES - width), width - 1 - lane) >= 0
        window[at] = jnp.where(halo, jnp.where(there, moved, 0.0), window[at])

    own_rows = pl.ds(pl.multiple_of(core * ye, 8), ye)
    sib_rows = pl.ds(pl.multiple_of((1 - core) * ye, 8), ye)
    zero_pads(k0, d1, d2, k1, f1, f2)
    windows = ((g0, 0, REACH_XB, 0), (k0, bx, REACH_X, REACH_XB))
    for p in range(REACH_X - REACH_XB):
        g0[1 + p] = jnp.zeros((yw, LANES), jnp.float32)
        g0[xw - p] = jnp.zeros((yw, LANES), jnp.float32)

    def halos(from_even, from_odd, rows):
        for window, _, width, at in windows:
            e, o = from_even[pl.ds(at, width)], from_odd[pl.ds(at, width)]
            window[pl.ds(1 + REACH_X - width, width), rows] = jnp.where(lo_there, jnp.where(even, o, e), 0.0)
            window[pl.ds(1 + REACH_X + bx, width), rows] = jnp.where(hi_there, jnp.where(even, e, o), 0.0)

    for window, at, _, _ in windows:
        window[pl.ds(1 + REACH_X, bx), own_rows] = own_in[pl.ds(at, bx)]
        window[pl.ds(1 + REACH_X, bx), sib_rows] = sib_in[pl.ds(at, bx)]
    halos(even_own, odd_own, own_rows)
    halos(even_sib, odd_sib, sib_rows)
    for m, row in enumerate(box_slots(bx)):
        for (f, p), at, width in row:
            merge(windows[f][0], 1 + REACH_X + p, width, z_there, strip(z_in, m, at, width))
    places = {item: (m, at, width) for m, row in enumerate(halo_slots()) for item, at, width in row}
    for (pair, f, x), place in places.items():
        if pair == 0:
            window, width = windows[f][0], place[2]
            e, o = strip(zx_in, *place), strip(zx_in, *places[1, f, x])
            merge(window, 1 + REACH_X - x, width, z_there & lo_there, jnp.where(even, o, e))
            merge(window, REACH_X + bx + x, width, z_there & hi_there, jnp.where(even, e, o))

    grid = Grid(xw, yw, LANES, 1, 1, False, geo["chunk0"])
    inner = Grid(xw - 8, yw, LANES, 1, 1, False, geo["chunk0_inner"])
    nothing = jnp.zeros((4, yw, LANES), jnp.float32)
    for ref in (g, d2):
        ref[pl.ds(1, 4)] = nothing
        ref[pl.ds(xw - 3, 4)] = nothing

    def first(at, here, inverse):
        scaled = g0[here] * inverse
        g0[here] = scaled
        d1[here] = FACTORS[0][1] * scaled

    grid.setup(k0, cx, cy, cz, iv, ds, 1.0, first)
    own0 = 1 + REACH_X - WIN0
    wide0 = bx + 2 * WIN0
    copies = []

    views = passed_views(geo, passed)

    def send(source, start, count):
        i = len(copies)
        copy = pltpu.make_async_copy(source.at[pl.ds(start, count)], views[i], sems.at[i])
        copy.start()
        copies.append(copy)

    send(cx, own0 - 1, wide0 + 1)
    send(cy, own0, wide0)
    send(cz, own0, wide0)
    send(iv, own0, wide0)
    send(g0, own0, wide0)

    def restrict(source, target, tmp, x_count, at, y_first, y_rows, shift):
        for i in range(x_count):
            j = i % tmp.shape[0]
            tmp[j] = source[at + 2 * i] + source[at + 2 * i + 1]
            v = tmp[j, pl.ds(y_first, y_rows // 2, stride=2)] + tmp[j, pl.ds(y_first + 1, y_rows // 2, stride=2)]
            target(i, 0.125 * pair_z(v, shift, LANES))

    x1, y1 = xw // 2, yw // 2

    def put_k1(i, v):
        k1[1 + i] = v

    def put_b1(i, v):
        h0[1 + i] = v

    restrict(k0, put_k1, half_y, x1, 1, 0, yw, 1)
    coeffs = (cx, cy, cz, iv)

    def second(here, v, value, direction):
        g[here] = value
        d2[here] = direction

    inner.step(coeffs, d1, g0, *FACTORS[1], second, 5)

    def third(here, v, value, direction):
        g[here] = value
        k0[here] = d1[here] + v + direction
        d1[here] = direction

    inner.step(coeffs, d2, g, *FACTORS[2], third, 5)
    send(k0, own0, wide0)

    def residual(here, v, value, direction):
        g[here] = value * ds[here]

    inner.step(coeffs, d1, g, 0.0, None, residual, 5)

    restrict(g, put_b1, half_y, x1, 1, 0, yw, 1)
    grid1 = Grid(x1, y1, LANES, 1, 2, False, geo["chunk1"])

    def first1(at, here, inverse):
        scaled = 4.0 * (h0[here] * inverse)
        h0[here] = scaled
        f1[here] = FACTORS[0][1] * scaled

    grid1.setup(k1, ex, ey, ez, ei, es, 0.25, first1)
    own1 = 1 + REACH_X // 2 - WIN1
    wide1 = bx // 2 + 2 * WIN1
    send(ex, own1 - 1, wide1 + 1)
    send(ey, own1, wide1)
    send(ez, own1, wide1)
    send(ei, own1, wide1)
    send(h0, own1, wide1)
    coeffs1 = (ex, ey, ez, ei)

    def second1(here, v, value, direction):
        h[here] = value
        f2[here] = direction

    grid1.step(coeffs1, f1, h0, *FACTORS[1], second1)

    def third1(here, v, value, direction):
        h[here] = value
        u1[here] = f1[here] + v + direction
        f1[here] = direction

    grid1.step(coeffs1, f2, h, *FACTORS[2], third1)
    send(u1, own1, wide1)
    mine = 1 + REACH_X // 2
    last = mine + bx // 2
    for source, low, high, at, count in ((u1, mine, last - WIN1, 0, 6), (h0, mine + 2, last - 5, 6, 3)):
        low, high = source[pl.ds(low, count)], source[pl.ds(high, count)]
        even_out[pl.ds(at, count)] = jnp.where(even, high, low)
        odd_out[pl.ds(at, count)] = jnp.where(even, low, high)

    def leave(source, target):
        copy = pltpu.make_async_copy(source, target, sems.at[len(copies)])
        copy.start()
        copies.append(copy)

    leave(even_out, even_any)
    leave(odd_out, odd_any)

    def residual1(here, v, value, direction):
        h[here] = value * es[here]

    grid1.step(coeffs1, f1, h, 0.0, None, residual1)

    place = lax.rem(2 * iz + core, 8)
    x2, y2 = bx // 4, geo["by"] // 2
    row, column = rows_of((LANES, LANES)), lanes_of((LANES, LANES))
    pick = (row == HALF * core + 4 * lax.rem(column, 16)).astype(jnp.float32)
    slot = lanes_of((y2, LANES)) // 16
    for f, source in enumerate((h, k1)):
        boxes = []
        restrict(source, lambda i, v, boxes=boxes: boxes.append(v), half_y1, x2, 1 + REACH_X // 2, geo["oy"] // 2, 2 * y2, 2)
        stacked = jnp.concatenate(boxes, axis=0)
        picked = picked_lanes(stacked, pick)
        packed = jnp.zeros((y2, LANES), jnp.float32)
        for p in range(x2):
            packed = jnp.where(slot == lax.rem(p + place, 8), picked[p * y2:(p + 1) * y2], packed)
        if geo["packed"]:
            for j in range(packed_out.shape[0]):
                if (j // nz) % 2 == f:
                    packed_out[j] = packed
        else:
            packed_out[f] = packed
    leave(packed_out, packed_any)
    for copy in copies:
        copy.wait()


def up_kernel(geo, *refs):
    refs = list(refs)

    def take(count):
        taken = refs[:count]
        del refs[:count]
        return taken

    count = 2 if geo["packed"] else 1
    arriving = take(count + 2)
    views = passed_views(geo, take(1)[0])
    in0, in1 = views[:6], views[6:]
    send_u, send_r, keep_u, keep_r = take(4)
    k2, cx2, cy2, cz2, iv2, ds2, g02, g2, da2, db2, w2, e2 = take(12)
    k3, cx3, cy3, cz3, iv3, ds3, g03, g3, da3, db3, w3, e3 = take(12)
    k4, cx4, cy4, cz4, iv4, g04, g4, da4, db4, e4 = take(10)
    cx1, cy1, cz1, iv1, g01, w1, u1, g1, da1, db1, e1 = take(11)
    cx0, cy0, cz0, iv0, g00, w0, u0, g0, da0, db0 = take(10)
    e2_wide, = take(1)
    gathered = take(count)
    from_even, from_odd, sems = take(3)
    core = core_of()
    ix, nx = lax.axis_index("gx"), lax.axis_size("gx")
    iz, nz = lax.axis_index("gz"), lax.axis_size("gz")
    yp = lax.axis_index("gy") // 2
    bx, by, yw = geo["bx"], geo["by"], geo["yw"]
    x2, y2, z2 = geo["x2"], geo["y2"], geo["z2"]
    wide0, wide1 = bx + 2 * WIN0, bx // 2 + 2 * WIN1

    arrivals = []
    for source, target in zip(arriving, (*gathered, from_even, from_odd)):
        arrivals.append(pltpu.make_async_copy(source, target, sems.at[16 + len(arrivals)]))
        arrivals[-1].start()
    copies = []
    for sources, targets, wide in ((in1, (cx1, cy1, cz1, iv1, g01, w1), wide1), (in0, (cx0, cy0, cz0, iv0, g00, w0), wide0)):
        for i, (source, target) in enumerate(zip(sources, targets)):
            there = target.at[pl.ds(0, wide + 1)] if i == 0 else target.at[pl.ds(1, wide)]
            copy = pltpu.make_async_copy(source, there, sems.at[len(copies)])
            copy.start()
            copies.append(copy)

    zero_pads(k2, da2, db2, e2, k3, da3, db3, e3, k4, da4, db4, e4, u1, da1, db1, u0, da0, db0)

    for copy in arrivals:
        copy.wait()
    if geo["packed"]:
        slot = lanes_of((y2, LANES)) // 16
        for gx in range(nx):
            for f, target in ((0, g02), (1, k2)):
                for p in range(8):
                    merged = jnp.zeros((y2, LANES), jnp.float32)
                    for gz in range(nz):
                        for cc in range(2):
                            at = (2 * gx + cc) * nz + gz
                            here = jnp.where(core == f, gathered[0][at], gathered[1][at])
                            merged = jnp.where(slot == (p + 2 * gz + cc) % 8, here, merged)
                    target[1 + 8 * gx + p] = pltpu.roll(merged, (LANES - 16 * p) % LANES, 1)
    else:
        g02[pl.ds(1, x2)] = gathered[0][0]
        k2[pl.ds(1, x2)] = gathered[0][1]

    def descend(grid, level, k, cx, cy, cz, iv, ds, g0, first_target):
        def first(at, here, inverse):
            scaled = 4.0**level * (g0[here] * inverse)
            g0[here] = scaled
            first_target[here] = FACTORS[0][1] * scaled

        grid.setup(k, cx, cy, cz, iv, ds, 0.25**level, first)

    def pre(grid, level, k, cx, cy, cz, iv, ds, g0, g, da, db, w):
        descend(grid, level, k, cx, cy, cz, iv, ds, g0, da)
        coeffs = (cx, cy, cz, iv)

        def second(here, v, value, direction):
            g[here] = value
            db[here] = direction

        grid.step(coeffs, da, g0, *FACTORS[1], second)

        def third(here, v, value, direction):
            g[here] = value
            w[here] = da[here] + v + direction
            da[here] = direction

        grid.step(coeffs, db, g, *FACTORS[2], third)

        def residual(here, v, value, direction):
            g[here] = value * ds[here]

        grid.step(coeffs, da, g, 0.0, None, residual)

    def post(grid, coeffs, g0, u, g, da, db, result, shrink=0):
        def step(i, *args):
            part = Grid(grid.x - 2 * i * shrink, grid.y, grid.z, grid.sy, grid.sz, grid.whole_z, grid.size)
            if shrink:
                part.size = part.x if grid.size == grid.x else 2
            part.step(coeffs, *args, 1 + i * shrink)

        def one(here, v, value, direction):
            g[here] = value
            da[here] = direction

        step(1, u, g0, *FACTORS[0], one)

        def two(here, v, value, direction):
            g[here] = value
            db[here] = direction

        step(2, da, g, *FACTORS[1], two)

        def three(here, v, value, direction):
            g[here] = value
            result[here] = u[here] + da[here] + v + direction
            da[here] = direction

        step(3, db, g, *FACTORS[2], three)

    def restrict(fine, coarse, count, shift):
        for i in range(count):
            v = fine[1 + 2 * i] + fine[2 + 2 * i]
            coarse[1 + i] = 0.125 * pair_z(pair_y(v, shift, y2), shift, z2)

    def prolong(coarse, w, target, count, shift):
        for i in range(count):
            middle = 0.75 * coarse[1 + i]
            for j, side in ((0, coarse[i]), (1, coarse[2 + i])):
                v = spread_y(middle + 0.25 * side, shift, y2)
                target[1 + 2 * i + j] = w[1 + 2 * i + j] + spread_z(v, shift, z2, True)

    def size_of(x):
        planes = max(1, 32 // ((y2 // 8) * (z2 // LANES)))
        return min(x, planes)

    x3, x4 = x2 // 2, x2 // 4
    grid2 = Grid(x2, y2, z2, 1, 1, True, size_of(x2))
    grid3 = Grid(x3, y2, z2, 2, 2, True, size_of(x3))
    grid4 = Grid(x4, y2, z2, 4, 4, True, size_of(x4))
    pre(grid2, 2, k2, cx2, cy2, cz2, iv2, ds2, g02, g2, da2, db2, w2)
    restrict(k2, k3, x3, 1)
    restrict(g2, g03, x3, 1)
    pre(grid3, 3, k3, cx3, cy3, cz3, iv3, ds3, g03, g3, da3, db3, w3)
    restrict(k3, k4, x4, 2)
    restrict(g3, g04, x4, 2)
    descend(grid4, 4, k4, cx4, cy4, cz4, iv4, None, g04, da4)
    e4[pl.ds(1, x4)] = da4[pl.ds(1, x4)]
    for sweep in range(1, COARSE_STEPS):
        src, dst = (da4, db4) if sweep % 2 else (db4, da4)

        def coarse(here, v, value, direction):
            g4[here] = value
            dst[here] = direction
            e4[here] = e4[here] + direction

        grid4.step((cx4, cy4, cz4, iv4), src, g04 if sweep == 1 else g4, *COARSE_FACTORS[sweep], coarse)
    prolong(e4, w3, e3, x4, 2)
    post(grid3, (cx3, cy3, cz3, iv3), g03, e3, g3, da3, db3, w3)
    e3[pl.ds(1, x3)] = w3[pl.ds(1, x3)]
    prolong(e3, w2, e2, x3, 1)
    post(grid2, (cx2, cy2, cz2, iv2), g02, e2, g2, da2, db2, w2)

    pad_y = geo["pad_y"]
    if pad_y:
        e2_wide[...] = jnp.zeros(e2_wide.shape, jnp.float32)
    else:
        edge = jnp.zeros((4,) + e2_wide.shape[1:], jnp.float32)
        e2_wide[pl.ds(0, 4)] = edge
        e2_wide[pl.ds(x2 + 4, 4)] = edge
    e2_wide[pl.ds(4, x2), pl.ds(pad_y, y2)] = w2[pl.ds(1, x2)]
    x2w, y2w = bx // 4 + 8, yw // 4
    cells, lane = rows_of((z2, LANES)), lanes_of((z2, LANES))
    shifted = jnp.where(core == 0, jnp.where(lane >= 104, -32, 0), jnp.where(lane < 24, 32, 0))
    pick = (cells == 32 * iz + lane // 4 + shifted).astype(jnp.float32)
    start = (bx // 4) * ix
    rows = pl.ds(pl.multiple_of(8 * yp, 8), y2w) if pad_y else pl.ds(0, y2w)
    window = e2_wide[pl.ds(start, x2w), rows].reshape(x2w * y2w, z2)
    window = picked_lanes(window, pick)
    window = window.reshape(x2w, y2w, LANES)

    def place_rows(target, plane, v, count):
        row = rows_of(v.shape)
        low = jnp.where(row >= 1, pltpu.roll(v, 1, 0), 0.0)
        high = jnp.where(row < count - 1, pltpu.roll(v, count - 1, 0), 0.0)
        target[plane, pl.ds(0, count, stride=2)] = 0.75 * v + 0.25 * low
        target[plane, pl.ds(1, count, stride=2)] = 0.75 * v + 0.25 * high

    for copy in copies[:6]:
        copy.wait()
    even, last1 = lax.rem(ix, 2) == 0, 1 + WIN1 + bx // 2
    for target, low, high, at, count in ((w1, 1, last1, 0, 6), (g01, 2, last1 + 2, 6, 3)):
        e, o = from_even[pl.ds(at, count)], from_odd[pl.ds(at, count)]
        low, high = pl.ds(low, count), pl.ds(high, count)
        target[low] = jnp.where(ix > 0, jnp.where(even, o, e), target[low])
        target[high] = jnp.where(ix < nx - 1, jnp.where(even, e, o), target[high])
    for plane in range(wide1):
        j = plane // 2
        v = 0.75 * window[j + 1] + 0.25 * window[j + 2 if plane % 2 else j]
        place_rows(u1, 1 + plane, spread_z(v, 2, LANES, False), y2w)
    grid1 = Grid(wide1, yw // 2, LANES, 1, 2, False, geo["chunk1"])

    def start1(at):
        here = pl.ds(at, grid1.size)
        u1[here] = jnp.where(iv1[here] > 0.0, w1[here] + u1[here], 0.0)

    chunks(wide1, start1, grid1.size)
    post(grid1, (cx1, cy1, cz1, iv1), g01, u1, g1, da1, db1, e1, 1)

    for copy in copies[6:]:
        copy.wait()
    grid0 = Grid(wide0, yw, LANES, 1, 1, False, geo["chunk_up"])

    def fill(i, carry):
        at = WIN1 + 1 - WIN0 // 2 + i
        middle = 0.75 * e1[at]
        for j, side in ((0, e1[at - 1]), (1, e1[at + 1])):
            place_rows(u0, 1 + 2 * i + j, spread_z(middle + 0.25 * side, 1, LANES, False), yw // 2)
        return carry

    lax.fori_loop(0, wide0 // 2, fill, 0, unroll=10)

    def start0(at):
        here = pl.ds(at, grid0.size)
        u0[here] = jnp.where(iv0[here] > 0.0, w0[here] + u0[here], 0.0)

    chunks(wide0, start0, grid0.size)
    coeffs0 = (cx0, cy0, cz0, iv0)
    post(grid0, coeffs0, g00, u0, g0, da0, db0, w0, 1)

    own = pl.ds(1 + WIN0, bx)
    own_rows = pl.ds(pl.multiple_of(geo["oy"] + core * by, 8), by)
    sib_rows = pl.ds(pl.multiple_of(geo["oy"] + (1 - core) * by, 8), by)
    leaving = []

    def leave(source, rows, target):
        copy = pltpu.make_async_copy(source.at[own, rows], target, sems.at[12 + len(leaving)])
        copy.start()
        leaving.append(copy)

    leave(w0, sib_rows, send_u)
    leave(w0, own_rows, keep_u)

    def residual(here, v, value, direction):
        g0[here] = value / iv0[here]

    Grid(bx, yw, LANES, 1, 1, False, geo["chunk_last"]).step(coeffs0, da0, g0, 0.0, None, residual, 1 + WIN0)
    leave(g0, sib_rows, send_r)
    leave(g0, own_rows, keep_r)
    for copy in leaving:
        copy.wait()


def array(*shape):
    return jax.ShapeDtypeStruct(shape, jnp.float32)


def on_device(right_side, conductivity):
    bx, by, bz = right_side.shape
    nx, ny, nz = (lax.axis_size(axis) for axis in AXES)
    pairs = ny // 2
    ix, iy, iz = (lax.axis_index(axis) for axis in AXES)
    core = iy % 2

    def index(x, p, c, z):
        return ((x % nx) * ny + (p % pairs) * 2 + c) * nz + z % nz

    every = [(x, p, z) for x in range(nx) for p in range(pairs) for z in range(nz)]

    def sibling(v):
        return lax.ppermute(v, "gy", [(i, i ^ 1) for i in range(ny)])

    def xor(v, axis, k):
        return lax.ppermute(v, axis, [(i, i ^ k) for i in range(lax.axis_size(axis))])

    def paired(v, first):
        perm = [(i, i) for i in range(nx)]
        for i in range(first, nx - 1, 2):
            perm[i], perm[i + 1] = (i, i + 1), (i + 1, i)
        return lax.ppermute(v, "gx", perm)

    def facing(v):
        perm = {}
        for x, p, z in every:
            if z > 0:
                a, b = index(x, p, 0, z), index(x, p, 1, z - 1)
                perm[a], perm[b] = b, a
        return lax.ppermute(v, AXES, [(i, perm.get(i, i)) for i in range(nx * ny * nz)])

    own_b, own_k, ye = right_side, conductivity, by
    if ny > 2:
        near = []
        far = []
        for p in range(pairs):
            near += [(2 * p, 2 * ((p - 1) % pairs) + 1), (2 * ((p - 1) % pairs) + 1, 2 * p)]
            far += [(2 * p, 2 * ((p + 1) % pairs)), (2 * p + 1, 2 * ((p - 1) % pairs) + 1)]
        there = jnp.where(core == 0, iy > 0, iy < ny - 1)

        def widened(v):
            one = jnp.where(there, lax.ppermute(v, "gy", near), 0.0)
            two = jnp.where(there, lax.ppermute(v, "gy", far), 0.0)
            return jnp.where(core == 0, jnp.concatenate([two, one, v], 1), jnp.concatenate([v, one, two], 1))

        own_b, own_k = widened(own_b), widened(own_k)
        ye = 3 * by
    yw = 2 * ye
    xw = bx + 2 * REACH_X
    geo = dict(
        bx=bx, by=by, ye=ye, yw=yw, xw=xw, oy=(yw - 2 * by) // 2, chunk0=56 if yw == 32 else 4, chunk0_inner=48 if yw == 32 else 4,
        chunk_up=40 if yw == 32 else 4, chunk_last=32 if yw == 32 else 4, chunk1=28 if yw == 32 else 4,
        packed=pairs == 1 and 32 * nz == LANES, x2=bx // 4 * nx, y2=by // 4 * ny, z2=bz // 4 * nz,
        pad_y=(yw // 4 - by // 2) // 2,
    )

    own = lax.optimization_barrier(jnp.concatenate([own_b, own_k], 0))
    even = ix % 2 == 0
    high = jnp.concatenate([own[bx - REACH_XB:bx], own[2 * bx - REACH_X:]], 0)
    low = jnp.concatenate([own[:REACH_XB], own[bx:bx + REACH_X]], 0)
    even_own = paired(jnp.where(even, high, low), 0)
    sib, odd_send = lax.optimization_barrier((sibling(own), jnp.where(even, low, high)))
    odd_own = paired(odd_send, 1)
    inside, hbm, anywhere = (pl.BlockSpec(memory_space=space) for space in (pltpu.VMEM, pltpu.HBM, pl.ANY))

    def call(name, kernel, ins, outs, scratch, hbm_ins=0, hbm_outs=0, limit=0, operand=inside, result=inside):
        held = sum(4 * math.prod(v.shape) for v in (*ins, *outs, *scratch) if v.dtype == jnp.float32)
        return pl.pallas_call(
            kernel, out_shape=outs, in_specs=[operand] * (len(ins) - hbm_ins) + [hbm] * hbm_ins,
            out_specs=[result] * (len(outs) - hbm_outs) + [hbm] * hbm_outs,
            scratch_shapes=scratch, name=name,
            compiler_params=pltpu.CompilerParams(vmem_limit_bytes=max(limit, held + 6 * 1024 * 1024)),
            cost_estimate=pl.CostEstimate(flops=4_000_000, bytes_accessed=8_000_000, transcendentals=0),
        )(*ins)

    def vmem(shape):
        return pltpu.VMEM(shape, jnp.float32)

    def pack(name, slots, plane_of, ins, later=()):
        kernel = functools.partial(pack_kernel, geo, slots, plane_of, len(ins))
        return call(name, kernel, (*ins, *later), [array(len(slots), yw, LANES)], [], len(later))[0]

    z_send = pack("pack_box", box_slots(bx), lambda item: (0, item[0] * bx + item[1]), (own, sib))
    z_in = facing(z_send)
    even_own, _ = lax.optimization_barrier((even_own, z_send))
    odd_own, _ = lax.optimization_barrier((odd_own, z_send))
    even_sib, odd_sib = sibling(even_own), sibling(odd_own)

    def halo_plane(item):
        pair, field, x = item
        first, count = (0, REACH_XB) if field == 0 else (REACH_XB, REACH_X)
        from_above = (lax.rem(lax.axis_index("gx"), 2) == 0) == (pair == 0)
        return pair, first + jnp.where(from_above, x - 1, count - x)

    zx_in = facing(pack("pack_halo", halo_slots(), halo_plane, (even_own, odd_own, even_sib, odd_sib), (z_in,)))

    wide0, wide1 = bx + 2 * WIN0, bx // 2 + 2 * WIN1
    x1, y1 = xw // 2, yw // 2
    some0 = vmem((xw + 2, yw, LANES))
    some1 = vmem((x1 + 2, y1, LANES))
    passed = array(6 * (wide0 + 1) + 3 * (wide1 + 1), yw, LANES)
    edge = 9
    ins = (own, sib, even_own, odd_own, even_sib, odd_sib, z_in, zx_in)
    sends = [array(nx * ny * nz if geo["packed"] else 2, by // 2, LANES), array(edge, y1, LANES), array(edge, y1, LANES)]
    down = call(
        "down", functools.partial(down_kernel, geo), ins, sends + [passed],
        [vmem(v.shape) for v in sends] + [some0] * 10 + [some1] * 11
        + [vmem((6, yw, LANES)), vmem((6, y1, LANES)), pltpu.SemaphoreType.DMA((15,))],
        hbm_outs=1, limit=VMEM_LIMIT, result=anywhere,
    )
    packed, even_send, odd_send, passed = down[0], down[1], down[2], down[3]
    from_even, from_odd = paired(even_send, 0), paired(odd_send, 1)

    if geo["packed"]:
        half = lax.all_to_all(packed, AXES, 0, 0, tiled=True)
        half, from_even, from_odd = lax.optimization_barrier((half, from_even, from_odd))
        gathered = (half, sibling(half))
    else:
        pieces = lax.all_gather(packed, AXES).reshape(nx, pairs, 2, nz, 2, by // 2, 8, 16)
        order = (jnp.arange(8) + 2 * jnp.arange(nz)[:, None, None] + jnp.arange(2)[:, None]) % 8
        order = jnp.transpose(order, (1, 0, 2))[None, None, :, :, None, None, :, None]
        pieces = jnp.take_along_axis(pieces, order, axis=6)
        gathered = (jnp.transpose(pieces, (4, 0, 6, 1, 5, 3, 2, 7)).reshape(2, geo["x2"], geo["y2"], geo["z2"]),)

    def level(planes, rows, lanes):
        return vmem((planes + 2, rows, lanes))

    x2, y2, z2 = geo["x2"], geo["y2"], geo["z2"]
    send_u, send_r, keep_u, keep_r = call(
        "up", functools.partial(up_kernel, geo), (*gathered, from_even, from_odd, passed), [array(bx, by, LANES)] * 4,
        [level(x2, y2, z2)] * 12 + [level(x2 // 2, y2, z2)] * 12 + [level(x2 // 4, y2, z2)] * 10
        + [level(wide1, y1, LANES)] * 11 + [level(wide0, yw, LANES)] * 10
        + [vmem((x2 + 8, y2 + 2 * geo["pad_y"], z2)), *(vmem(v.shape) for v in gathered), vmem(from_even.shape), vmem(from_odd.shape)]
        + [pltpu.SemaphoreType.DMA((20,))],
        hbm_ins=1, limit=VMEM_LIMIT, operand=anywhere, result=anywhere,
    )
    mine = lanes_of((1, 1, LANES)) // HALF == core
    return jnp.where(mine, keep_u, sibling(send_u)), jnp.where(mine, keep_r, sibling(send_r))


def solution(mesh):
    specs = (P(*AXES), P(*AXES))
    return jax.shard_map(on_device, mesh=mesh, in_specs=specs, out_specs=specs, check_vma=False)
```

```python
import functools
import math
import jax
import jax.numpy as jnp
from jax import lax
from jax.experimental import pallas as pl
from jax.experimental.pallas import tpu as pltpu
from jax.sharding import PartitionSpec as P

LEVELS = 4
STEPS = 3
COARSE_STEPS = 8
LOWER_EDGE = 0.3
UPPER_EDGE = 2.0

LANES = 128
HALF = 64
REACH_X = 12
REACH_XB = 9
REACH_Z = 20
WIN0 = 4
WIN1 = REACH_X // 2
VMEM_LIMIT = 48 * 1024 * 1024
AXES = ("gx", "gy", "gz")


def chebyshev_factors(sweeps):
    centre_value = 0.5 * (UPPER_EDGE + LOWER_EDGE)
    half_width = 0.5 * (UPPER_EDGE - LOWER_EDGE)
    ratio_value = centre_value / half_width
    damping = 1.0 / ratio_value
    factors = [(0.0, 1.0 / centre_value)]
    for _ in range(1, sweeps):
        damping_next = 1.0 / (2.0 * ratio_value - damping)
        factors.append((damping_next * damping, 2.0 * damping_next / half_width))
        damping = damping_next
    return factors


FACTORS = chebyshev_factors(STEPS)
COARSE_FACTORS = chebyshev_factors(COARSE_STEPS)


def chunks(count, body, size, first=1):
    if count == size:
        body(first)
    else:
        def step(i, carry):
            body(first + i * size)
            return carry
        lax.fori_loop(0, count // size, step, 0)


def rows_of(shape):
    return lax.broadcasted_iota(jnp.int32, shape, len(shape) - 2)


def lanes_of(shape):
    return lax.broadcasted_iota(jnp.int32, shape, len(shape) - 1)


class Grid:
    def __init__(self, x, y, z, sy, sz, whole_z, size):
        self.x, self.y, self.z, self.sy, self.sz = x, y, z, sy, sz
        self.whole_z, self.size = whole_z, size

    def up_y(self, v):
        return pltpu.roll(v, self.y - self.sy, v.ndim - 2)

    def down_y(self, v):
        return pltpu.roll(v, self.sy, v.ndim - 2)

    def up_z(self, v):
        return pltpu.roll(v, self.z - self.sz, v.ndim - 1)

    def down_z(self, v):
        return pltpu.roll(v, self.sz, v.ndim - 1)

    def setup(self, k_ref, cx, cy, cz, iv, ds, scale, after=None):
        cx[0] = 0.5 * (k_ref[0] + k_ref[1])

        def body(at):
            here = pl.ds(at, self.size)
            k = k_ref[here]
            row, lane = rows_of(k.shape), lanes_of(k.shape)
            k_next = k_ref[pl.ds(at + 1, self.size)]
            k_prev = k_ref[pl.ds(at - 1, self.size)]
            not_last = row < self.y - self.sy
            k_up = jnp.where(not_last, self.up_y(k), 0.0)
            k_down = jnp.where(row >= self.sy, self.down_y(k), 0.0)
            z_up, z_down = self.up_z(k), self.down_z(k)
            if self.whole_z:
                inner = lane < self.z - self.sz
                z_up = jnp.where(inner, z_up, 0.0)
                z_down = jnp.where(lane >= self.sz, z_down, 0.0)
            total = 3.0 * k + 0.5 * ((k_next + k_prev) + (k_up + k_down) + (z_up + z_down))
            inverse = jnp.where(k > 0.0, 1.0 / total, 0.0)
            cx[here] = 0.5 * (k + k_next)
            cy[here] = jnp.where(not_last, 0.5 * (k + k_up), 0.0)
            across = 0.5 * (k + z_up)
            cz[here] = jnp.where(inner, across, 0.0) if self.whole_z else across
            iv[here] = inverse
            if ds is not None:
                ds[here] = scale * total
            if after is not None:
                after(at, here, inverse)

        chunks(self.x, body, self.size)

    def step(self, coeffs, src, g_in, keep, push, out, first=1, count=None):
        cx, cy, cz, iv = coeffs

        def body(at):
            here = pl.ds(at, self.size)
            planes, x_coeff = src[pl.ds(at - 1, self.size + 2)], cx[pl.ds(at - 1, self.size + 1)]
            v = planes[1:-1]
            y_coeff, z_coeff = cy[here], cz[here]
            near = x_coeff[1:] * planes[2:] + x_coeff[:-1] * planes[:-2]
            near = near + (y_coeff * self.up_y(v) + self.down_y(y_coeff * v))
            near = near + (z_coeff * self.up_z(v) + self.down_z(z_coeff * v))
            g = g_in[here] - v + iv[here] * near
            out(here, v, g, None if push is None else (keep * v + push * g if keep else push * g))

        chunks(count or self.x, body, self.size, first)


def pair_z(v, shift, lanes):
    even = (lanes_of(v.shape) // shift) % 2 == 0
    return v + jnp.where(even, pltpu.roll(v, lanes - shift, v.ndim - 1), pltpu.roll(v, shift, v.ndim - 1))


def pair_y(v, shift, rows):
    even = (rows_of(v.shape) // shift) % 2 == 0
    return v + jnp.where(even, pltpu.roll(v, rows - shift, v.ndim - 2), pltpu.roll(v, shift, v.ndim - 2))


def spread_z(v, shift, lanes, whole):
    lane = lanes_of(v.shape)
    even = (lane // shift) % 2 == 0
    low, high = pltpu.roll(v, shift, v.ndim - 1), pltpu.roll(v, lanes - shift, v.ndim - 1)
    if whole:
        low = jnp.where(lane >= shift, low, 0.0)
        high = jnp.where(lane < lanes - shift, high, 0.0)
    return 0.75 * v + 0.25 * jnp.where(even, low, high)


def spread_y(v, shift, rows):
    row = rows_of(v.shape)
    even = (row // shift) % 2 == 0
    low = jnp.where(row >= shift, pltpu.roll(v, shift, v.ndim - 2), 0.0)
    high = jnp.where(row < rows - shift, pltpu.roll(v, rows - shift, v.ndim - 2), 0.0)
    return 0.75 * v + 0.25 * jnp.where(even, low, high)


def picked_lanes(v, pick):
    pick, total = pick.astype(jnp.bfloat16), None
    for _ in range(3):
        part = v.astype(jnp.bfloat16)
        v = v - part.astype(jnp.float32)
        product = jnp.dot(part, pick, preferred_element_type=jnp.float32)
        total = product if total is None else total + product
    return total


def zero_pads(*refs):
    for ref in refs:
        ref[0] = jnp.zeros(ref.shape[1:], jnp.float32)
        ref[ref.shape[0] - 1] = jnp.zeros(ref.shape[1:], jnp.float32)


def core_of():
    return lax.rem(lax.axis_index("gy"), 2)


def reaches():
    source1 = {0: WIN1 + 2, 1: WIN1 + 1, 2: WIN1, 3: 0}
    coeff1 = {a: max(source1.get(a, -1) + 1, source1.get(a - 1, -1), source1.get(a + 1, -1), min(WIN1, 7 - a)) for a in range(7)}
    residual0 = {0: 2 * source1[0]}
    coeff0 = {0: 2 * coeff1[0]}
    for a in range(1, 7):
        for x in (2 * a - 1, 2 * a):
            coeff0[x] = 2 * coeff1[a]
            if a in source1:
                residual0[x] = 2 * source1[a]

    def grown(steps, x):
        return max([z + steps - abs(x - at) for at, z in residual0.items() if abs(x - at) <= steps], default=0)

    source = [grown(3, x) for x in range(REACH_XB + 1)]
    coeff = [max(grown(4, x), coeff0[x]) for x in range(REACH_X + 1)]
    assert max(source + coeff) <= REACH_Z
    return source, coeff


def slots_of(items):
    rows, used = [], LANES
    for item, width in items:
        if width:
            if used + width > LANES:
                rows.append([])
                used = 0
            rows[-1].append((item, used, width))
            used += width
    return rows


def box_slots(bx):
    source, coeff = reaches()
    return slots_of([((0, p), source[0]) for p in range(bx)] + [((1, p), coeff[0]) for p in range(bx)])


def halo_slots():
    source, coeff = reaches()
    items = []
    for pair in range(2):
        items += [((pair, 0, x), source[x]) for x in range(1, REACH_XB + 1)]
        items += [((pair, 1, x), coeff[x]) for x in range(1, REACH_X + 1)]
    return slots_of(items)


def pack_kernel(geo, slots, plane_of, count, *refs):
    own, sib, z_out = refs[:count // 2], refs[count // 2:count], refs[-1]
    core, ye = core_of(), geo["ye"]
    lane = lanes_of((ye, LANES))
    for fields, half in ((own, core), (sib, 1 - core)):
        rows = pl.ds(pl.multiple_of(half * ye, 8), ye)
        for m, row in enumerate(slots):
            packed = jnp.zeros((ye, LANES), jnp.float32)
            for item, at, width in row:
                shift = jnp.where(core == 1, (at + width) % LANES, at)
                field, plane = plane_of(item)
                packed = jnp.where((lane >= at) & (lane < at + width), pltpu.roll(fields[field][plane], shift, 1), packed)
            z_out[m, rows] = packed


def passed_views(geo, ref):
    wide0, wide1, rows = geo["bx"] + 2 * WIN0, geo["bx"] // 2 + 2 * WIN1, geo["yw"] // 2
    views, at = [], 0
    for i in range(6):
        views.append(ref.at[pl.ds(at, wide0 + (i == 0))])
        at += wide0 + 1
    for i in range(6):
        views.append(ref.at[pl.ds(at + i // 2 * (wide1 + 1), wide1 + (i == 0)), pl.ds(i % 2 * rows, rows)])
    return views


def down_kernel(geo, *refs):
    (own_in, sib_in, even_own, odd_own, even_sib, odd_sib, z_in, zx_in, packed_any, even_any, odd_any, passed,
     packed_out, even_out, odd_out,
     k0, cx, cy, cz, iv, ds, g0, g, d1, d2,
     k1, ex, ey, ez, ei, es, h0, h, f1, f2, u1, half_y, half_y1, sems) = refs
    core = core_of()
    ix, nx = lax.axis_index("gx"), lax.axis_size("gx")
    iz, nz = lax.axis_index("gz"), lax.axis_size("gz")
    bx, ye, yw, xw = geo["bx"], geo["ye"], geo["yw"], geo["xw"]
    z_there = jnp.where(core == 0, iz > 0, iz < nz - 1)
    lo_there, hi_there = ix > 0, ix < nx - 1
    even = lax.rem(ix, 2) == 0

    lane = lanes_of((yw, LANES))

    def strip(ref, m, at, width):
        shift = jnp.where(core == 0, (2 * LANES - width - at) % LANES, (LANES - at) % LANES)
        return pltpu.roll(ref[m], shift, 1)

    def merge(window, at, width, there, moved):
        halo = jnp.where(core == 0, lane - (LANES - width), width - 1 - lane) >= 0
        window[at] = jnp.where(halo, jnp.where(there, moved, 0.0), window[at])

    own_rows = pl.ds(pl.multiple_of(core * ye, 8), ye)
    sib_rows = pl.ds(pl.multiple_of((1 - core) * ye, 8), ye)
    zero_pads(k0, d1, d2, k1, f1, f2)
    windows = ((g0, 0, REACH_XB, 0), (k0, bx, REACH_X, REACH_XB))
    for p in range(REACH_X - REACH_XB):
        g0[1 + p] = jnp.zeros((yw, LANES), jnp.float32)
        g0[xw - p] = jnp.zeros((yw, LANES), jnp.float32)

    def halos(from_even, from_odd, rows):
        for window, _, width, at in windows:
            e, o = from_even[pl.ds(at, width)], from_odd[pl.ds(at, width)]
            window[pl.ds(1 + REACH_X - width, width), rows] = jnp.where(lo_there, jnp.where(even, o, e), 0.0)
            window[pl.ds(1 + REACH_X + bx, width), rows] = jnp.where(hi_there, jnp.where(even, e, o), 0.0)

    for window, at, _, _ in windows:
        window[pl.ds(1 + REACH_X, bx), own_rows] = own_in[pl.ds(at, bx)]
        window[pl.ds(1 + REACH_X, bx), sib_rows] = sib_in[pl.ds(at, bx)]
    halos(even_own, odd_own, own_rows)
    halos(even_sib, odd_sib, sib_rows)
    for m, row in enumerate(box_slots(bx)):
        for (f, p), at, width in row:
            merge(windows[f][0], 1 + REACH_X + p, width, z_there, strip(z_in, m, at, width))
    places = {item: (m, at, width) for m, row in enumerate(halo_slots()) for item, at, width in row}
    for (pair, f, x), place in places.items():
        if pair == 0:
            window, width = windows[f][0], place[2]
            e, o = strip(zx_in, *place), strip(zx_in, *places[1, f, x])
            merge(window, 1 + REACH_X - x, width, z_there & lo_there, jnp.where(even, o, e))
            merge(window, REACH_X + bx + x, width, z_there & hi_there, jnp.where(even, e, o))

    grid = Grid(xw, yw, LANES, 1, 1, False, geo["chunk0"])
    inner = Grid(xw - 8, yw, LANES, 1, 1, False, geo["chunk0_inner"])
    nothing = jnp.zeros((4, yw, LANES), jnp.float32)
    for ref in (g, d2):
        ref[pl.ds(1, 4)] = nothing
        ref[pl.ds(xw - 3, 4)] = nothing

    def first(at, here, inverse):
        scaled = g0[here] * inverse
        g0[here] = scaled
        d1[here] = FACTORS[0][1] * scaled

    grid.setup(k0, cx, cy, cz, iv, ds, 1.0, first)
    own0 = 1 + REACH_X - WIN0
    wide0 = bx + 2 * WIN0
    copies = []

    views = passed_views(geo, passed)

    def send(source, start, count):
        i = len(copies)
        copy = pltpu.make_async_copy(source.at[pl.ds(start, count)], views[i], sems.at[i])
        copy.start()
        copies.append(copy)

    send(cx, own0 - 1, wide0 + 1)
    send(cy, own0, wide0)
    send(cz, own0, wide0)
    send(iv, own0, wide0)
    send(g0, own0, wide0)

    def restrict(source, target, tmp, x_count, at, y_first, y_rows, shift):
        for i in range(x_count):
            j = i % tmp.shape[0]
            v = source[at + 2 * i] + source[at + 2 * i + 1]
            tmp[j] = v + pltpu.roll(v, v.shape[0] - 1, 0)
            v = tmp[j, pl.ds(y_first, y_rows // 2, stride=2)]
            target(i, 0.125 * pair_z(v, shift, LANES))

    x1, y1 = xw // 2, yw // 2

    def put_k1(i, v):
        k1[1 + i] = v

    def put_b1(i, v):
        h0[1 + i] = v

    restrict(k0, put_k1, half_y, x1, 1, 0, yw, 1)
    coeffs = (cx, cy, cz, iv)

    def second(here, v, value, direction):
        g[here] = value
        d2[here] = direction

    inner.step(coeffs, d1, g0, *FACTORS[1], second, 5)

    def third(here, v, value, direction):
        g[here] = value
        k0[here] = d1[here] + v + direction
        d1[here] = direction

    inner.step(coeffs, d2, g, *FACTORS[2], third, 5)
    send(k0, own0, wide0)

    def residual(here, v, value, direction):
        g[here] = value * ds[here]

    inner.step(coeffs, d1, g, 0.0, None, residual, 5)

    restrict(g, put_b1, half_y, x1, 1, 0, yw, 1)
    grid1 = Grid(x1, y1, LANES, 1, 2, False, geo["chunk1"])

    def first1(at, here, inverse):
        scaled = 4.0 * (h0[here] * inverse)
        h0[here] = scaled
        f1[here] = FACTORS[0][1] * scaled

    grid1.setup(k1, ex, ey, ez, ei, es, 0.25, first1)
    own1 = 1 + REACH_X // 2 - WIN1
    wide1 = bx // 2 + 2 * WIN1
    send(ex, own1 - 1, wide1 + 1)
    send(ey, own1, wide1)
    send(ez, own1, wide1)
    send(ei, own1, wide1)
    send(h0, own1, wide1)
    coeffs1 = (ex, ey, ez, ei)

    def second1(here, v, value, direction):
        h[here] = value
        f2[here] = direction

    grid1.step(coeffs1, f1, h0, *FACTORS[1], second1)

    def third1(here, v, value, direction):
        h[here] = value
        u1[here] = f1[here] + v + direction
        f1[here] = direction

    grid1.step(coeffs1, f2, h, *FACTORS[2], third1)
    send(u1, own1, wide1)
    mine = 1 + REACH_X // 2
    last = mine + bx // 2
    for source, low, high, at, count in ((u1, mine, last - WIN1, 0, 6), (h0, mine + 2, last - 5, 6, 3)):
        low, high = source[pl.ds(low, count)], source[pl.ds(high, count)]
        even_out[pl.ds(at, count)] = jnp.where(even, high, low)
        odd_out[pl.ds(at, count)] = jnp.where(even, low, high)

    def leave(source, target):
        copy = pltpu.make_async_copy(source, target, sems.at[len(copies)])
        copy.start()
        copies.append(copy)

    leave(even_out, even_any)
    leave(odd_out, odd_any)

    def residual1(here, v, value, direction):
        h[here] = value * es[here]

    grid1.step(coeffs1, f1, h, 0.0, None, residual1)

    place = lax.rem(2 * iz + core, 8)
    x2, y2 = bx // 4, geo["by"] // 2
    row, column = rows_of((LANES, LANES)), lanes_of((LANES, LANES))
    pick = (row == HALF * core + 4 * lax.rem(column, 16)).astype(jnp.float32)
    slot = lanes_of((y2, LANES)) // 16
    for f, source in enumerate((h, k1)):
        boxes = []
        restrict(source, lambda i, v, boxes=boxes: boxes.append(v), half_y1, x2, 1 + REACH_X // 2, geo["oy"] // 2, 2 * y2, 2)
        stacked = jnp.concatenate(boxes, axis=0)
        picked = picked_lanes(stacked, pick)
        packed = jnp.zeros((y2, LANES), jnp.float32)
        for p in range(x2):
            packed = jnp.where(slot == lax.rem(p + place, 8), picked[p * y2:(p + 1) * y2], packed)
        if geo["packed"]:
            for j in range(packed_out.shape[0]):
                if (j // nz) % 2 == f:
                    packed_out[j] = packed
        else:
            packed_out[f] = packed
    leave(packed_out, packed_any)
    for copy in copies:
        copy.wait()


def up_kernel(geo, *refs):
    refs = list(refs)

    def take(count):
        taken = refs[:count]
        del refs[:count]
        return taken

    count = 2 if geo["packed"] else 1
    arriving = take(count + 2)
    views = passed_views(geo, take(1)[0])
    in0, in1 = views[:6], views[6:]
    send_u, send_r, keep_u, keep_r = take(4)
    k2, cx2, cy2, cz2, iv2, ds2, g02, g2, da2, db2, w2, e2 = take(12)
    k3, cx3, cy3, cz3, iv3, ds3, g03, g3, da3, db3, w3, e3 = take(12)
    k4, cx4, cy4, cz4, iv4, g04, g4, da4, db4, e4 = take(10)
    cx1, cy1, cz1, iv1, g01, w1, u1, g1, da1, db1, e1 = take(11)
    cx0, cy0, cz0, iv0, g00, w0, u0, g0, da0, db0 = take(10)
    e2_wide, spread1, spread0 = take(3)
    gathered = take(count)
    from_even, from_odd, sems = take(3)
    core = core_of()
    ix, nx = lax.axis_index("gx"), lax.axis_size("gx")
    iz, nz = lax.axis_index("gz"), lax.axis_size("gz")
    yp = lax.axis_index("gy") // 2
    bx, by, yw = geo["bx"], geo["by"], geo["yw"]
    x2, y2, z2 = geo["x2"], geo["y2"], geo["z2"]
    wide0, wide1 = bx + 2 * WIN0, bx // 2 + 2 * WIN1

    arrivals = []
    for source, target in zip(arriving, (*gathered, from_even, from_odd)):
        arrivals.append(pltpu.make_async_copy(source, target, sems.at[16 + len(arrivals)]))
        arrivals[-1].start()
    copies = []
    for sources, targets, wide in ((in1, (cx1, cy1, cz1, iv1, g01, w1), wide1), (in0, (cx0, cy0, cz0, iv0, g00, w0), wide0)):
        for i, (source, target) in enumerate(zip(sources, targets)):
            there = target.at[pl.ds(0, wide + 1)] if i == 0 else target.at[pl.ds(1, wide)]
            copy = pltpu.make_async_copy(source, there, sems.at[len(copies)])
            copy.start()
            copies.append(copy)

    zero_pads(k2, da2, db2, e2, k3, da3, db3, e3, k4, da4, db4, e4, u1, da1, db1, u0, da0, db0)

    for copy in arrivals:
        copy.wait()
    if geo["packed"]:
        slot = lanes_of((y2, LANES)) // 16
        for gx in range(nx):
            for f, target in ((0, g02), (1, k2)):
                for p in range(8):
                    merged = jnp.zeros((y2, LANES), jnp.float32)
                    for gz in range(nz):
                        for cc in range(2):
                            at = (2 * gx + cc) * nz + gz
                            here = jnp.where(core == f, gathered[0][at], gathered[1][at])
                            merged = jnp.where(slot == (p + 2 * gz + cc) % 8, here, merged)
                    target[1 + 8 * gx + p] = pltpu.roll(merged, (LANES - 16 * p) % LANES, 1)
    else:
        g02[pl.ds(1, x2)] = gathered[0][0]
        k2[pl.ds(1, x2)] = gathered[0][1]

    def descend(grid, level, k, cx, cy, cz, iv, ds, g0, first_target):
        def first(at, here, inverse):
            scaled = 4.0**level * (g0[here] * inverse)
            g0[here] = scaled
            first_target[here] = FACTORS[0][1] * scaled

        grid.setup(k, cx, cy, cz, iv, ds, 0.25**level, first)

    def pre(grid, level, k, cx, cy, cz, iv, ds, g0, g, da, db, w):
        descend(grid, level, k, cx, cy, cz, iv, ds, g0, da)
        coeffs = (cx, cy, cz, iv)

        def second(here, v, value, direction):
            g[here] = value
            db[here] = direction

        grid.step(coeffs, da, g0, *FACTORS[1], second)

        def third(here, v, value, direction):
            g[here] = value
            w[here] = da[here] + v + direction
            da[here] = direction

        grid.step(coeffs, db, g, *FACTORS[2], third)

        def residual(here, v, value, direction):
            g[here] = value * ds[here]

        grid.step(coeffs, da, g, 0.0, None, residual)

    def post(grid, coeffs, g0, u, g, da, db, result, shrink=0):
        def step(i, *args):
            part = Grid(grid.x - 2 * i * shrink, grid.y, grid.z, grid.sy, grid.sz, grid.whole_z, grid.size)
            if shrink:
                part.size = part.x if grid.size == grid.x else 2
            part.step(coeffs, *args, 1 + i * shrink)

        def one(here, v, value, direction):
            g[here] = value
            da[here] = direction

        step(1, u, g0, *FACTORS[0], one)

        def two(here, v, value, direction):
            g[here] = value
            db[here] = direction

        step(2, da, g, *FACTORS[1], two)

        def three(here, v, value, direction):
            g[here] = value
            result[here] = u[here] + da[here] + v + direction
            da[here] = direction

        step(3, db, g, *FACTORS[2], three)

    def restrict(fine, coarse, count, shift):
        for i in range(count):
            v = fine[1 + 2 * i] + fine[2 + 2 * i]
            coarse[1 + i] = 0.125 * pair_z(pair_y(v, shift, y2), shift, z2)

    def prolong(coarse, w, target, count, shift):
        for i in range(count):
            middle = 0.75 * coarse[1 + i]
            for j, side in ((0, coarse[i]), (1, coarse[2 + i])):
                v = spread_y(middle + 0.25 * side, shift, y2)
                target[1 + 2 * i + j] = w[1 + 2 * i + j] + spread_z(v, shift, z2, True)

    def size_of(x):
        planes = max(1, 32 // ((y2 // 8) * (z2 // LANES)))
        return min(x, planes)

    x3, x4 = x2 // 2, x2 // 4
    grid2 = Grid(x2, y2, z2, 1, 1, True, size_of(x2))
    grid3 = Grid(x3, y2, z2, 2, 2, True, size_of(x3))
    grid4 = Grid(x4, y2, z2, 4, 4, True, size_of(x4))
    pre(grid2, 2, k2, cx2, cy2, cz2, iv2, ds2, g02, g2, da2, db2, w2)
    restrict(k2, k3, x3, 1)
    restrict(g2, g03, x3, 1)
    pre(grid3, 3, k3, cx3, cy3, cz3, iv3, ds3, g03, g3, da3, db3, w3)
    restrict(k3, k4, x4, 2)
    restrict(g3, g04, x4, 2)
    descend(grid4, 4, k4, cx4, cy4, cz4, iv4, None, g04, da4)
    e4[pl.ds(1, x4)] = da4[pl.ds(1, x4)]
    for sweep in range(1, COARSE_STEPS):
        src, dst = (da4, db4) if sweep % 2 else (db4, da4)

        def coarse(here, v, value, direction):
            g4[here] = value
            dst[here] = direction
            e4[here] = e4[here] + direction

        grid4.step((cx4, cy4, cz4, iv4), src, g04 if sweep == 1 else g4, *COARSE_FACTORS[sweep], coarse)
    prolong(e4, w3, e3, x4, 2)
    post(grid3, (cx3, cy3, cz3, iv3), g03, e3, g3, da3, db3, w3)
    e3[pl.ds(1, x3)] = w3[pl.ds(1, x3)]
    prolong(e3, w2, e2, x3, 1)
    post(grid2, (cx2, cy2, cz2, iv2), g02, e2, g2, da2, db2, w2)

    pad_y = geo["pad_y"]
    if pad_y:
        e2_wide[...] = jnp.zeros(e2_wide.shape, jnp.float32)
    else:
        edge = jnp.zeros((4,) + e2_wide.shape[1:], jnp.float32)
        e2_wide[pl.ds(0, 4)] = edge
        e2_wide[pl.ds(x2 + 4, 4)] = edge
    e2_wide[pl.ds(4, x2), pl.ds(pad_y, y2)] = w2[pl.ds(1, x2)]
    x2w, y2w = bx // 4 + 8, yw // 4
    cells, lane = rows_of((z2, LANES)), lanes_of((z2, LANES))
    shifted = jnp.where(core == 0, jnp.where(lane >= 104, -32, 0), jnp.where(lane < 24, 32, 0))
    pick = (cells == 32 * iz + lane // 4 + shifted).astype(jnp.float32)
    start = (bx // 4) * ix
    rows = pl.ds(pl.multiple_of(8 * yp, 8), y2w) if pad_y else pl.ds(0, y2w)
    window = e2_wide[pl.ds(start, x2w), rows].reshape(x2w * y2w, z2)
    window = picked_lanes(window, pick)
    window = window.reshape(x2w, y2w, LANES)

    def place_rows(target, plane, v, count):
        row = rows_of(v.shape)
        low = jnp.where(row >= 1, pltpu.roll(v, 1, 0), 0.0)
        high = jnp.where(row < count - 1, pltpu.roll(v, count - 1, 0), 0.0)
        target[plane, pl.ds(0, count, stride=2)] = 0.75 * v + 0.25 * low
        target[plane, pl.ds(1, count, stride=2)] = 0.75 * v + 0.25 * high

    for copy in copies[:6]:
        copy.wait()
    even, last1 = lax.rem(ix, 2) == 0, 1 + WIN1 + bx // 2
    for target, low, high, at, count in ((w1, 1, last1, 0, 6), (g01, 2, last1 + 2, 6, 3)):
        e, o = from_even[pl.ds(at, count)], from_odd[pl.ds(at, count)]
        low, high = pl.ds(low, count), pl.ds(high, count)
        target[low] = jnp.where(ix > 0, jnp.where(even, o, e), target[low])
        target[high] = jnp.where(ix < nx - 1, jnp.where(even, e, o), target[high])
    for plane in range(wide1):
        j = plane // 2
        v = 0.75 * window[j + 1] + 0.25 * window[j + 2 if plane % 2 else j]
        place_rows(spread1, 1 + plane, spread_z(v, 2, LANES, False), y2w)
    grid1 = Grid(wide1, yw // 2, LANES, 1, 2, False, geo["chunk1"])

    def start1(at):
        here = pl.ds(at, grid1.size)
        u1[here] = jnp.where(iv1[here] > 0.0, w1[here] + spread1[here, pl.ds(0, yw // 2)], 0.0)

    chunks(wide1, start1, grid1.size)
    post(grid1, (cx1, cy1, cz1, iv1), g01, u1, g1, da1, db1, e1, 1)

    for copy in copies[6:]:
        copy.wait()
    grid0 = Grid(wide0, yw, LANES, 1, 1, False, geo["chunk_up"])

    def fill(i, carry):
        at = WIN1 + 1 - WIN0 // 2 + i
        middle = 0.75 * e1[at]
        for j, side in ((0, e1[at - 1]), (1, e1[at + 1])):
            place_rows(spread0, 1 + 2 * i + j, spread_z(middle + 0.25 * side, 1, LANES, False), yw // 2)
        return carry

    lax.fori_loop(0, wide0 // 2, fill, 0, unroll=10)

    def start0(at):
        here = pl.ds(at, grid0.size)
        u0[here] = jnp.where(iv0[here] > 0.0, w0[here] + spread0[here, pl.ds(0, yw)], 0.0)

    chunks(wide0, start0, grid0.size)
    coeffs0 = (cx0, cy0, cz0, iv0)
    post(grid0, coeffs0, g00, u0, g0, da0, db0, w0, 1)

    own = pl.ds(1 + WIN0, bx)
    own_rows = pl.ds(pl.multiple_of(geo["oy"] + core * by, 8), by)
    sib_rows = pl.ds(pl.multiple_of(geo["oy"] + (1 - core) * by, 8), by)
    leaving = []

    def leave(source, rows, target):
        copy = pltpu.make_async_copy(source.at[own, rows], target, sems.at[12 + len(leaving)])
        copy.start()
        leaving.append(copy)

    leave(w0, sib_rows, send_u)
    leave(w0, own_rows, keep_u)

    def residual(here, v, value, direction):
        g0[here] = value / iv0[here]

    Grid(bx, yw, LANES, 1, 1, False, geo["chunk_last"]).step(coeffs0, da0, g0, 0.0, None, residual, 1 + WIN0)
    leave(g0, sib_rows, send_r)
    leave(g0, own_rows, keep_r)
    for copy in leaving:
        copy.wait()


def array(*shape):
    return jax.ShapeDtypeStruct(shape, jnp.float32)


def on_device(right_side, conductivity):
    bx, by, bz = right_side.shape
    nx, ny, nz = (lax.axis_size(axis) for axis in AXES)
    pairs = ny // 2
    ix, iy, iz = (lax.axis_index(axis) for axis in AXES)
    core = iy % 2

    def index(x, p, c, z):
        return ((x % nx) * ny + (p % pairs) * 2 + c) * nz + z % nz

    every = [(x, p, z) for x in range(nx) for p in range(pairs) for z in range(nz)]

    def sibling(v):
        return lax.ppermute(v, "gy", [(i, i ^ 1) for i in range(ny)])

    def xor(v, axis, k):
        return lax.ppermute(v, axis, [(i, i ^ k) for i in range(lax.axis_size(axis))])

    def paired(v, first):
        perm = [(i, i) for i in range(nx)]
        for i in range(first, nx - 1, 2):
            perm[i], perm[i + 1] = (i, i + 1), (i + 1, i)
        return lax.ppermute(v, "gx", perm)

    def facing(v):
        perm = {}
        for x, p, z in every:
            if z > 0:
                a, b = index(x, p, 0, z), index(x, p, 1, z - 1)
                perm[a], perm[b] = b, a
        return lax.ppermute(v, AXES, [(i, perm.get(i, i)) for i in range(nx * ny * nz)])

    own_b, own_k, ye = right_side, conductivity, by
    if ny > 2:
        near = []
        far = []
        for p in range(pairs):
            near += [(2 * p, 2 * ((p - 1) % pairs) + 1), (2 * ((p - 1) % pairs) + 1, 2 * p)]
            far += [(2 * p, 2 * ((p + 1) % pairs)), (2 * p + 1, 2 * ((p - 1) % pairs) + 1)]
        there = jnp.where(core == 0, iy > 0, iy < ny - 1)

        def widened(v):
            one = jnp.where(there, lax.ppermute(v, "gy", near), 0.0)
            two = jnp.where(there, lax.ppermute(v, "gy", far), 0.0)
            return jnp.where(core == 0, jnp.concatenate([two, one, v], 1), jnp.concatenate([v, one, two], 1))

        own_b, own_k = widened(own_b), widened(own_k)
        ye = 3 * by
    yw = 2 * ye
    xw = bx + 2 * REACH_X
    geo = dict(
        bx=bx, by=by, ye=ye, yw=yw, xw=xw, oy=(yw - 2 * by) // 2, chunk0=56 if yw == 32 else 4, chunk0_inner=48 if yw == 32 else 4,
        chunk_up=40 if yw == 32 else 4, chunk_last=32 if yw == 32 else 4, chunk1=28 if yw == 32 else 4,
        packed=pairs == 1 and 32 * nz == LANES, x2=bx // 4 * nx, y2=by // 4 * ny, z2=bz // 4 * nz,
        pad_y=(yw // 4 - by // 2) // 2,
    )

    own = lax.optimization_barrier(jnp.concatenate([own_b, own_k], 0))
    even = ix % 2 == 0
    high = jnp.concatenate([own[bx - REACH_XB:bx], own[2 * bx - REACH_X:]], 0)
    low = jnp.concatenate([own[:REACH_XB], own[bx:bx + REACH_X]], 0)
    even_own = paired(jnp.where(even, high, low), 0)
    sib, odd_send = lax.optimization_barrier((sibling(own), jnp.where(even, low, high)))
    odd_own = paired(odd_send, 1)
    inside, hbm, anywhere = (pl.BlockSpec(memory_space=space) for space in (pltpu.VMEM, pltpu.HBM, pl.ANY))

    def call(name, kernel, ins, outs, scratch, hbm_ins=0, hbm_outs=0, limit=0, operand=inside, result=inside):
        held = sum(4 * math.prod(v.shape) for v in (*ins, *outs, *scratch) if v.dtype == jnp.float32)
        return pl.pallas_call(
            kernel, out_shape=outs, in_specs=[operand] * (len(ins) - hbm_ins) + [hbm] * hbm_ins,
            out_specs=[result] * (len(outs) - hbm_outs) + [hbm] * hbm_outs,
            scratch_shapes=scratch, name=name,
            compiler_params=pltpu.CompilerParams(vmem_limit_bytes=max(limit, held + 6 * 1024 * 1024)),
            cost_estimate=pl.CostEstimate(flops=4_000_000, bytes_accessed=8_000_000, transcendentals=0),
        )(*ins)

    def vmem(shape):
        return pltpu.VMEM(shape, jnp.float32)

    def pack(name, slots, plane_of, ins, later=()):
        kernel = functools.partial(pack_kernel, geo, slots, plane_of, len(ins))
        return call(name, kernel, (*ins, *later), [array(len(slots), yw, LANES)], [], len(later))[0]

    z_send = pack("pack_box", box_slots(bx), lambda item: (0, item[0] * bx + item[1]), (own, sib))
    z_in = facing(z_send)
    even_own, _ = lax.optimization_barrier((even_own, z_send))
    odd_own, _ = lax.optimization_barrier((odd_own, z_send))
    even_sib, odd_sib = sibling(even_own), sibling(odd_own)

    def halo_plane(item):
        pair, field, x = item
        first, count = (0, REACH_XB) if field == 0 else (REACH_XB, REACH_X)
        from_above = (lax.rem(lax.axis_index("gx"), 2) == 0) == (pair == 0)
        return pair, first + jnp.where(from_above, x - 1, count - x)

    zx_in = facing(pack("pack_halo", halo_slots(), halo_plane, (even_own, odd_own, even_sib, odd_sib), (z_in,)))

    wide0, wide1 = bx + 2 * WIN0, bx // 2 + 2 * WIN1
    x1, y1 = xw // 2, yw // 2
    some0 = vmem((xw + 2, yw, LANES))
    some1 = vmem((x1 + 2, y1, LANES))
    passed = array(6 * (wide0 + 1) + 3 * (wide1 + 1), yw, LANES)
    edge = 9
    ins = (own, sib, even_own, odd_own, even_sib, odd_sib, z_in, zx_in)
    sends = [array(nx * ny * nz if geo["packed"] else 2, by // 2, LANES), array(edge, y1, LANES), array(edge, y1, LANES)]
    down = call(
        "down", functools.partial(down_kernel, geo), ins, sends + [passed],
        [vmem(v.shape) for v in sends] + [some0] * 10 + [some1] * 11
        + [vmem((6, yw, LANES)), vmem((6, y1, LANES)), pltpu.SemaphoreType.DMA((15,))],
        hbm_outs=1, limit=VMEM_LIMIT, result=anywhere,
    )
    packed, even_send, odd_send, passed = down[0], down[1], down[2], down[3]
    from_even, from_odd = paired(even_send, 0), paired(odd_send, 1)

    if geo["packed"]:
        half = lax.all_to_all(packed, AXES, 0, 0, tiled=True)
        half, from_even, from_odd = lax.optimization_barrier((half, from_even, from_odd))
        gathered = (half, sibling(half))
    else:
        pieces = lax.all_gather(packed, AXES).reshape(nx, pairs, 2, nz, 2, by // 2, 8, 16)
        order = (jnp.arange(8) + 2 * jnp.arange(nz)[:, None, None] + jnp.arange(2)[:, None]) % 8
        order = jnp.transpose(order, (1, 0, 2))[None, None, :, :, None, None, :, None]
        pieces = jnp.take_along_axis(pieces, order, axis=6)
        gathered = (jnp.transpose(pieces, (4, 0, 6, 1, 5, 3, 2, 7)).reshape(2, geo["x2"], geo["y2"], geo["z2"]),)

    def level(planes, rows, lanes):
        return vmem((planes + 2, rows, lanes))

    x2, y2, z2 = geo["x2"], geo["y2"], geo["z2"]
    send_u, send_r, keep_u, keep_r = call(
        "up", functools.partial(up_kernel, geo), (*gathered, from_even, from_odd, passed), [array(bx, by, LANES)] * 4,
        [level(x2, y2, z2)] * 12 + [level(x2 // 2, y2, z2)] * 12 + [level(x2 // 4, y2, z2)] * 10
        + [level(wide1, y1, LANES)] * 11 + [level(wide0, yw, LANES)] * 10
        + [vmem((x2 + 8, y2 + 2 * geo["pad_y"], z2)), level(wide1, y1 + 8, LANES), level(wide0, yw + 8, LANES), *(vmem(v.shape) for v in gathered), vmem(from_even.shape), vmem(from_odd.shape)]
        + [pltpu.SemaphoreType.DMA((20,))],
        hbm_ins=1, limit=VMEM_LIMIT, operand=anywhere, result=anywhere,
    )
    mine = lanes_of((1, 1, LANES)) // HALF == core
    return jnp.where(mine, keep_u, sibling(send_u)), jnp.where(mine, keep_r, sibling(send_r))


def solution(mesh):
    specs = (P(*AXES), P(*AXES))
    return jax.shard_map(on_device, mesh=mesh, in_specs=specs, out_specs=specs, check_vma=False)
```

```python
import functools
import math
import jax
import jax.numpy as jnp
from jax import lax
from jax.experimental import pallas as pl
from jax.experimental.pallas import tpu as pltpu
from jax.sharding import PartitionSpec as P

LEVELS = 4
STEPS = 3
COARSE_STEPS = 8
LOWER_EDGE = 0.3
UPPER_EDGE = 2.0

LANES = 128
HALF = 64
REACH_X = 12
REACH_XB = 9
REACH_Z = 20
WIN0 = 4
WIN1 = REACH_X // 2
VMEM_LIMIT = 48 * 1024 * 1024
AXES = ("gx", "gy", "gz")


def chebyshev_factors(sweeps):
    centre_value = 0.5 * (UPPER_EDGE + LOWER_EDGE)
    half_width = 0.5 * (UPPER_EDGE - LOWER_EDGE)
    ratio_value = centre_value / half_width
    damping = 1.0 / ratio_value
    factors = [(0.0, 1.0 / centre_value)]
    for _ in range(1, sweeps):
        damping_next = 1.0 / (2.0 * ratio_value - damping)
        factors.append((damping_next * damping, 2.0 * damping_next / half_width))
        damping = damping_next
    return factors


FACTORS = chebyshev_factors(STEPS)
COARSE_FACTORS = chebyshev_factors(COARSE_STEPS)


def chunks(count, body, size, first=1):
    if count == size:
        body(first)
    else:
        def step(i, carry):
            body(first + i * size)
            return carry
        lax.fori_loop(0, count // size, step, 0)


def rows_of(shape):
    return lax.broadcasted_iota(jnp.int32, shape, len(shape) - 2)


def lanes_of(shape):
    return lax.broadcasted_iota(jnp.int32, shape, len(shape) - 1)


class Grid:
    def __init__(self, x, y, z, sy, sz, whole_z, size):
        self.x, self.y, self.z, self.sy, self.sz = x, y, z, sy, sz
        self.whole_z, self.size = whole_z, size

    def part(self, less):
        x = self.x - 2 * less
        return Grid(x, self.y, self.z, self.sy, self.sz, self.whole_z, x if self.size == self.x else 2)

    def up_y(self, v):
        return pltpu.roll(v, self.y - self.sy, v.ndim - 2)

    def down_y(self, v):
        return pltpu.roll(v, self.sy, v.ndim - 2)

    def up_z(self, v):
        return pltpu.roll(v, self.z - self.sz, v.ndim - 1)

    def down_z(self, v):
        return pltpu.roll(v, self.sz, v.ndim - 1)

    def setup(self, k_ref, cx, cy, cz, iv, ds, scale, after=None):
        cx[0] = 0.5 * (k_ref[0] + k_ref[1])

        def body(at):
            here = pl.ds(at, self.size)
            k = k_ref[here]
            row, lane = rows_of(k.shape), lanes_of(k.shape)
            k_next = k_ref[pl.ds(at + 1, self.size)]
            k_prev = k_ref[pl.ds(at - 1, self.size)]
            not_last = row < self.y - self.sy
            k_up = jnp.where(not_last, self.up_y(k), 0.0)
            k_down = jnp.where(row >= self.sy, self.down_y(k), 0.0)
            z_up, z_down = self.up_z(k), self.down_z(k)
            if self.whole_z:
                inner = lane < self.z - self.sz
                z_up = jnp.where(inner, z_up, 0.0)
                z_down = jnp.where(lane >= self.sz, z_down, 0.0)
            total = 3.0 * k + 0.5 * ((k_next + k_prev) + (k_up + k_down) + (z_up + z_down))
            inverse = jnp.where(k > 0.0, 1.0 / total, 0.0)
            cx[here] = 0.5 * (k + k_next)
            cy[here] = jnp.where(not_last, 0.5 * (k + k_up), 0.0)
            across = 0.5 * (k + z_up)
            cz[here] = jnp.where(inner, across, 0.0) if self.whole_z else across
            iv[here] = inverse
            if ds is not None:
                ds[here] = scale * total
            if after is not None:
                after(at, here, inverse)

        chunks(self.x, body, self.size)

    def step(self, coeffs, src, g_in, keep, push, out, first=1, count=None):
        cx, cy, cz, iv = coeffs

        def body(at):
            here = pl.ds(at, self.size)
            planes, x_coeff = src[pl.ds(at - 1, self.size + 2)], cx[pl.ds(at - 1, self.size + 1)]
            v = planes[1:-1]
            y_coeff, z_coeff = cy[here], cz[here]
            near = x_coeff[1:] * planes[2:] + x_coeff[:-1] * planes[:-2]
            near = near + (y_coeff * self.up_y(v) + self.down_y(y_coeff * v))
            near = near + (z_coeff * self.up_z(v) + self.down_z(z_coeff * v))
            g = g_in[here] - v + iv[here] * near
            out(here, v, g, None if push is None else (keep * v + push * g if keep else push * g))

        chunks(count or self.x, body, self.size, first)


def pair_z(v, shift, lanes):
    even = (lanes_of(v.shape) // shift) % 2 == 0
    return v + jnp.where(even, pltpu.roll(v, lanes - shift, v.ndim - 1), pltpu.roll(v, shift, v.ndim - 1))


def pair_y(v, shift, rows):
    even = (rows_of(v.shape) // shift) % 2 == 0
    return v + jnp.where(even, pltpu.roll(v, rows - shift, v.ndim - 2), pltpu.roll(v, shift, v.ndim - 2))


def spread_z(v, shift, lanes, whole):
    lane = lanes_of(v.shape)
    even = (lane // shift) % 2 == 0
    low, high = pltpu.roll(v, shift, v.ndim - 1), pltpu.roll(v, lanes - shift, v.ndim - 1)
    if whole:
        low = jnp.where(lane >= shift, low, 0.0)
        high = jnp.where(lane < lanes - shift, high, 0.0)
    return 0.75 * v + 0.25 * jnp.where(even, low, high)


def spread_y(v, shift, rows):
    row = rows_of(v.shape)
    even = (row // shift) % 2 == 0
    low = jnp.where(row >= shift, pltpu.roll(v, shift, v.ndim - 2), 0.0)
    high = jnp.where(row < rows - shift, pltpu.roll(v, rows - shift, v.ndim - 2), 0.0)
    return 0.75 * v + 0.25 * jnp.where(even, low, high)


def picked_lanes(v, pick):
    pick, total = pick.astype(jnp.bfloat16), None
    for _ in range(3):
        part = v.astype(jnp.bfloat16)
        v = v - part.astype(jnp.float32)
        product = jnp.dot(part, pick, preferred_element_type=jnp.float32)
        total = product if total is None else total + product
    return total


def zero_pads(*refs):
    for ref in refs:
        ref[0] = jnp.zeros(ref.shape[1:], jnp.float32)
        ref[ref.shape[0] - 1] = jnp.zeros(ref.shape[1:], jnp.float32)


def core_of():
    return lax.rem(lax.axis_index("gy"), 2)


def reaches():
    source1 = {0: WIN1 + 2, 1: WIN1 + 1, 2: WIN1, 3: 0}
    coeff1 = {a: max(source1.get(a, -1) + 1, source1.get(a - 1, -1), source1.get(a + 1, -1), min(WIN1, 7 - a)) for a in range(7)}
    residual0 = {0: 2 * source1[0]}
    coeff0 = {0: 2 * coeff1[0]}
    for a in range(1, 7):
        for x in (2 * a - 1, 2 * a):
            coeff0[x] = 2 * coeff1[a]
            if a in source1:
                residual0[x] = 2 * source1[a]

    def grown(steps, x):
        return max([z + steps - abs(x - at) for at, z in residual0.items() if abs(x - at) <= steps], default=0)

    source = [grown(3, x) for x in range(REACH_XB + 1)]
    coeff = [max(grown(4, x), coeff0[x]) for x in range(REACH_X + 1)]
    assert max(source + coeff) <= REACH_Z
    return source, coeff


def slots_of(items):
    rows, used = [], LANES
    for item, width in items:
        if width:
            if used + width > LANES:
                rows.append([])
                used = 0
            rows[-1].append((item, used, width))
            used += width
    return rows


def box_slots(bx):
    source, coeff = reaches()
    return slots_of([((0, p), source[0]) for p in range(bx)] + [((1, p), coeff[0]) for p in range(bx)])


def halo_slots():
    source, coeff = reaches()
    items = []
    for pair in range(2):
        items += [((pair, 0, x), source[x]) for x in range(1, REACH_XB + 1)]
        items += [((pair, 1, x), coeff[x]) for x in range(1, REACH_X + 1)]
    return slots_of(items)


def pack_kernel(geo, slots, plane_of, count, *refs):
    own, sib, z_out = refs[:count // 2], refs[count // 2:count], refs[-1]
    core, ye = core_of(), geo["ye"]
    lane = lanes_of((ye, LANES))
    for fields, half in ((own, core), (sib, 1 - core)):
        rows = pl.ds(pl.multiple_of(half * ye, 8), ye)
        for m, row in enumerate(slots):
            packed = jnp.zeros((ye, LANES), jnp.float32)
            for item, at, width in row:
                shift = jnp.where(core == 1, (at + width) % LANES, at)
                field, plane = plane_of(item)
                packed = jnp.where((lane >= at) & (lane < at + width), pltpu.roll(fields[field][plane], shift, 1), packed)
            z_out[m, rows] = packed


def passed_views(geo, ref):
    wide0, wide1, rows = geo["bx"] + 2 * WIN0, geo["bx"] // 2 + 2 * WIN1, geo["yw"] // 2
    views, at = [], 0
    for i in range(6):
        views.append(ref.at[pl.ds(at, wide0 + (i == 0))])
        at += wide0 + 1
    for i in range(6):
        views.append(ref.at[pl.ds(at + i // 2 * (wide1 + 1), wide1 + (i == 0)), pl.ds(i % 2 * rows, rows)])
    return views


def down_kernel(geo, *refs):
    (own_in, sib_in, even_own, odd_own, even_sib, odd_sib, z_in, zx_in, packed_any, even_any, odd_any, passed,
     packed_out, even_out, odd_out,
     k0, cx, cy, cz, iv, ds, g0, g, d1, d2,
     k1, ex, ey, ez, ei, es, h0, h, f1, f2, u1, half_y, half_y1, sems) = refs
    core = core_of()
    ix, nx = lax.axis_index("gx"), lax.axis_size("gx")
    iz, nz = lax.axis_index("gz"), lax.axis_size("gz")
    bx, ye, yw, xw = geo["bx"], geo["ye"], geo["yw"], geo["xw"]
    z_there = jnp.where(core == 0, iz > 0, iz < nz - 1)
    lo_there, hi_there = ix > 0, ix < nx - 1
    even = lax.rem(ix, 2) == 0

    lane = lanes_of((yw, LANES))

    def strip(ref, m, at, width):
        shift = jnp.where(core == 0, (2 * LANES - width - at) % LANES, (LANES - at) % LANES)
        return pltpu.roll(ref[m], shift, 1)

    def merge(window, at, width, there, moved):
        halo = jnp.where(core == 0, lane - (LANES - width), width - 1 - lane) >= 0
        window[at] = jnp.where(halo, jnp.where(there, moved, 0.0), window[at])

    own_rows = pl.ds(pl.multiple_of(core * ye, 8), ye)
    sib_rows = pl.ds(pl.multiple_of((1 - core) * ye, 8), ye)
    zero_pads(k0, d1, d2, k1, f1, f2)
    windows = ((g0, 0, REACH_XB, 0), (k0, bx, REACH_X, REACH_XB))
    for p in range(REACH_X - REACH_XB):
        g0[1 + p] = jnp.zeros((yw, LANES), jnp.float32)
        g0[xw - p] = jnp.zeros((yw, LANES), jnp.float32)

    def halos(from_even, from_odd, rows):
        for window, _, width, at in windows:
            e, o = from_even[pl.ds(at, width)], from_odd[pl.ds(at, width)]
            window[pl.ds(1 + REACH_X - width, width), rows] = jnp.where(lo_there, jnp.where(even, o, e), 0.0)
            window[pl.ds(1 + REACH_X + bx, width), rows] = jnp.where(hi_there, jnp.where(even, e, o), 0.0)

    for window, at, _, _ in windows:
        window[pl.ds(1 + REACH_X, bx), own_rows] = own_in[pl.ds(at, bx)]
        window[pl.ds(1 + REACH_X, bx), sib_rows] = sib_in[pl.ds(at, bx)]
    halos(even_own, odd_own, own_rows)
    halos(even_sib, odd_sib, sib_rows)
    for m, row in enumerate(box_slots(bx)):
        for (f, p), at, width in row:
            merge(windows[f][0], 1 + REACH_X + p, width, z_there, strip(z_in, m, at, width))
    places = {item: (m, at, width) for m, row in enumerate(halo_slots()) for item, at, width in row}
    for (pair, f, x), place in places.items():
        if pair == 0:
            window, width = windows[f][0], place[2]
            e, o = strip(zx_in, *place), strip(zx_in, *places[1, f, x])
            merge(window, 1 + REACH_X - x, width, z_there & lo_there, jnp.where(even, o, e))
            merge(window, REACH_X + bx + x, width, z_there & hi_there, jnp.where(even, e, o))

    grid = Grid(xw, yw, LANES, 1, 1, False, geo["chunk0"])
    inner = Grid(xw - 8, yw, LANES, 1, 1, False, geo["chunk0_inner"])
    nothing = jnp.zeros((4, yw, LANES), jnp.float32)
    for ref in (g, d2):
        ref[pl.ds(1, 4)] = nothing
        ref[pl.ds(xw - 3, 4)] = nothing

    def first(at, here, inverse):
        scaled = g0[here] * inverse
        g0[here] = scaled
        d1[here] = FACTORS[0][1] * scaled

    grid.setup(k0, cx, cy, cz, iv, ds, 1.0, first)
    own0 = 1 + REACH_X - WIN0
    wide0 = bx + 2 * WIN0
    copies = []

    views = passed_views(geo, passed)

    def send(source, start, count):
        i = len(copies)
        copy = pltpu.make_async_copy(source.at[pl.ds(start, count)], views[i], sems.at[i])
        copy.start()
        copies.append(copy)

    send(cx, own0 - 1, wide0 + 1)
    send(cy, own0, wide0)
    send(cz, own0, wide0)
    send(iv, own0, wide0)
    send(g0, own0, wide0)

    def restrict(source, target, tmp, x_count, at, y_first, y_rows, shift):
        for i in range(x_count):
            j = i % tmp.shape[0]
            v = source[at + 2 * i] + source[at + 2 * i + 1]
            tmp[j] = v + pltpu.roll(v, v.shape[0] - 1, 0)
            v = tmp[j, pl.ds(y_first, y_rows // 2, stride=2)]
            target(i, 0.125 * pair_z(v, shift, LANES))

    x1, y1 = xw // 2, yw // 2

    def put_k1(i, v):
        k1[1 + i] = v

    def put_b1(i, v):
        h0[1 + i] = v

    restrict(k0, put_k1, half_y, x1, 1, 0, yw, 1)
    coeffs = (cx, cy, cz, iv)

    def second(here, v, value, direction):
        g[here] = value
        d2[here] = direction

    inner.step(coeffs, d1, g0, *FACTORS[1], second, 5)

    def third(here, v, value, direction):
        g[here] = value
        k0[here] = d1[here] + v + direction
        d1[here] = direction

    inner.part(1).step(coeffs, d2, g, *FACTORS[2], third, 6)
    send(k0, own0, wide0)

    def residual(here, v, value, direction):
        g[here] = value * ds[here]

    inner.part(2).step(coeffs, d1, g, 0.0, None, residual, 7)

    restrict(g, put_b1, half_y, x1, 1, 0, yw, 1)
    grid1 = Grid(x1, y1, LANES, 1, 2, False, geo["chunk1"])

    def first1(at, here, inverse):
        scaled = 4.0 * (h0[here] * inverse)
        h0[here] = scaled
        f1[here] = FACTORS[0][1] * scaled

    grid1.setup(k1, ex, ey, ez, ei, es, 0.25, first1)
    own1 = 1 + REACH_X // 2 - WIN1
    wide1 = bx // 2 + 2 * WIN1
    send(ex, own1 - 1, wide1 + 1)
    send(ey, own1, wide1)
    send(ez, own1, wide1)
    send(ei, own1, wide1)
    send(h0, own1, wide1)
    coeffs1 = (ex, ey, ez, ei)

    def second1(here, v, value, direction):
        h[here] = value
        f2[here] = direction

    grid1.step(coeffs1, f1, h0, *FACTORS[1], second1)

    def third1(here, v, value, direction):
        h[here] = value
        u1[here] = f1[here] + v + direction
        f1[here] = direction

    grid1.step(coeffs1, f2, h, *FACTORS[2], third1)
    send(u1, own1, wide1)
    mine = 1 + REACH_X // 2
    last = mine + bx // 2
    for source, low, high, at, count in ((u1, mine, last - WIN1, 0, 6), (h0, mine + 2, last - 5, 6, 3)):
        low, high = source[pl.ds(low, count)], source[pl.ds(high, count)]
        even_out[pl.ds(at, count)] = jnp.where(even, high, low)
        odd_out[pl.ds(at, count)] = jnp.where(even, low, high)

    def leave(source, target):
        copy = pltpu.make_async_copy(source, target, sems.at[len(copies)])
        copy.start()
        copies.append(copy)

    leave(even_out, even_any)
    leave(odd_out, odd_any)

    def residual1(here, v, value, direction):
        h[here] = value * es[here]

    grid1.step(coeffs1, f1, h, 0.0, None, residual1)

    place = lax.rem(2 * iz + core, 8)
    x2, y2 = bx // 4, geo["by"] // 2
    row, column = rows_of((LANES, LANES)), lanes_of((LANES, LANES))
    pick = (row == HALF * core + 4 * lax.rem(column, 16)).astype(jnp.float32)
    slot = lanes_of((y2, LANES)) // 16
    for f, source in enumerate((h, k1)):
        boxes = []
        restrict(source, lambda i, v, boxes=boxes: boxes.append(v), half_y1, x2, 1 + REACH_X // 2, geo["oy"] // 2, 2 * y2, 2)
        stacked = jnp.concatenate(boxes, axis=0)
        picked = picked_lanes(stacked, pick)
        packed = jnp.zeros((y2, LANES), jnp.float32)
        for p in range(x2):
            packed = jnp.where(slot == lax.rem(p + place, 8), picked[p * y2:(p + 1) * y2], packed)
        if geo["packed"]:
            for j in range(packed_out.shape[0]):
                if (j // nz) % 2 == f:
                    packed_out[j] = packed
        else:
            packed_out[f] = packed
    leave(packed_out, packed_any)
    for copy in copies:
        copy.wait()


def up_kernel(geo, *refs):
    refs = list(refs)

    def take(count):
        taken = refs[:count]
        del refs[:count]
        return taken

    count = 2 if geo["packed"] else 1
    arriving = take(count + 2)
    views = passed_views(geo, take(1)[0])
    in0, in1 = views[:6], views[6:]
    send_u, send_r, keep_u, keep_r = take(4)
    k2, cx2, cy2, cz2, iv2, ds2, g02, g2, da2, db2, w2, e2 = take(12)
    k3, cx3, cy3, cz3, iv3, ds3, g03, g3, da3, db3, w3, e3 = take(12)
    k4, cx4, cy4, cz4, iv4, g04, g4, da4, db4, e4 = take(10)
    cx1, cy1, cz1, iv1, g01, w1, u1, g1, da1, db1, e1 = take(11)
    cx0, cy0, cz0, iv0, g00, w0, u0, g0, da0, db0 = take(10)
    e2_wide, spread1, spread0 = take(3)
    gathered = take(count)
    from_even, from_odd, sems = take(3)
    core = core_of()
    ix, nx = lax.axis_index("gx"), lax.axis_size("gx")
    iz, nz = lax.axis_index("gz"), lax.axis_size("gz")
    yp = lax.axis_index("gy") // 2
    bx, by, yw = geo["bx"], geo["by"], geo["yw"]
    x2, y2, z2 = geo["x2"], geo["y2"], geo["z2"]
    wide0, wide1 = bx + 2 * WIN0, bx // 2 + 2 * WIN1

    arrivals = []
    for source, target in zip(arriving, (*gathered, from_even, from_odd)):
        arrivals.append(pltpu.make_async_copy(source, target, sems.at[16 + len(arrivals)]))
        arrivals[-1].start()
    copies = []
    for sources, targets, wide in ((in1, (cx1, cy1, cz1, iv1, g01, w1), wide1), (in0, (cx0, cy0, cz0, iv0, g00, w0), wide0)):
        for i, (source, target) in enumerate(zip(sources, targets)):
            there = target.at[pl.ds(0, wide + 1)] if i == 0 else target.at[pl.ds(1, wide)]
            copy = pltpu.make_async_copy(source, there, sems.at[len(copies)])
            copy.start()
            copies.append(copy)

    zero_pads(k2, da2, db2, e2, k3, da3, db3, e3, k4, da4, db4, e4, u1, da1, db1, u0, da0, db0)

    for copy in arrivals:
        copy.wait()
    if geo["packed"]:
        slot = lanes_of((y2, LANES)) // 16
        for gx in range(nx):
            for f, target in ((0, g02), (1, k2)):
                for p in range(8):
                    merged = jnp.zeros((y2, LANES), jnp.float32)
                    for gz in range(nz):
                        for cc in range(2):
                            at = (2 * gx + cc) * nz + gz
                            here = jnp.where(core == f, gathered[0][at], gathered[1][at])
                            merged = jnp.where(slot == (p + 2 * gz + cc) % 8, here, merged)
                    target[1 + 8 * gx + p] = pltpu.roll(merged, (LANES - 16 * p) % LANES, 1)
    else:
        g02[pl.ds(1, x2)] = gathered[0][0]
        k2[pl.ds(1, x2)] = gathered[0][1]

    def descend(grid, level, k, cx, cy, cz, iv, ds, g0, first_target):
        def first(at, here, inverse):
            scaled = 4.0**level * (g0[here] * inverse)
            g0[here] = scaled
            first_target[here] = FACTORS[0][1] * scaled

        grid.setup(k, cx, cy, cz, iv, ds, 0.25**level, first)

    def pre(grid, level, k, cx, cy, cz, iv, ds, g0, g, da, db, w):
        descend(grid, level, k, cx, cy, cz, iv, ds, g0, da)
        coeffs = (cx, cy, cz, iv)

        def second(here, v, value, direction):
            g[here] = value
            db[here] = direction

        grid.step(coeffs, da, g0, *FACTORS[1], second)

        def third(here, v, value, direction):
            g[here] = value
            w[here] = da[here] + v + direction
            da[here] = direction

        grid.step(coeffs, db, g, *FACTORS[2], third)

        def residual(here, v, value, direction):
            g[here] = value * ds[here]

        grid.step(coeffs, da, g, 0.0, None, residual)

    def post(grid, coeffs, g0, u, g, da, db, result, shrink=0):
        def step(i, *args):
            part = Grid(grid.x - 2 * i * shrink, grid.y, grid.z, grid.sy, grid.sz, grid.whole_z, grid.size)
            if shrink:
                part.size = part.x if grid.size == grid.x else 2
            part.step(coeffs, *args, 1 + i * shrink)

        def one(here, v, value, direction):
            g[here] = value
            da[here] = direction

        step(1, u, g0, *FACTORS[0], one)

        def two(here, v, value, direction):
            g[here] = value
            db[here] = direction

        step(2, da, g, *FACTORS[1], two)

        def three(here, v, value, direction):
            g[here] = value
            result[here] = u[here] + da[here] + v + direction
            da[here] = direction

        step(3, db, g, *FACTORS[2], three)

    def restrict(fine, coarse, count, shift):
        for i in range(count):
            v = fine[1 + 2 * i] + fine[2 + 2 * i]
            coarse[1 + i] = 0.125 * pair_z(pair_y(v, shift, y2), shift, z2)

    def prolong(coarse, w, target, count, shift):
        for i in range(count):
            middle = 0.75 * coarse[1 + i]
            for j, side in ((0, coarse[i]), (1, coarse[2 + i])):
                v = spread_y(middle + 0.25 * side, shift, y2)
                target[1 + 2 * i + j] = w[1 + 2 * i + j] + spread_z(v, shift, z2, True)

    def size_of(x):
        planes = max(1, 32 // ((y2 // 8) * (z2 // LANES)))
        return min(x, planes)

    x3, x4 = x2 // 2, x2 // 4
    grid2 = Grid(x2, y2, z2, 1, 1, True, size_of(x2))
    grid3 = Grid(x3, y2, z2, 2, 2, True, size_of(x3))
    grid4 = Grid(x4, y2, z2, 4, 4, True, size_of(x4))
    pre(grid2, 2, k2, cx2, cy2, cz2, iv2, ds2, g02, g2, da2, db2, w2)
    restrict(k2, k3, x3, 1)
    restrict(g2, g03, x3, 1)
    pre(grid3, 3, k3, cx3, cy3, cz3, iv3, ds3, g03, g3, da3, db3, w3)
    restrict(k3, k4, x4, 2)
    restrict(g3, g04, x4, 2)
    descend(grid4, 4, k4, cx4, cy4, cz4, iv4, None, g04, da4)
    e4[pl.ds(1, x4)] = da4[pl.ds(1, x4)]
    for sweep in range(1, COARSE_STEPS):
        src, dst = (da4, db4) if sweep % 2 else (db4, da4)

        def coarse(here, v, value, direction):
            g4[here] = value
            dst[here] = direction
            e4[here] = e4[here] + direction

        grid4.step((cx4, cy4, cz4, iv4), src, g04 if sweep == 1 else g4, *COARSE_FACTORS[sweep], coarse)
    prolong(e4, w3, e3, x4, 2)
    post(grid3, (cx3, cy3, cz3, iv3), g03, e3, g3, da3, db3, w3)
    e3[pl.ds(1, x3)] = w3[pl.ds(1, x3)]
    prolong(e3, w2, e2, x3, 1)
    post(grid2, (cx2, cy2, cz2, iv2), g02, e2, g2, da2, db2, w2)

    pad_y = geo["pad_y"]
    if pad_y:
        e2_wide[...] = jnp.zeros(e2_wide.shape, jnp.float32)
    else:
        edge = jnp.zeros((4,) + e2_wide.shape[1:], jnp.float32)
        e2_wide[pl.ds(0, 4)] = edge
        e2_wide[pl.ds(x2 + 4, 4)] = edge
    e2_wide[pl.ds(4, x2), pl.ds(pad_y, y2)] = w2[pl.ds(1, x2)]
    x2w, y2w = bx // 4 + 8, yw // 4
    cells, lane = rows_of((z2, LANES)), lanes_of((z2, LANES))
    shifted = jnp.where(core == 0, jnp.where(lane >= 104, -32, 0), jnp.where(lane < 24, 32, 0))
    pick = (cells == 32 * iz + lane // 4 + shifted).astype(jnp.float32)
    start = (bx // 4) * ix
    rows = pl.ds(pl.multiple_of(8 * yp, 8), y2w) if pad_y else pl.ds(0, y2w)
    window = e2_wide[pl.ds(start, x2w), rows].reshape(x2w * y2w, z2)
    window = picked_lanes(window, pick)
    window = window.reshape(x2w, y2w, LANES)

    def place_rows(target, plane, v, count):
        row = rows_of(v.shape)
        low = jnp.where(row >= 1, pltpu.roll(v, 1, 0), 0.0)
        high = jnp.where(row < count - 1, pltpu.roll(v, count - 1, 0), 0.0)
        target[plane, pl.ds(0, count, stride=2)] = 0.75 * v + 0.25 * low
        target[plane, pl.ds(1, count, stride=2)] = 0.75 * v + 0.25 * high

    for copy in copies[:6]:
        copy.wait()
    even, last1 = lax.rem(ix, 2) == 0, 1 + WIN1 + bx // 2
    for target, low, high, at, count in ((w1, 1, last1, 0, 6), (g01, 2, last1 + 2, 6, 3)):
        e, o = from_even[pl.ds(at, count)], from_odd[pl.ds(at, count)]
        low, high = pl.ds(low, count), pl.ds(high, count)
        target[low] = jnp.where(ix > 0, jnp.where(even, o, e), target[low])
        target[high] = jnp.where(ix < nx - 1, jnp.where(even, e, o), target[high])
    for plane in range(wide1):
        j = plane // 2
        v = 0.75 * window[j + 1] + 0.25 * window[j + 2 if plane % 2 else j]
        place_rows(spread1, 1 + plane, spread_z(v, 2, LANES, False), y2w)
    grid1 = Grid(wide1, yw // 2, LANES, 1, 2, False, geo["chunk1"])

    def start1(at):
        here = pl.ds(at, grid1.size)
        u1[here] = jnp.where(iv1[here] > 0.0, w1[here] + spread1[here, pl.ds(0, yw // 2)], 0.0)

    chunks(wide1, start1, grid1.size)
    post(grid1, (cx1, cy1, cz1, iv1), g01, u1, g1, da1, db1, e1, 1)

    for copy in copies[6:]:
        copy.wait()
    grid0 = Grid(wide0, yw, LANES, 1, 1, False, geo["chunk_up"])

    def fill(i, carry):
        at = WIN1 + 1 - WIN0 // 2 + i
        middle = 0.75 * e1[at]
        for j, side in ((0, e1[at - 1]), (1, e1[at + 1])):
            place_rows(spread0, 1 + 2 * i + j, spread_z(middle + 0.25 * side, 1, LANES, False), yw // 2)
        return carry

    lax.fori_loop(0, wide0 // 2, fill, 0, unroll=True)

    def start0(at):
        here = pl.ds(at, grid0.size)
        u0[here] = jnp.where(iv0[here] > 0.0, w0[here] + spread0[here, pl.ds(0, yw)], 0.0)

    chunks(wide0, start0, grid0.size)
    coeffs0 = (cx0, cy0, cz0, iv0)
    post(grid0, coeffs0, g00, u0, g0, da0, db0, w0, 1)

    own = pl.ds(1 + WIN0, bx)
    own_rows = pl.ds(pl.multiple_of(geo["oy"] + core * by, 8), by)
    sib_rows = pl.ds(pl.multiple_of(geo["oy"] + (1 - core) * by, 8), by)
    leaving = []

    def leave(source, rows, target):
        copy = pltpu.make_async_copy(source.at[own, rows], target, sems.at[12 + len(leaving)])
        copy.start()
        leaving.append(copy)

    leave(w0, sib_rows, send_u)
    leave(w0, own_rows, keep_u)

    def residual(here, v, value, direction):
        g0[here] = value / iv0[here]

    Grid(bx, yw, LANES, 1, 1, False, geo["chunk_last"]).step(coeffs0, da0, g0, 0.0, None, residual, 1 + WIN0)
    leave(g0, sib_rows, send_r)
    leave(g0, own_rows, keep_r)
    for copy in leaving:
        copy.wait()


def array(*shape):
    return jax.ShapeDtypeStruct(shape, jnp.float32)


def on_device(right_side, conductivity):
    bx, by, bz = right_side.shape
    nx, ny, nz = (lax.axis_size(axis) for axis in AXES)
    pairs = ny // 2
    ix, iy, iz = (lax.axis_index(axis) for axis in AXES)
    core = iy % 2

    def index(x, p, c, z):
        return ((x % nx) * ny + (p % pairs) * 2 + c) * nz + z % nz

    every = [(x, p, z) for x in range(nx) for p in range(pairs) for z in range(nz)]

    def sibling(v):
        return lax.ppermute(v, "gy", [(i, i ^ 1) for i in range(ny)])

    def xor(v, axis, k):
        return lax.ppermute(v, axis, [(i, i ^ k) for i in range(lax.axis_size(axis))])

    def paired(v, first):
        perm = [(i, i) for i in range(nx)]
        for i in range(first, nx - 1, 2):
            perm[i], perm[i + 1] = (i, i + 1), (i + 1, i)
        return lax.ppermute(v, "gx", perm)

    def facing(v):
        perm = {}
        for x, p, z in every:
            if z > 0:
                a, b = index(x, p, 0, z), index(x, p, 1, z - 1)
                perm[a], perm[b] = b, a
        return lax.ppermute(v, AXES, [(i, perm.get(i, i)) for i in range(nx * ny * nz)])

    own_b, own_k, ye = right_side, conductivity, by
    if ny > 2:
        near = []
        far = []
        for p in range(pairs):
            near += [(2 * p, 2 * ((p - 1) % pairs) + 1), (2 * ((p - 1) % pairs) + 1, 2 * p)]
            far += [(2 * p, 2 * ((p + 1) % pairs)), (2 * p + 1, 2 * ((p - 1) % pairs) + 1)]
        there = jnp.where(core == 0, iy > 0, iy < ny - 1)

        def widened(v):
            one = jnp.where(there, lax.ppermute(v, "gy", near), 0.0)
            two = jnp.where(there, lax.ppermute(v, "gy", far), 0.0)
            return jnp.where(core == 0, jnp.concatenate([two, one, v], 1), jnp.concatenate([v, one, two], 1))

        own_b, own_k = widened(own_b), widened(own_k)
        ye = 3 * by
    yw = 2 * ye
    xw = bx + 2 * REACH_X
    geo = dict(
        bx=bx, by=by, ye=ye, yw=yw, xw=xw, oy=(yw - 2 * by) // 2, chunk0=56 if yw == 32 else 4, chunk0_inner=48 if yw == 32 else 4,
        chunk_up=40 if yw == 32 else 4, chunk_last=32 if yw == 32 else 4, chunk1=28 if yw == 32 else 4,
        packed=pairs == 1 and 32 * nz == LANES, x2=bx // 4 * nx, y2=by // 4 * ny, z2=bz // 4 * nz,
        pad_y=(yw // 4 - by // 2) // 2,
    )

    own = lax.optimization_barrier(jnp.concatenate([own_b, own_k], 0))
    even = ix % 2 == 0
    high = jnp.concatenate([own[bx - REACH_XB:bx], own[2 * bx - REACH_X:]], 0)
    low = jnp.concatenate([own[:REACH_XB], own[bx:bx + REACH_X]], 0)
    even_own = paired(jnp.where(even, high, low), 0)
    sib, odd_send = lax.optimization_barrier((sibling(own), jnp.where(even, low, high)))
    odd_own = paired(odd_send, 1)
    inside, hbm, anywhere = (pl.BlockSpec(memory_space=space) for space in (pltpu.VMEM, pltpu.HBM, pl.ANY))

    def call(name, kernel, ins, outs, scratch, hbm_ins=0, hbm_outs=0, limit=0, operand=inside, result=inside):
        held = sum(4 * math.prod(v.shape) for v in (*ins, *outs, *scratch) if v.dtype == jnp.float32)
        return pl.pallas_call(
            kernel, out_shape=outs, in_specs=[operand] * (len(ins) - hbm_ins) + [hbm] * hbm_ins,
            out_specs=[result] * (len(outs) - hbm_outs) + [hbm] * hbm_outs,
            scratch_shapes=scratch, name=name,
            compiler_params=pltpu.CompilerParams(vmem_limit_bytes=max(limit, held + 6 * 1024 * 1024)),
            cost_estimate=pl.CostEstimate(flops=4_000_000, bytes_accessed=8_000_000, transcendentals=0),
        )(*ins)

    def vmem(shape):
        return pltpu.VMEM(shape, jnp.float32)

    def pack(name, slots, plane_of, ins, later=()):
        kernel = functools.partial(pack_kernel, geo, slots, plane_of, len(ins))
        return call(name, kernel, (*ins, *later), [array(len(slots), yw, LANES)], [], len(later))[0]

    z_send = pack("pack_box", box_slots(bx), lambda item: (0, item[0] * bx + item[1]), (own, sib))
    z_in = facing(z_send)
    even_own, _ = lax.optimization_barrier((even_own, z_send))
    odd_own, _ = lax.optimization_barrier((odd_own, z_send))
    even_sib, odd_sib = sibling(even_own), sibling(odd_own)

    def halo_plane(item):
        pair, field, x = item
        first, count = (0, REACH_XB) if field == 0 else (REACH_XB, REACH_X)
        from_above = (lax.rem(lax.axis_index("gx"), 2) == 0) == (pair == 0)
        return pair, first + jnp.where(from_above, x - 1, count - x)

    zx_in = facing(pack("pack_halo", halo_slots(), halo_plane, (even_own, odd_own, even_sib, odd_sib), (z_in,)))

    wide0, wide1 = bx + 2 * WIN0, bx // 2 + 2 * WIN1
    x1, y1 = xw // 2, yw // 2
    some0 = vmem((xw + 2, yw, LANES))
    some1 = vmem((x1 + 2, y1, LANES))
    passed = array(6 * (wide0 + 1) + 3 * (wide1 + 1), yw, LANES)
    edge = 9
    ins = (own, sib, even_own, odd_own, even_sib, odd_sib, z_in, zx_in)
    sends = [array(nx * ny * nz if geo["packed"] else 2, by // 2, LANES), array(edge, y1, LANES), array(edge, y1, LANES)]
    down = call(
        "down", functools.partial(down_kernel, geo), ins, sends + [passed],
        [vmem(v.shape) for v in sends] + [some0] * 10 + [some1] * 11
        + [vmem((6, yw, LANES)), vmem((6, y1, LANES)), pltpu.SemaphoreType.DMA((15,))],
        hbm_outs=1, limit=VMEM_LIMIT, result=anywhere,
    )
    packed, even_send, odd_send, passed = down[0], down[1], down[2], down[3]
    from_even, from_odd = paired(even_send, 0), paired(odd_send, 1)

    if geo["packed"]:
        half = lax.all_to_all(packed, AXES, 0, 0, tiled=True)
        half, from_even, from_odd = lax.optimization_barrier((half, from_even, from_odd))
        gathered = (half, sibling(half))
    else:
        pieces = lax.all_gather(packed, AXES).reshape(nx, pairs, 2, nz, 2, by // 2, 8, 16)
        order = (jnp.arange(8) + 2 * jnp.arange(nz)[:, None, None] + jnp.arange(2)[:, None]) % 8
        order = jnp.transpose(order, (1, 0, 2))[None, None, :, :, None, None, :, None]
        pieces = jnp.take_along_axis(pieces, order, axis=6)
        gathered = (jnp.transpose(pieces, (4, 0, 6, 1, 5, 3, 2, 7)).reshape(2, geo["x2"], geo["y2"], geo["z2"]),)

    def level(planes, rows, lanes):
        return vmem((planes + 2, rows, lanes))

    x2, y2, z2 = geo["x2"], geo["y2"], geo["z2"]
    send_u, send_r, keep_u, keep_r = call(
        "up", functools.partial(up_kernel, geo), (*gathered, from_even, from_odd, passed), [array(bx, by, LANES)] * 4,
        [level(x2, y2, z2)] * 12 + [level(x2 // 2, y2, z2)] * 12 + [level(x2 // 4, y2, z2)] * 10
        + [level(wide1, y1, LANES)] * 11 + [level(wide0, yw, LANES)] * 10
        + [vmem((x2 + 8, y2 + 2 * geo["pad_y"], z2)), level(wide1, y1 + 8, LANES), level(wide0, yw + 8, LANES), *(vmem(v.shape) for v in gathered), vmem(from_even.shape), vmem(from_odd.shape)]
        + [pltpu.SemaphoreType.DMA((20,))],
        hbm_ins=1, limit=VMEM_LIMIT, operand=anywhere, result=anywhere,
    )
    mine = lanes_of((1, 1, LANES)) // HALF == core
    return jnp.where(mine, keep_u, sibling(send_u)), jnp.where(mine, keep_r, sibling(send_r))


def solution(mesh):
    specs = (P(*AXES), P(*AXES))
    return jax.shard_map(on_device, mesh=mesh, in_specs=specs, out_specs=specs, check_vma=False)
```
